128 devices in a mesh: section: 2 (over y_lo), dp: 16 (over z, x), tensor: 4 (over y_hi, core).
Axes of the slice: x: 4, y: 4 (y_hi: 2, y_lo: 2; y = y_hi * 2 + y_lo), z: 4, core: 2. Of those that a mesh axis runs over, the one named last changes fastest.
Arguments:
- inputs: bfloat16 [2, 16, 128, 1024], P(None, 'dp'), may hold values from -6 to 6
- cotangent: bfloat16 [2, 16, 128, 1024], P(None, 'dp'), may hold values from -6 to 6
- norm_gain1: bfloat16 [2, 1024], P('section'), may hold values from 0.099609375 to 1.8984375
- w_query: bfloat16 [2, 1024, 1024], P('section', None, 'tensor'), may hold values from -0.1875 to 0.1875
- w_key: bfloat16 [2, 1024, 1024], P('section', None, 'tensor'), may hold values from -0.1875 to 0.1875
- w_value: bfloat16 [2, 1024, 2048], P('section', None, 'tensor'), may hold values from -0.1875 to 0.1875
- conv_query: bfloat16 [2, 4, 1024], P('section', None, 'tensor'), may hold values from -3 to 3
- conv_key: bfloat16 [2, 4, 1024], P('section', None, 'tensor'), may hold values from -3 to 3
- conv_value: bfloat16 [2, 4, 2048], P('section', None, 'tensor'), may hold values from -3 to 3
- w_beta: bfloat16 [2, 1024, 8], P('section', None, 'tensor'), may hold values from -0.1875 to 0.1875
- w_decay: bfloat16 [2, 1024, 8], P('section', None, 'tensor'), may hold values from -0.1875 to 0.1875
- log_rate: float32 [2, 8], P('section', 'tensor'), may hold values from -4.5 to -1
- step_bias: float32 [2, 8], P('section', 'tensor'), may hold values from -1 to 1
- out_gain: bfloat16 [2, 2048], P('section', 'tensor'), may hold values from 0.099609375 to 1.8984375
- w_gate_out: bfloat16 [2, 1024, 2048], P('section', None, 'tensor'), may hold values from -0.1875 to 0.1875
- w_out: bfloat16 [2, 2048, 1024], P('section', 'tensor'), may hold values from -0.1875 to 0.1875
- norm_gain2: bfloat16 [2, 1024], P('section'), may hold values from 0.099609375 to 1.8984375
- w_ffn_gate: bfloat16 [2, 1024, 2816], P('section', None, 'tensor'), may hold values from -0.1875 to 0.1875
- w_ffn_up: bfloat16 [2, 1024, 2816], P('section', None, 'tensor'), may hold values from -0.1875 to 0.1875
- w_ffn_down: bfloat16 [2, 2816, 1024], P('section', 'tensor'), may hold values from -0.15625 to 0.15625
Outputs:
- hidden_out: bfloat16 [2, 2, 16, 128, 1024], P('section', None, 'dp')
- input_grad: bfloat16 [2, 2, 16, 128, 1024], P('section', None, 'dp')
- grad_norm_gain1: float32 [2, 1024], P('section')
- grad_query: float32 [2, 1024, 1024], P('section', 'dp', 'tensor')
- grad_key: float32 [2, 1024, 1024], P('section', 'dp', 'tensor')
- grad_value: float32 [2, 1024, 2048], P('section', 'dp', 'tensor')
- grad_conv_query: float32 [2, 4, 1024], P('section', None, 'tensor')
- grad_conv_key: float32 [2, 4, 1024], P('section', None, 'tensor')
- grad_conv_value: float32 [2, 4, 2048], P('section', None, 'tensor')
- grad_beta: float32 [2, 1024, 8], P('section', 'dp', 'tensor')
- grad_decay: float32 [2, 1024, 8], P('section', 'dp', 'tensor')
- grad_log_rate: float32 [2, 8], P('section', 'tensor')
- grad_step_bias: float32 [2, 8], P('section', 'tensor')
- grad_out_gain: float32 [2, 2048], P('section', 'tensor')
- grad_gate_out: float32 [2, 1024, 2048], P('section', 'dp', 'tensor')
- grad_out: float32 [2, 2048, 1024], P('section', 'tensor', 'dp')
- grad_norm_gain2: float32 [2, 1024], P('section')
- grad_ffn_gate: float32 [2, 1024, 2816], P('section', 'dp', 'tensor')
- grad_ffn_up: float32 [2, 1024, 2816], P('section', 'dp', 'tensor')
- grad_ffn_down: float32 [2, 2816, 1024], P('section', 'tensor', 'dp')
The draws below stay inside these ranges and needn't reach their ends.
All inputs are finite; a program needn't handle non-finite values.
Results may differ from the reference program's by a relative error of at most 0.033.
Values may be sent and summed in bfloat16 or wider, within the bound.
A program may use at most 128 MiB of HBM per device.

```python
import jax
import jax.numpy as jnp
from jax import lax

D = 1024
H = 8
FF = 2816
CONV = 4
GROUP = 64
MB = 2
LEN = 128
SEQS = 16
HK = 1024
HV = 2048


def levels(stream_key, extent, shards, low, largest):
    def one(axis_at, parts):
        steps = jax.random.uniform(jax.random.fold_in(jax.random.fold_in(stream_key, 6), axis_at), (parts,), jnp.float32, low / len(shards), largest / len(shards))
        return jnp.repeat(jnp.exp(steps), extent[axis_at] // parts).reshape((-1,) + (1,) * (len(extent) - axis_at - 1))

    loudness = one(*shards[0])
    for cut in shards[1:]:
        loudness = loudness * one(*cut)
    return loudness


def centred(own_key, dims, deviation, bound, split=(), kind=jnp.bfloat16):
    drawn = deviation * jax.random.normal(own_key, dims, jnp.float32)
    if split:
        drawn = drawn * levels(own_key, dims, split, -0.22, 0.18)
    return jnp.clip(drawn, -bound, bound).astype(kind)


def setup_inputs(seed: int = 0) -> dict:
    arg_keys = jax.random.split(jax.random.key(seed), 21)
    return {
        "inputs": centred(arg_keys[0], (MB, SEQS, LEN, D), 1.0, 6.0, ((1, 16),)),
        "cotangent": centred(arg_keys[1], (MB, SEQS, LEN, D), 1.0, 6.0, ((1, 16),)),
        "norm_gain1": jnp.clip(1.0 + 0.18 * jax.random.normal(arg_keys[2], (2, D), jnp.float32), 0.099609375, 1.8984375).astype(jnp.bfloat16),
        "w_query": centred(arg_keys[3], (2, D, HK), D ** -0.5, 0.1875, ((0, 2), (2, 4))),
        "w_key": centred(arg_keys[4], (2, D, HK), D ** -0.5, 0.1875, ((0, 2), (2, 4))),
        "w_value": centred(arg_keys[5], (2, D, HV), D ** -0.5, 0.1875, ((0, 2), (2, 4))),
        "conv_query": centred(arg_keys[6], (2, CONV, HK), CONV ** -0.5, 3.0, ((0, 2), (2, 4))),
        "conv_key": centred(arg_keys[7], (2, CONV, HK), CONV ** -0.5, 3.0, ((0, 2), (2, 4))),
        "conv_value": centred(arg_keys[8], (2, CONV, HV), CONV ** -0.5, 3.0, ((0, 2), (2, 4))),
        "w_beta": centred(arg_keys[9], (2, D, H), D ** -0.5, 0.1875, ((0, 2), (2, 4))),
        "w_decay": centred(arg_keys[10], (2, D, H), D ** -0.5, 0.1875, ((0, 2), (2, 4))),
        "log_rate": jnp.clip(-4.5 + 3.5 * jax.random.uniform(arg_keys[11], (2, H), jnp.float32) ** levels(arg_keys[11], (2, H), ((0, 2), (1, 4)), -0.2, 0.2), -4.5, -1.0),
        "step_bias": jnp.clip(jax.random.uniform(arg_keys[12], (2, H), jnp.float32, -1.0, 1.0) * levels(arg_keys[12], (2, H), ((0, 2), (1, 4)), -0.4, 0.0), -1.0, 1.0),
        "out_gain": jnp.clip(1.0 + 0.18 * jax.random.normal(arg_keys[13], (2, HV), jnp.float32), 0.099609375, 1.8984375).astype(jnp.bfloat16),
        "w_gate_out": centred(arg_keys[14], (2, D, HV), D ** -0.5, 0.1875, ((0, 2), (2, 4))),
        "w_out": centred(arg_keys[15], (2, HV, D), (HV // 2) ** -0.5, 0.1875, ((0, 2), (1, 4))),
        "norm_gain2": jnp.clip(1.0 + 0.18 * jax.random.normal(arg_keys[16], (2, D), jnp.float32), 0.099609375, 1.8984375).astype(jnp.bfloat16),
        "w_ffn_gate": centred(arg_keys[17], (2, D, FF), D ** -0.5, 0.1875, ((0, 2), (2, 4))),
        "w_ffn_up": centred(arg_keys[18], (2, D, FF), D ** -0.5, 0.1875, ((0, 2), (2, 4))),
        "w_ffn_down": centred(arg_keys[19], (2, FF, D), (FF // 2) ** -0.5, 0.15625, ((0, 2), (1, 4))),
    }


@jax.custom_vjp
def low(v):
    return lax.optimization_barrier(v.astype(jnp.bfloat16)).astype(jnp.float32)

@jax.custom_vjp
def low_back(v):
    return v

def low_keep(v):
    return (low(v), None)

def low_pass(kept, grad):
    return (grad,)

def back_keep(v):
    return (v, None)

def back_low(kept, grad):
    return (low(grad),)
low.defvjp(low_keep, low_pass)
low_back.defvjp(back_keep, back_low)

def product(left, right):
    return jnp.matmul(left, right, precision=lax.Precision.HIGHEST)

def rms_norm(activations, gain_vec):
    return activations * lax.rsqrt(lax.optimization_barrier(jnp.mean(activations * activations, axis=-1, keepdims=True)) + 1e-06) * gain_vec

def short_conv(signal, kernel):
    kernel_len = kernel.shape[0]
    seq_len = signal.shape[1]
    padded = jnp.pad(signal, ((0, 0), (kernel_len - 1, 0), (0, 0)))
    summed = padded[:, 0:seq_len, :] * kernel[0]
    for offset in range(1, kernel_len):
        summed = summed + padded[:, offset:offset + seq_len, :] * kernel[offset]
    return jax.nn.silu(summed)

def unit_rows(vectors):
    return vectors * lax.rsqrt(lax.optimization_barrier(jnp.sum(vectors * vectors, axis=-1, keepdims=True)) + 1e-06)

def block_step(state, block):
    queries, key_vecs, values, beta_gates, log_decay = block
    block_len = log_decay.shape[-1]
    cumulative = jnp.cumsum(log_decay, axis=-1)
    row_ids = lax.broadcasted_iota(jnp.int32, (block_len, block_len), 0)
    col_ids = lax.broadcasted_iota(jnp.int32, (block_len, block_len), 1)
    strict = row_ids > col_ids
    within = row_ids >= col_ids
    log_gaps = cumulative[..., :, None] - cumulative[..., None, :]
    lower_decay = jnp.where(strict, jnp.exp(jnp.where(strict, log_gaps, 0.0)), 0.0)
    full_decay = jnp.where(within, jnp.exp(jnp.where(within, log_gaps, 0.0)), 0.0)
    key_key = jnp.einsum('bhid,bhjd->bhij', key_vecs, key_vecs, precision=lax.Precision.HIGHEST)
    system = jnp.eye(block_len, dtype=jnp.float32) + beta_gates[..., :, None] * key_key * lower_decay
    stacked_rhs = jnp.concatenate([beta_gates[..., None] * values, (beta_gates * jnp.exp(cumulative))[..., None] * key_vecs], axis=-1)
    solved = lax.linalg.triangular_solve(system, stacked_rhs, left_side=True, lower=True)
    value_width = values.shape[-1]
    fresh = solved[..., :value_width] - jnp.einsum('bhcd,bhde->bhce', solved[..., value_width:], state, precision=lax.Precision.HIGHEST)
    scores = jnp.einsum('bhid,bhjd->bhij', queries, key_vecs, precision=lax.Precision.HIGHEST) * full_decay
    output = jnp.exp(cumulative)[..., None] * jnp.einsum('bhcd,bhde->bhce', queries, state, precision=lax.Precision.HIGHEST)
    output = output + jnp.einsum('bhij,bhje->bhie', scores, fresh, precision=lax.Precision.HIGHEST)
    final_log = cumulative[..., -1:]
    carried = jnp.exp(final_log)[..., None] * state
    carried = carried + jnp.einsum('bhcd,bhce->bhde', key_vecs * jnp.exp(final_log - cumulative)[..., None], fresh, precision=lax.Precision.HIGHEST)
    return (carried, output)

def delta_rule(queries, key_vecs, values, beta_gates, log_decay):
    batch_size, seq_len, head_count, key_width = queries.shape
    value_width = values.shape[-1]
    block_count = seq_len // GROUP

    def blocks(array_in):
        array_in = array_in.reshape((batch_size, block_count, GROUP, head_count) + array_in.shape[3:])
        return jnp.moveaxis(array_in, (1, 3), (0, 2))
    start_state = jnp.zeros((batch_size, head_count, key_width, value_width), jnp.float32)
    pieces = (blocks(queries), blocks(key_vecs), blocks(values), blocks(beta_gates), blocks(log_decay))
    unused, outputs = lax.scan(jax.checkpoint(block_step), start_state, pieces)
    outputs = jnp.moveaxis(outputs, (0, 2), (1, 3))
    return outputs.reshape(batch_size, seq_len, head_count, value_width)

def token_mixer(normed, w_query, w_key, w_value, conv_query, conv_key, conv_value, w_beta, w_decay, log_rate, step_bias, out_gain, w_gate_out, w_out):
    head_count = w_beta.shape[1]
    batch_size, seq_len, unused = normed.shape
    source = low(normed)
    queries = short_conv(low_back(product(source, w_query)), conv_query).reshape(batch_size, seq_len, head_count, -1)
    key_vecs = short_conv(low_back(product(source, w_key)), conv_key).reshape(batch_size, seq_len, head_count, -1)
    values = short_conv(low_back(product(source, w_value)), conv_value).reshape(batch_size, seq_len, head_count, -1)
    queries = unit_rows(queries) * queries.shape[-1] ** (-0.5)
    key_vecs = unit_rows(key_vecs)
    beta_gates = jax.nn.sigmoid(low_back(product(source, w_beta)))
    log_decay = -jnp.exp(log_rate) * jax.nn.softplus(low_back(product(source, w_decay)) + step_bias)
    mixed = delta_rule(queries, key_vecs, values, beta_gates, log_decay)
    mixed = mixed * lax.rsqrt(lax.optimization_barrier(jnp.mean(mixed * mixed, axis=-1, keepdims=True)) + 1e-05) * out_gain.reshape(head_count, -1)
    gate_pre = low_back(product(source, w_gate_out)).reshape(batch_size, seq_len, head_count, -1)
    mixed = (mixed * jax.nn.silu(gate_pre)).reshape(batch_size, seq_len, -1)
    return product(low(mixed), w_out)

def feed_forward(normed, w_ffn_gate, w_ffn_up, w_ffn_down):
    source = low(normed)
    gate_pre = low_back(product(source, w_ffn_gate))
    up_pre = low_back(product(source, w_ffn_up))
    hidden = low(jax.nn.silu(gate_pre) * up_pre)
    return product(hidden, w_ffn_down)

def full_layer(activations, params):
    middle = activations + token_mixer(rms_norm(activations, params[0]), *params[1:14])
    return middle + feed_forward(rms_norm(middle, params[14]), *params[15:18])

def reference(inputs, cotangent, norm_gain1, w_query, w_key, w_value, conv_query, conv_key, conv_value, w_beta, w_decay, log_rate, step_bias, out_gain, w_gate_out, w_out, norm_gain2, w_ffn_gate, w_ffn_up, w_ffn_down):
    weights_all = (norm_gain1, w_query, w_key, w_value, conv_query, conv_key, conv_value, w_beta, w_decay, log_rate, step_bias, out_gain, w_gate_out, w_out, norm_gain2, w_ffn_gate, w_ffn_up, w_ffn_down)
    first_params = tuple((w[0].astype(jnp.float32) for w in weights_all))
    second_params = tuple((w[1].astype(jnp.float32) for w in weights_all))
    shape_in = inputs.shape
    source = inputs.astype(jnp.float32).reshape(shape_in[0] * shape_in[1], shape_in[2], shape_in[3])
    target = cotangent.astype(jnp.float32).reshape(source.shape)

    def two_layers(activations, sent_zero, params_one, params_two):
        between = low_back(low(full_layer(activations, params_one)) + sent_zero)
        return (full_layer(between, params_two), between)
    zero_field = jnp.zeros_like(source)
    final_out, pull_back, between = jax.vjp(two_layers, source, zero_field, first_params, second_params, has_aux=True)
    d_source, d_sent, grads_one, grads_two = pull_back(target)
    hidden_out = jnp.stack([between, final_out]).reshape((2,) + shape_in).astype(jnp.bfloat16)
    input_grad = jnp.stack([d_source, d_sent]).reshape((2,) + shape_in).astype(jnp.bfloat16)
    grads = [jnp.stack([grads_one[i], grads_two[i]]) for i in range(18)]
    return (hidden_out, input_grad, grads[0], grads[1], grads[2], grads[3], grads[4], grads[5], grads[6], grads[7], grads[8], grads[9], grads[10], grads[11], grads[12], grads[13], grads[14], grads[15], grads[16], grads[17])
```

```python
import functools

import jax
import jax.numpy as jnp
from jax import lax
from jax.experimental import pallas as pl
from jax.experimental.pallas import tpu as pltpu
from jax.sharding import PartitionSpec as P

F32 = jnp.float32
BF16 = jnp.bfloat16
MESH = pl.DeviceIdType.MESH
LEN = 128
ROWS = 64
HEADS = 2
DK = 128
DV = 256
SCALE = DK**-0.5
PQ, PK, PV, PG, PB, PEND = 0, 256, 512, 1024, 1536, 1664
FPAD = 768
NA = PEND + 512
NB = 3 * FPAD


def dot(left, right):
    return jnp.dot(left.astype(BF16), right.astype(BF16), preferred_element_type=F32)


def dot_nt(left, right):
    return lax.dot_general(
        left.astype(BF16),
        right.astype(BF16),
        (((1,), (1,)), ((), ())),
        preferred_element_type=F32,
    )


def dot_full(left, right):
    return jnp.dot(left, right, precision=lax.Precision.HIGHEST, preferred_element_type=F32)


def sigmoid(v):
    return 1.0 / (1.0 + jnp.exp(-v))


def rows_of(shape):
    return lax.broadcasted_iota(jnp.int32, shape, 0)


def shift_down(v, steps):
    if steps == 0:
        return v
    return jnp.where(rows_of(v.shape) >= steps, pltpu.roll(v, steps, 0), 0.0)


def shift_up(v, steps):
    if steps == 0:
        return v
    count = v.shape[0]
    return jnp.where(rows_of(v.shape) < count - steps, pltpu.roll(v, count - steps, 0), 0.0)


def conv_sum(v, taps):
    total = v * taps[3:4]
    for j in range(3):
        total = total + shift_down(v, 3 - j) * taps[j : j + 1]
    return total


def silu_slope(z):
    s = sigmoid(z)
    return s * (1.0 + z * (1.0 - s))


def unit_inverses(systems):
    row = lax.broadcasted_iota(jnp.int32, (LEN, LEN), 0)
    col = lax.broadcasted_iota(jnp.int32, (LEN, LEN), 1)
    eye = jnp.where(row == col, 1.0, 0.0)

    def band(level):
        same = (row >> (level + 1)) == (col >> (level + 1))
        return same & (((row >> level) & 1) == 1) & (((col >> level) & 1) == 0)

    first = band(0)
    inverses = [eye - jnp.where(first, m, 0.0) for m in systems]
    for level in range(1, 7):
        at = band(level)
        halves = [dot(t, jnp.where(at, m, 0.0)) for t, m in zip(inverses, systems)]
        inverses = [t - dot(x, t) for t, x in zip(inverses, halves)]
    return inverses


def rms_back(z, gain, dn):
    inv = lax.rsqrt(jnp.mean(z * z, axis=-1, keepdims=True) + 1e-06)
    hat = z * inv
    weighted = dn * gain
    dz = (weighted - hat * jnp.mean(weighted * hat, axis=-1, keepdims=True)) * inv
    return dz, jnp.sum(dn * hat, axis=0, keepdims=True)


def layer_kernel(
    inp, cot, g1, wq, wk, wv, cvq, cvk, cvv, wba, lrate, sbias, ogain, wgo, wo, g2, wfg, wfu, wfd,
    hid, ing, a1, dpr, a2, dgu, dho, mix, dyo, act, small,
    xbuf, ybuf, nbuf, hbuf, dbuf, gbuf,
    part, r1, r2, fwd, hrow, drow, acc,
    proj, zsum, qkv, gpre, onorm, dmix, upg, upu,
    tinv, amat, dmat, emat, umat, cols, gains,
    rs_s, rs_r, ag_s, ag_r, hop_s, hop_r, ga_s, ga_r,
):
    section = lax.axis_index("section")
    t = lax.axis_index("tensor")
    hi = t // 2
    core = t % 2
    sib = hi * 2 + (1 - core)
    opp = (1 - hi) * 2 + core
    other = 1 - section

    def remote(src, dst, ssem, rsem, device):
        return pltpu.make_async_remote_copy(
            src_ref=src, dst_ref=dst, send_sem=ssem, recv_sem=rsem,
            device_id=device, device_id_type=MESH,
        )

    barrier = pltpu.get_barrier_semaphore()
    for step in range(1, 4):
        pl.semaphore_signal(
            barrier, inc=1, device_id={"tensor": (t + step) % 4}, device_id_type=MESH
        )
    for step in range(4):
        pl.semaphore_signal(
            barrier, inc=1, device_id={"section": other, "tensor": (t + step) % 4},
            device_id_type=MESH,
        )
    pl.semaphore_wait(barrier, 7)

    def reduce_scatter(ph):
        far = remote(
            part.at[ph, 2 * (1 - hi) + 1 - core], r1.at[ph, 0], rs_s.at[ph, 0], rs_r.at[ph, 0],
            {"tensor": sib},
        )
        near = remote(
            part.at[ph, 2 * hi + 1 - core], r1.at[ph, 1], rs_s.at[ph, 1], rs_r.at[ph, 1],
            {"tensor": sib},
        )
        far.start()
        near.start()
        far.wait_recv()
        fwd[ph] = (part[ph, opp].astype(F32) + r1[ph, 0].astype(F32)).astype(BF16)
        cross = remote(
            fwd.at[ph], r2.at[ph], rs_s.at[ph, 2], rs_r.at[ph, 2], {"tensor": opp}
        )
        cross.start()
        near.wait_recv()
        acc[...] = part[ph, t].astype(F32) + r1[ph, 1].astype(F32)
        cross.wait_recv()
        total = acc[...] + r2[ph].astype(F32)
        far.wait_send()
        near.wait_send()
        cross.wait_send()
        return total

    class Gather:
        def __init__(self, buf, k):
            self.far = remote(buf.at[t], buf.at[t], ag_s.at[k, 0], ag_r.at[k, 0], {"tensor": opp})
            self.near = remote(buf.at[t], buf.at[t], ag_s.at[k, 1], ag_r.at[k, 1], {"tensor": sib})
            self.pass_on = remote(
                buf.at[opp], buf.at[opp], ag_s.at[k, 2], ag_r.at[k, 2], {"tensor": sib}
            )

        def start(self):
            self.far.start()
            self.near.start()

        def middle(self):
            self.far.wait_recv()
            self.pass_on.start()

        def finish(self):
            self.near.wait_recv()
            self.pass_on.wait_recv()
            self.far.wait_send()
            self.near.wait_send()
            self.pass_on.wait_send()

    def hop_send(buf, dst, k):
        copies = [
            remote(
                buf.at[t], dst.at[t], hop_s.at[k, y], hop_r.at[k, hi],
                {"section": other, "tensor": 2 * y + core},
            )
            for y in range(2)
        ]
        for copy in copies:
            copy.start()
        for copy in copies:
            copy.wait_send()

    def hop_receive(dst, k):
        passes = []
        for y in range(2):
            at = 2 * y + core
            remote(
                dst.at[at], dst.at[at], hop_s.at[k, y], hop_r.at[k, y],
                {"section": other, "tensor": t},
            ).wait_recv()
            pass_on = remote(
                dst.at[at], dst.at[at], hop_s.at[k, 2 + y], hop_r.at[k, 2 + y], {"tensor": sib}
            )
            pass_on.start()
            passes.append(pass_on)
        for pass_on in passes:
            pass_on.wait_recv()
        for pass_on in passes:
            pass_on.wait_send()

    def put_part(ph, value):
        for c in range(4):
            part[ph, c] = value[ROWS * c : ROWS * (c + 1)].astype(BF16)

    pairs = [(s, h) for s in range(2) for h in range(HEADS)]
    row = lax.broadcasted_iota(jnp.int32, (LEN, LEN), 0)
    col = lax.broadcasted_iota(jnp.int32, (LEN, LEN), 1)
    within = row >= col
    strict = row > col
    gain1 = g1[...].astype(F32)
    gain2 = g2[...].astype(F32)
    ogains = ogain[...].astype(F32)
    taps_q = cvq[...].astype(F32)
    taps_k = cvk[...].astype(F32)
    taps_v = cvv[...].astype(F32)

    def seq(s):
        return slice(LEN * s, LEN * (s + 1))

    def qc(h):
        return slice(PQ + DK * h, PQ + DK * (h + 1))

    def kc(h):
        return slice(PK + DK * h, PK + DK * (h + 1))

    def vc(h):
        return slice(PV + DV * h, PV + DV * (h + 1))

    def hv(h):
        return slice(DV * h, DV * (h + 1))

    @pl.when(section == 0)
    def _():
        for c in range(4):
            xbuf[c] = inp[ROWS * c : ROWS * (c + 1)]

    @pl.when(section == 1)
    def _():
        hop_receive(xbuf, 0)

    for c in range(4):
        x = xbuf[c].astype(F32)
        inv = lax.rsqrt(jnp.mean(x * x, axis=-1, keepdims=True) + 1e-06)
        a1[ROWS * c : ROWS * (c + 1)] = (x * inv * gain1).astype(BF16)
    source = a1[...]
    proj[:, PQ:PK] = dot(source, wq[...])
    proj[:, PK:PV] = dot(source, wk[...])
    proj[:, PV:PG] = dot(source, wv[...])
    pba = dot(source, wba[...])
    gpre[...] = dot(source, wgo[...])

    lane = lax.broadcasted_iota(jnp.int32, (LEN, LEN), 1)
    ltri = jnp.where(within, 1.0, 0.0)
    utri = jnp.where(row <= col, 1.0, 0.0)
    betas, decays, slopes = [], [], []
    for s, h in pairs:
        betas.append(sigmoid(pba[seq(s), h : h + 1]))
        pre = pba[seq(s), 2 + h : 3 + h] + sbias[0:1, h : h + 1]
        soft = jnp.maximum(pre, 0.0) + jnp.log1p(jnp.exp(-jnp.abs(pre)))
        rate = -jnp.exp(lrate[0:1, h : h + 1])
        decays.append(rate * soft)
        slopes.append(rate * sigmoid(pre))
    packed = jnp.zeros((LEN, LEN), F32)
    for i in range(4):
        packed = jnp.where(lane == i, decays[i], packed)
    cums = dot_full(ltri, packed)

    for s, h in pairs:
        z = conv_sum(proj[seq(s), qc(h)], taps_q[:, DK * h : DK * (h + 1)])
        zsum[seq(s), qc(h)] = z
        c = z * sigmoid(z)
        rq = lax.rsqrt(jnp.sum(c * c, axis=-1, keepdims=True) + 1e-06)
        qkv[seq(s), qc(h)] = c * (rq * SCALE)
        z = conv_sum(proj[seq(s), kc(h)], taps_k[:, DK * h : DK * (h + 1)])
        zsum[seq(s), kc(h)] = z
        c = z * sigmoid(z)
        rk = lax.rsqrt(jnp.sum(c * c, axis=-1, keepdims=True) + 1e-06)
        qkv[seq(s), kc(h)] = c * rk
        z = conv_sum(proj[seq(s), vc(h)], taps_v[:, hv(h)])
        zsum[seq(s), vc(h)] = z
        qkv[seq(s), vc(h)] = z * sigmoid(z)
        i = 2 * s + h
        cols[0, i] = jnp.broadcast_to(betas[i], (LEN, LEN))
        cols[1, i] = jnp.broadcast_to(decays[i], (LEN, LEN))
        cols[2, i] = jnp.broadcast_to(slopes[i], (LEN, LEN))
        cols[3, i] = jnp.broadcast_to(rq, (LEN, LEN))
        cols[4, i] = jnp.broadcast_to(rk, (LEN, LEN))

    systems = []
    for i, (s, h) in enumerate(pairs):
        cum = jnp.broadcast_to(cums[:, i : i + 1], (LEN, LEN))
        gaps = cum - cum.T
        decay = jnp.where(within, jnp.exp(jnp.where(within, gaps, 0.0)), 0.0)
        dmat[i] = decay
        kn = qkv[seq(s), kc(h)]
        e = jnp.where(strict, dot_nt(kn, kn) * decay, 0.0)
        emat[i] = e
        systems.append(cols[0, i] * e)
        amat[i] = dot_nt(qkv[seq(s), qc(h)], kn) * decay
    for i, inverse in enumerate(unit_inverses(systems)):
        tinv[i] = inverse.astype(BF16)
    for i, (s, h) in enumerate(pairs):
        w = qkv[seq(s), vc(h)] * cols[0, i][:, 0:1]
        umat[i] = dot(tinv[i], w).astype(BF16)
    for i, (s, h) in enumerate(pairs):
        o = dot(amat[i], umat[i])
        ro = lax.rsqrt(jnp.mean(o * o, axis=-1, keepdims=True) + 1e-05)
        cols[5, i] = jnp.broadcast_to(ro, (LEN, LEN))
        on = o * ro
        onorm[seq(s), hv(h)] = on
        gp = gpre[seq(s), hv(h)]
        mix[seq(s), hv(h)] = (on * ogains[:, hv(h)] * (gp * sigmoid(gp))).astype(BF16)

    put_part(0, dot(mix[...], wo[...]))
    hrow[...] = xbuf[t].astype(F32) + reduce_scatter(0)
    h_mine = hrow[...]
    inv = lax.rsqrt(jnp.mean(h_mine * h_mine, axis=-1, keepdims=True) + 1e-06)
    nbuf[t] = (h_mine * inv * gain2).astype(BF16)
    gather = Gather(nbuf, 0)
    gather.start()
    gather.middle()
    gather.finish()
    for c in range(4):
        a2[ROWS * c : ROWS * (c + 1)] = nbuf[c]
    source = a2[...]
    upg[...] = dot(source, wfg[...])
    upu[...] = dot(source, wfu[...])
    ug = upg[...]
    s_act = (ug * sigmoid(ug) * upu[...]).astype(BF16)
    act[:, 704:FPAD] = jnp.zeros((2 * LEN, FPAD - 704), BF16)
    act[:, 0:704] = s_act
    put_part(1, dot(s_act, wfd[...]))
    ybuf[t] = (hrow[...] + reduce_scatter(1)).astype(BF16)
    hidden = Gather(ybuf, 1)

    @pl.when(section == 0)
    def _():
        hop_send(ybuf, xbuf, 0)

    hidden.start()

    @pl.when(section == 1)
    def _():
        for c in range(4):
            dbuf[c] = cot[ROWS * c : ROWS * (c + 1)]

    @pl.when(section == 0)
    def _():
        hidden.middle()
        hop_receive(dbuf, 1)

    for c in range(4):
        dyo[ROWS * c : ROWS * (c + 1)] = dbuf[c]
    ds = dot_nt(dyo[...], wfd[...])
    ug = upg[...]
    uu = upu[...]
    sg = sigmoid(ug)
    pad = jnp.zeros((2 * LEN, FPAD - 704), BF16)
    dgu[:, 704:FPAD] = pad
    dgu[:, FPAD + 704 :] = pad
    dgu[:, 0:704] = (ds * uu * (sg * (1.0 + ug * (1.0 - sg)))).astype(BF16)
    dgu[:, FPAD : FPAD + 704] = (ds * (ug * sg)).astype(BF16)
    put_part(2, dot_nt(dgu[:, 0:704], wfg[...]) + dot_nt(dgu[:, FPAD : FPAD + 704], wfu[...]))
    dn = reduce_scatter(2)
    dz, dgain2 = rms_back(hrow[...], gain2, dn)
    drow[...] = dbuf[t].astype(F32) + dz
    hbuf[t] = drow[...].astype(BF16)
    gather = Gather(hbuf, 2)
    gather.start()

    @pl.when(section == 1)
    def _():
        hidden.middle()

    gather.middle()
    gather.finish()
    for c in range(4):
        dho[ROWS * c : ROWS * (c + 1)] = hbuf[c]
    dmix[...] = dot_nt(dho[...], wo[...])

    small[...] = jnp.zeros_like(small)
    douts = [jnp.zeros((1, DV), F32) for _ in range(HEADS)]
    dos = []
    for i, (s, h) in enumerate(pairs):
        dm = dmix[seq(s), hv(h)]
        gp = gpre[seq(s), hv(h)]
        sg = sigmoid(gp)
        on = onorm[seq(s), hv(h)]
        og = ogains[:, hv(h)]
        dgate = dm * on
        dpr[seq(s), PG + DV * h : PG + DV * (h + 1)] = (
            dgate * og * (sg * (1.0 + gp * (1.0 - sg)))
        ).astype(BF16)
        silu_g = gp * sg
        douts[h] = douts[h] + jnp.sum(dgate * silu_g, axis=0, keepdims=True)
        don = dm * silu_g * og
        ro = cols[5, i][:, 0:1]
        do = ro * (don - on * jnp.mean(don * on, axis=-1, keepdims=True))
        dos.append(do.astype(BF16))
    for h in range(HEADS):
        small[6:7, hv(h)] = douts[h]
    das = [dot_nt(dos[i], umat[i]) for i in range(4)]
    dus = [dot(amat[i].T, dos[i]) for i in range(4)]
    dws = [dot(tinv[i].astype(F32).T, dus[i]) for i in range(4)]
    dms = [jnp.where(strict, -dot_nt(dws[i], umat[i]), 0.0) for i in range(4)]
    dbetas, dcs, dqs, dks = [], [], [], []
    for i, (s, h) in enumerate(pairs):
        beta = cols[0, i]
        e = emat[i]
        decay = dmat[i]
        v = qkv[seq(s), vc(h)]
        de = dms[i] * e
        dbetas.append(
            jnp.sum(dws[i] * v, axis=-1, keepdims=True) + jnp.sum(de, axis=-1, keepdims=True)
        )
        dgap = das[i] * amat[i] + de * beta
        dcs.append(jnp.sum(dgap - dgap.T, axis=-1, keepdims=True))
        dqk = das[i] * decay
        dkk = dms[i] * beta * decay
        kn = qkv[seq(s), kc(h)]
        qn = qkv[seq(s), qc(h)]
        dqs.append(dot(dqk, kn))
        dks.append(dot(dqk.T, qn) + dot(dkk + dkk.T, kn))
    packed = jnp.zeros((LEN, LEN), F32)
    for i in range(4):
        packed = jnp.where(lane == i, dcs[i], packed)
    dgs = dot_full(utri, packed)

    dcq = [jnp.zeros((1, DK), F32) for _ in range(4 * HEADS)]
    dck = [jnp.zeros((1, DK), F32) for _ in range(4 * HEADS)]
    dcv = [jnp.zeros((1, DV), F32) for _ in range(4 * HEADS)]

    def conv_back(dz, at_rows, at_cols, taps, sums, h):
        pre = proj[at_rows, at_cols]
        total = dz * taps[3:4]
        for j in range(3):
            total = total + shift_up(dz, 3 - j) * taps[j : j + 1]
        for j in range(4):
            sums[4 * h + j] = sums[4 * h + j] + jnp.sum(
                dz * shift_down(pre, 3 - j), axis=0, keepdims=True
            )
        dpr[at_rows, at_cols] = total.astype(BF16)

    for i, (s, h) in enumerate(pairs):
        qn = qkv[seq(s), qc(h)]
        dq = dqs[i]
        dc = (cols[3, i] * SCALE) * (
            dq - qn * (jnp.sum(qn * dq, axis=-1, keepdims=True) * (1.0 / (SCALE * SCALE)))
        )
        dz = dc * silu_slope(zsum[seq(s), qc(h)])
        conv_back(dz, seq(s), qc(h), taps_q[:, DK * h : DK * (h + 1)], dcq, h)
        kn = qkv[seq(s), kc(h)]
        dk = dks[i]
        dc = cols[4, i] * (dk - kn * jnp.sum(kn * dk, axis=-1, keepdims=True))
        dz = dc * silu_slope(zsum[seq(s), kc(h)])
        conv_back(dz, seq(s), kc(h), taps_k[:, DK * h : DK * (h + 1)], dck, h)
        dv = dws[i] * cols[0, i][:, 0:1]
        dz = dv * silu_slope(zsum[seq(s), vc(h)])
        conv_back(dz, seq(s), vc(h), taps_v[:, hv(h)], dcv, h)
    for h in range(HEADS):
        for j in range(4):
            small[2 + j : 3 + j, DK * h : DK * (h + 1)] = dcq[4 * h + j]
            small[2 + j : 3 + j, 256 + DK * h : 256 + DK * (h + 1)] = dck[4 * h + j]
            small[2 + j : 3 + j, 512 + DV * h : 512 + DV * (h + 1)] = dcv[4 * h + j]
    lane_row = lax.broadcasted_iota(jnp.int32, (1, LEN), 1)
    scal = jnp.zeros((1, LEN), F32)
    for s in range(2):
        block = jnp.zeros((LEN, LEN), F32)
        for h in range(HEADS):
            i = 2 * s + h
            beta = cols[0, i]
            dg = jnp.broadcast_to(dgs[:, i : i + 1], (LEN, LEN))
            dpb = dbetas[i] * beta * (1.0 - beta)
            dpa = dg * cols[2, i]
            block = jnp.where(lane == h, dpb, block)
            block = jnp.where(lane == 2 + h, dpa, block)
            scal = scal + jnp.where(
                lane_row == h, jnp.sum(dg * cols[1, i], axis=0, keepdims=True), 0.0
            )
            scal = scal + jnp.where(lane_row == 2 + h, jnp.sum(dpa, axis=0, keepdims=True), 0.0)
        dpr[seq(s), PB:PEND] = block.astype(BF16)
    small[6:7, 512:640] = scal

    value = dot_nt(dpr[:, PQ:PK], wq[...])
    value = value + dot_nt(dpr[:, PK:PV], wk[...])
    value = value + dot_nt(dpr[:, PV:PG], wv[...])
    value = value + dot_nt(dpr[:, PG:PB], wgo[...])
    value = value + dot_nt(dpr[:, PB:PEND], wba[...])
    put_part(3, value)
    dn = reduce_scatter(3)
    dz, dgain1 = rms_back(xbuf[t].astype(F32), gain1, dn)
    gbuf[t] = (drow[...] + dz).astype(BF16)
    back = Gather(gbuf, 3)

    @pl.when(section == 1)
    def _():
        hop_send(gbuf, dbuf, 1)

    back.start()
    zero = jnp.zeros((6, 1024), F32)
    gains[0] = jnp.concatenate([dgain1, dgain2, zero], axis=0)
    sums = [
        remote(
            gains.at[0], gains.at[step], ga_s.at[step - 1], ga_r.at[step - 1],
            {"tensor": (t + step) % 4},
        )
        for step in range(1, 4)
    ]
    for copy in sums:
        copy.start()
    back.middle()
    hidden.finish()
    for c in range(4):
        hid[ROWS * c : ROWS * (c + 1)] = ybuf[c]
    for copy in sums:
        copy.wait_recv()
    total = gains[0] + gains[1] + gains[2] + gains[3]
    small[0:2] = total[0:2]
    back.finish()
    for c in range(4):
        ing[ROWS * c : ROWS * (c + 1)] = gbuf[c]
    for copy in sums:
        copy.wait_send()


def run_layer(args):
    tokens = 2 * LEN
    results = (
        ((tokens, 1024), BF16), ((tokens, 1024), BF16), ((tokens, 1024), BF16),
        ((tokens, PEND), BF16), ((tokens, 1024), BF16), ((tokens, 2 * FPAD), BF16),
        ((tokens, 1024), BF16), ((tokens, 512), BF16), ((tokens, 1024), BF16),
        ((tokens, FPAD), BF16), ((8, 1024), F32),
    )
    chunk = (4, ROWS, 1024)
    buffers = [pltpu.VMEM(chunk, BF16)] * 6 + [
        pltpu.VMEM((4,) + chunk, BF16),
        pltpu.VMEM((4, 2, ROWS, 1024), BF16),
        pltpu.VMEM((4, ROWS, 1024), BF16),
        pltpu.VMEM((4, ROWS, 1024), BF16),
        pltpu.VMEM((ROWS, 1024), F32),
        pltpu.VMEM((ROWS, 1024), F32),
        pltpu.VMEM((ROWS, 1024), F32),
        pltpu.VMEM((tokens, 1024), F32),
        pltpu.VMEM((tokens, 1024), F32),
        pltpu.VMEM((tokens, 1024), F32),
        pltpu.VMEM((tokens, 512), F32),
        pltpu.VMEM((tokens, 512), F32),
        pltpu.VMEM((tokens, 512), F32),
        pltpu.VMEM((tokens, 704), F32),
        pltpu.VMEM((tokens, 704), F32),
        pltpu.VMEM((4, LEN, LEN), BF16),
        pltpu.VMEM((4, LEN, LEN), F32),
        pltpu.VMEM((4, LEN, LEN), F32),
        pltpu.VMEM((4, LEN, LEN), F32),
        pltpu.VMEM((4, LEN, DV), BF16),
        pltpu.VMEM((6, 4, LEN, LEN), F32),
        pltpu.VMEM((4, 8, 1024), F32),
    ]
    sems = [
        pltpu.SemaphoreType.DMA((4, 3)), pltpu.SemaphoreType.DMA((4, 3)),
        pltpu.SemaphoreType.DMA((4, 3)), pltpu.SemaphoreType.DMA((4, 3)),
        pltpu.SemaphoreType.DMA((2, 4)), pltpu.SemaphoreType.DMA((2, 4)),
        pltpu.SemaphoreType.DMA((3,)), pltpu.SemaphoreType.DMA((3,)),
    ]
    return pl.pallas_call(
        layer_kernel,
        out_shape=[jax.ShapeDtypeStruct(s, d) for s, d in results],
        in_specs=[pl.BlockSpec(memory_space=pltpu.VMEM)] * len(args),
        out_specs=[pl.BlockSpec(memory_space=pltpu.VMEM)] * len(results),
        scratch_shapes=buffers + sems,
        compiler_params=pltpu.CompilerParams(
            collective_id=0, has_side_effects=True, vmem_limit_bytes=58 * 1024 * 1024
        ),
        name="layer",
    )(*args)


def grad_kernel(
    a1, dpr, a2, dgu, dho, mix, dyo, act, small,
    gq, gk, gv, gb, gd, ggo, gout, gfg, gfu, gfd,
    dg1, dcq, dck, dcv, dlr, dsb, dog, dg2,
    ga, gz, a1p, a1m, a2p, a2m, b1p, b1m, b2p, b2m,
    ha, hb, c1p, c1m, c2p, c2m, d1p, d1m, d2p, d2m,
    sx, sz, send, recv, ssend, srecv,
):
    place = lax.axis_index("dp")
    z = place // 4
    x = place % 4

    def at_x(step):
        return {"dp": z * 4 + (x + step) % 4}

    def at_z(step):
        return {"dp": ((z + step) % 4) * 4 + x}

    def remote(src, dst, ssem, rsem, device):
        return pltpu.make_async_remote_copy(
            src_ref=src, dst_ref=dst, send_sem=ssem, recv_sem=rsem,
            device_id=device, device_id_type=MESH,
        )

    barrier = pltpu.get_barrier_semaphore()
    for step in range(1, 4):
        pl.semaphore_signal(barrier, inc=1, device_id=at_x(step), device_id_type=MESH)
        pl.semaphore_signal(barrier, inc=1, device_id=at_z(step), device_id_type=MESH)

    def outer(left, right, width, store):
        for rows in range(4):
            lt = left[:, 256 * rows : 256 * (rows + 1)].T
            for start in range(0, width, 256):
                size = min(256, width - start)
                value = jnp.dot(
                    lt, right[:, start : start + size], preferred_element_type=F32
                ).astype(BF16)
                for part in range(4):
                    store(rows, part, start, size, value[ROWS * part : ROWS * (part + 1)])

    def into_a(offset):
        def store(zz, xx, start, size, value):
            ga[xx, zz, :, offset + start : offset + start + size] = value
        return store

    def into_b(offset):
        def store(zz, xx, start, size, value):
            gz[zz, xx, :, offset + start : offset + start + size] = value
        return store

    outer(a1, dpr, PEND, into_a(0))
    outer(dho, mix, 512, into_a(PEND))
    outer(a2, dgu, 2 * FPAD, into_b(0))
    outer(dyo, act, FPAD, into_b(2 * FPAD))

    pl.semaphore_wait(barrier, 6)

    class Ring:
        def __init__(self, g, me, where, bufs, k, half):
            one_p, one_m, two_p, two_m = bufs
            self.g, self.me, self.bufs, self.half = g, me, bufs, half
            self.right = right = (me + 1) % 4
            self.left = left = (me + 3) % 4
            far = (me + 2) % 4
            lo, up = pl.ds(0, half), pl.ds(half, half)
            self.lo, self.up = lo, up
            self.p1 = remote(g.at[far, lo], one_p, send.at[k, 0], recv.at[k, 0], where(1))
            self.m1 = remote(g.at[far, up], one_m, send.at[k, 1], recv.at[k, 1], where(3))
            self.p2 = remote(g.at[right, up], two_p.at[up], send.at[k, 2], recv.at[k, 2], where(1))
            self.m2 = remote(g.at[left, lo], two_m.at[lo], send.at[k, 3], recv.at[k, 3], where(3))
            self.p3 = remote(g.at[right, lo], two_p.at[lo], send.at[k, 4], recv.at[k, 4], where(1))
            self.m3 = remote(g.at[left, up], two_m.at[up], send.at[k, 5], recv.at[k, 5], where(3))

        def start(self):
            for copy in (self.p1, self.m1, self.p2, self.m2):
                copy.start()

        def relay(self):
            one_p, one_m, two_p, two_m = self.bufs
            g, lo, up = self.g, self.lo, self.up
            self.p1.wait_recv()
            add_into(g.at[self.right, lo], one_p)
            self.p3.start()
            self.m1.wait_recv()
            add_into(g.at[self.left, up], one_m)
            self.m3.start()

        def arrive(self):
            for copy in (self.p2, self.m2, self.p3, self.m3):
                copy.wait_recv()

        def sent(self):
            for copy in (self.p1, self.m1, self.p2, self.m2, self.p3, self.m3):
                copy.wait_send()

    def add_into(ref, other):
        if len(other.shape) == 3:
            @pl.loop(0, other.shape[0])
            def _(c):
                ref[c] = (ref[c].astype(F32) + other[c].astype(F32)).astype(BF16)
        else:
            ref[...] = (ref[...].astype(F32) + other[...].astype(F32)).astype(BF16)

    sx[0] = small[...]
    small_x = [
        remote(sx.at[0], sx.at[step], ssend.at[step - 1], srecv.at[step - 1], at_x(step))
        for step in range(1, 4)
    ]
    small_z = [
        remote(sz.at[0], sz.at[step], ssend.at[step + 2], srecv.at[step + 2], at_z(step))
        for step in range(1, 4)
    ]
    first_a = Ring(ga, x, at_x, (a1p, a1m, a2p, a2m), 0, 2)
    first_b = Ring(gz, z, at_z, (b1p, b1m, b2p, b2m), 1, 2)
    second_a = Ring(ha, z, at_z, (c1p, c1m, c2p, c2m), 2, 32)
    second_b = Ring(hb, x, at_x, (d1p, d1m, d2p, d2m), 3, 32)
    first_a.start()
    first_b.start()
    for copy in small_x:
        copy.start()
    first_a.relay()
    first_b.relay()
    for copy in small_x:
        copy.wait_recv()
    sz[0] = sx[0] + sx[1] + sx[2] + sx[3]
    for copy in small_z:
        copy.start()

    def merge(ring, out):
        _, _, two_p, two_m = ring.bufs

        @pl.loop(0, 4)
        def _(c):
            out[c] = (
                ring.g[ring.me, c].astype(F32) + two_p[c].astype(F32) + two_m[c].astype(F32)
            ).astype(BF16)

    first_a.arrive()
    merge(first_a, ha)
    second_a.start()
    first_b.arrive()
    merge(first_b, hb)
    second_b.start()
    second_a.relay()
    second_b.relay()
    for copy in small_z:
        copy.wait_recv()
    sums = sz[0] + sz[1] + sz[2] + sz[3]
    dg1[...] = sums[0:1]
    dg2[...] = sums[1:2]
    dcq[...] = sums[2:6, 0:256]
    dck[...] = sums[2:6, 256:512]
    dcv[...] = sums[2:6, 512:1024]
    dog[...] = sums[6:7, 0:512]
    dlr[...] = sums[6:7, 512:514]
    dsb[...] = sums[6:7, 514:516]

    def total(ring, start, size):
        _, _, two_p, two_m = ring.bufs
        at = slice(start, start + size)
        return (
            ring.g[ring.me, :, at].astype(F32)
            + two_p[:, at].astype(F32)
            + two_m[:, at].astype(F32)
        )

    second_a.arrive()
    gq[...] = total(second_a, PQ, 256)
    gk[...] = total(second_a, PK, 256)
    gv[...] = total(second_a, PV, 512)
    ggo[...] = total(second_a, PG, 512)
    pair = total(second_a, PB, 128)
    gb[...] = pair[:, 0:2]
    gd[...] = pair[:, 2:4]
    gout[...] = total(second_a, PEND, 512).T
    second_b.arrive()
    gfg[...] = total(second_b, 0, FPAD)[:, 0:704]
    gfu[...] = total(second_b, FPAD, FPAD)[:, 0:704]
    gfd[...] = total(second_b, 2 * FPAD, FPAD).T[0:704]
    for ring in (first_a, first_b, second_a, second_b):
        ring.sent()
    for copy in small_x + small_z:
        copy.wait_send()


def run_grads(args):
    results = (
        (ROWS, 256), (ROWS, 256), (ROWS, 512), (ROWS, 2), (ROWS, 2), (ROWS, 512),
        (512, ROWS), (ROWS, 704), (ROWS, 704), (704, ROWS),
        (1, 1024), (4, 256), (4, 256), (4, 512), (1, 2), (1, 2), (1, 512), (1, 1024),
    )

    def first(n):
        return [pltpu.VMEM((2, ROWS, n), BF16)] * 2 + [pltpu.VMEM((4, ROWS, n), BF16)] * 2

    def second(n):
        return [pltpu.VMEM((ROWS // 2, n), BF16)] * 2 + [pltpu.VMEM((ROWS, n), BF16)] * 2

    buffers = (
        [pltpu.VMEM((4, 4, ROWS, NA), BF16), pltpu.VMEM((4, 4, ROWS, NB), BF16)]
        + first(NA)
        + first(NB)
        + [pltpu.VMEM((4, ROWS, NA), BF16), pltpu.VMEM((4, ROWS, NB), BF16)]
        + second(NA)
        + second(NB)
        + [pltpu.VMEM((4, 8, 1024), F32)] * 2
    )
    sems = [
        pltpu.SemaphoreType.DMA((4, 6)), pltpu.SemaphoreType.DMA((4, 6)),
        pltpu.SemaphoreType.DMA((6,)), pltpu.SemaphoreType.DMA((6,)),
    ]
    return pl.pallas_call(
        grad_kernel,
        out_shape=[jax.ShapeDtypeStruct(s, F32) for s in results],
        in_specs=[pl.BlockSpec(memory_space=pltpu.VMEM)] * len(args),
        out_specs=[pl.BlockSpec(memory_space=pltpu.VMEM)] * len(results),
        scratch_shapes=buffers + sems,
        compiler_params=pltpu.CompilerParams(
            collective_id=1, has_side_effects=True, vmem_limit_bytes=58 * 1024 * 1024
        ),
        name="grads",
    )(*args)


def per_device(
    inputs, cotangent, norm_gain1, w_query, w_key, w_value, conv_query, conv_key, conv_value,
    w_beta, w_decay, log_rate, step_bias, out_gain, w_gate_out, w_out, norm_gain2,
    w_ffn_gate, w_ffn_up, w_ffn_down,
):
    tokens = 2 * LEN
    width = inputs.shape[-1]
    wba = jnp.concatenate(
        [w_beta[0], w_decay[0], jnp.zeros((width, LEN - 4), BF16)], axis=1
    )
    out = run_layer((
        inputs.reshape(tokens, width), cotangent.reshape(tokens, width),
        norm_gain1, w_query[0], w_key[0], w_value[0],
        conv_query[0], conv_key[0], conv_value[0], wba, log_rate, step_bias, out_gain,
        w_gate_out[0], w_out[0], norm_gain2, w_ffn_gate[0], w_ffn_up[0], w_ffn_down[0],
    ))
    hidden, input_grad = (v.reshape((1,) + inputs.shape) for v in out[:2])
    (gq, gk, gv, gb, gd, ggo, gout, gfg, gfu, gfd, dg1, dcq, dck, dcv, dlr, dsb, dog, dg2) = (
        run_grads(tuple(out[2:]))
    )
    return (
        hidden, input_grad, dg1, gq[None], gk[None], gv[None], dcq[None], dck[None], dcv[None],
        gb[None], gd[None], dlr, dsb, dog, ggo[None], gout[None], dg2,
        gfg[None], gfu[None], gfd[None],
    )


def solution(mesh):
    three = P("section", None, "tensor")
    in_specs = (
        P(None, "dp", None, None), P(None, "dp", None, None), P("section", None),
        three, three, three, three, three, three, three, three,
        P("section", "tensor"), P("section", "tensor"), P("section", "tensor"),
        three, P("section", "tensor", None), P("section", None),
        three, three, P("section", "tensor", None),
    )
    spread = P("section", "dp", "tensor")
    out_specs = (
        P("section", None, "dp", None, None), P("section", None, "dp", None, None),
        P("section", None), spread, spread, spread, three, three, three, spread, spread,
        P("section", "tensor"), P("section", "tensor"), P("section", "tensor"),
        spread, P("section", "tensor", "dp"), P("section", None),
        spread, spread, P("section", "tensor", "dp"),
    )
    return jax.shard_map(
        per_device, mesh=mesh, in_specs=in_specs, out_specs=out_specs, check_vma=False
    )
```

```python
import functools

import jax
import jax.numpy as jnp
from jax import lax
from jax.experimental import pallas as pl
from jax.experimental.pallas import tpu as pltpu
from jax.sharding import PartitionSpec as P

F32 = jnp.float32
BF16 = jnp.bfloat16
MESH = pl.DeviceIdType.MESH
LEN = 128
ROWS = 64
HEADS = 2
DK = 128
DV = 256
SCALE = DK**-0.5
PQ, PK, PV, PG, PB, PEND = 0, 256, 512, 1024, 1536, 1664
FPAD = 768
NA = PEND + 512
NB = 3 * FPAD


def dot(left, right):
    return jnp.dot(left.astype(BF16), right.astype(BF16), preferred_element_type=F32)


def dot_nt(left, right):
    return lax.dot_general(
        left.astype(BF16),
        right.astype(BF16),
        (((1,), (1,)), ((), ())),
        preferred_element_type=F32,
    )


def dot_full(left, right):
    return jnp.dot(left, right, precision=lax.Precision.HIGHEST, preferred_element_type=F32)


def sigmoid(v):
    return 1.0 / (1.0 + jnp.exp(-v))


def rows_of(shape):
    return lax.broadcasted_iota(jnp.int32, shape, 0)


def shift_down(v, steps):
    if steps == 0:
        return v
    return jnp.where(rows_of(v.shape) >= steps, pltpu.roll(v, steps, 0), 0.0)


def shift_up(v, steps):
    if steps == 0:
        return v
    count = v.shape[0]
    return jnp.where(rows_of(v.shape) < count - steps, pltpu.roll(v, count - steps, 0), 0.0)


def conv_sum(v, taps):
    total = v * taps[3:4]
    for j in range(3):
        total = total + shift_down(v, 3 - j) * taps[j : j + 1]
    return total


def silu_slope(z):
    s = sigmoid(z)
    return s * (1.0 + z * (1.0 - s))


def unit_inverses(systems):
    row = lax.broadcasted_iota(jnp.int32, (LEN, LEN), 0)
    col = lax.broadcasted_iota(jnp.int32, (LEN, LEN), 1)
    eye = jnp.where(row == col, 1.0, 0.0)

    def band(level):
        same = (row >> (level + 1)) == (col >> (level + 1))
        return same & (((row >> level) & 1) == 1) & (((col >> level) & 1) == 0)

    first = band(0)
    inverses = [eye - jnp.where(first, m, 0.0) for m in systems]
    for level in range(1, 7):
        at = band(level)
        halves = [dot(t, jnp.where(at, m, 0.0)) for t, m in zip(inverses, systems)]
        inverses = [t - dot(x, t) for t, x in zip(inverses, halves)]
    return inverses


def rms_back(z, gain, dn):
    inv = lax.rsqrt(jnp.mean(z * z, axis=-1, keepdims=True) + 1e-06)
    hat = z * inv
    weighted = dn * gain
    dz = (weighted - hat * jnp.mean(weighted * hat, axis=-1, keepdims=True)) * inv
    return dz, jnp.sum(dn * hat, axis=0, keepdims=True)


def layer_kernel(
    inp, cot, g1, wq, wk, wv, cvq, cvk, cvv, wb, wd, lrate, sbias, ogain, wgo, wo, g2, wfg, wfu, wfd,
    hid, ing, a1, dpr, a2, dgu, dho, mix, dyo, act, small,
    part, r1, r2, fwd, hopb, gbuf, xrow, hrow, drow,
    proj, zsum, qkv, gpre, onorm, dmix, upg, upu, dact,
    tinv, amat, dmat, emat, umat, cols, gains,
    rs_s, rs_r, op_s, op_r, ag_s, ag_r, hop_s, hop_r, ga_s, ga_r,
):
    section = lax.axis_index("section")
    t = lax.axis_index("tensor")
    hi = t // 2
    core = t % 2
    sib = hi * 2 + (1 - core)
    opp = (1 - hi) * 2 + core
    other = 1 - section
    pieces = range(2)

    def remote(src, dst, ssem, rsem, device):
        return pltpu.make_async_remote_copy(
            src_ref=src, dst_ref=dst, send_sem=ssem, recv_sem=rsem,
            device_id=device, device_id_type=MESH,
        )

    barrier = pltpu.get_barrier_semaphore()
    for step in range(1, 4):
        pl.semaphore_signal(
            barrier, inc=1, device_id={"tensor": (t + step) % 4}, device_id_type=MESH
        )
    for step in range(4):
        pl.semaphore_signal(
            barrier, inc=1, device_id={"section": other, "tensor": (t + step) % 4},
            device_id_type=MESH,
        )
    pl.semaphore_wait(barrier, 7)

    def pair_sum(ph):
        return [
            remote(part.at[ph, 1 - core, p], r1.at[ph, p], rs_s.at[ph, p], rs_r.at[ph, p],
                   {"tensor": sib})
            for p in pieces
        ]

    def chip_swap(ph):
        return [
            remote(fwd.at[ph, p], r2.at[ph, p], op_s.at[ph, p], op_r.at[ph, p], {"tensor": opp})
            for p in pieces
        ]

    def pair_share(k):
        return [
            remote(gbuf.at[k, core, p], gbuf.at[k, core, p], ag_s.at[k, p], ag_r.at[k, p],
                   {"tensor": sib})
            for p in pieces
        ]

    def started(copies):
        for copy in copies:
            copy.start()

    def received(copies):
        for copy in copies:
            copy.wait_recv()

    def sent(copies):
        for copy in copies:
            copy.wait_send()

    def pair_total(ph, p):
        return part[ph, core, p].astype(F32) + r1[ph, p].astype(F32)

    def chip_total(ph, p):
        return fwd[ph, p].astype(F32) + r2[ph, p].astype(F32)

    def all_sum(ph, k, finish, between=None):
        firsts, swaps, shares = pair_sum(ph), chip_swap(ph), pair_share(k)
        started(firsts)
        for p in pieces:
            firsts[p].wait_recv()
            fwd[ph, p] = pair_total(ph, p).astype(BF16)
            swaps[p].start()
        if between is not None:
            between()
        for p in pieces:
            swaps[p].wait_recv()
            gbuf[k, core, p] = finish(p, chip_total(ph, p)).astype(BF16)
            shares[p].start()
        received(shares)
        sent(firsts + swaps + shares)

    def hop_send(ph, k):
        return [
            remote(fwd.at[ph, p], hopb.at[k, hi, p], hop_s.at[k, y, p], hop_r.at[k, hi, p],
                   {"section": other, "tensor": 2 * y + core})
            for p in pieces
            for y in range(2)
        ]

    def hop_receive(k, share, finish):
        shares = pair_share(share)
        for p in pieces:
            for y in range(2):
                remote(hopb.at[k, y, p], hopb.at[k, y, p], hop_s.at[k, y, p], hop_r.at[k, y, p],
                       {"section": other, "tensor": t}).wait_recv()
            value = (hopb[k, 0, p].astype(F32) + hopb[k, 1, p].astype(F32)).astype(BF16)
            gbuf[share, core, p] = finish(p, value)
            shares[p].start()
        received(shares)
        sent(shares)

    def put_part(ph, value):
        for s in range(2):
            for p in pieces:
                at = LEN * s + ROWS * p
                part[ph, s, p] = value[at : at + ROWS].astype(BF16)

    def spread(k, out):
        for s in range(2):
            for p in pieces:
                at = LEN * s + ROWS * p
                out[at : at + ROWS] = gbuf[k, s, p]

    def piece(p):
        return slice(ROWS * p, ROWS * (p + 1))

    def normed(x, gain):
        inv = lax.rsqrt(jnp.mean(x * x, axis=-1, keepdims=True) + 1e-06)
        return (x * inv * gain).astype(BF16)

    pairs = [(s, h) for s in range(2) for h in range(HEADS)]
    row = lax.broadcasted_iota(jnp.int32, (LEN, LEN), 0)
    col = lax.broadcasted_iota(jnp.int32, (LEN, LEN), 1)
    within = row >= col
    strict = row > col
    gain1 = g1[...].astype(F32)
    gain2 = g2[...].astype(F32)
    ogains = ogain[...].astype(F32)
    taps_q = cvq[...].astype(F32)
    taps_k = cvk[...].astype(F32)
    taps_v = cvv[...].astype(F32)

    def seq(s):
        return slice(LEN * s, LEN * (s + 1))

    def qc(h):
        return slice(PQ + DK * h, PQ + DK * (h + 1))

    def kc(h):
        return slice(PK + DK * h, PK + DK * (h + 1))

    def vc(h):
        return slice(PV + DV * h, PV + DV * (h + 1))

    def hv(h):
        return slice(DV * h, DV * (h + 1))

    @pl.when(section == 0)
    def _():
        for c in range(4):
            at = slice(ROWS * c, ROWS * (c + 1))
            a1[at] = normed(inp[at].astype(F32), gain1)
        for p in pieces:
            at = pl.multiple_of(core * LEN + ROWS * p, ROWS)
            xrow[piece(p)] = inp[pl.ds(at, ROWS)].astype(F32)

    def take_input(p, value):
        x = value.astype(F32)
        xrow[piece(p)] = x
        return normed(x, gain1)

    @pl.when(section == 1)
    def _():
        dyo[...] = cot[...]
        dact[...] = dot_nt(cot[...], wfd[...])
        hop_receive(0, 0, take_input)
        spread(0, a1)

    source = a1[...]
    proj[:, PQ:PK] = dot(source, wq[...])
    proj[:, PK:PV] = dot(source, wk[...])
    proj[:, PV:PG] = dot(source, wv[...])
    wba = jnp.concatenate(
        [wb[...].astype(F32), wd[...].astype(F32), jnp.zeros((4, 1024), F32)], axis=0
    ).astype(BF16)
    pba = dot_nt(source, wba)
    gpre[...] = dot(source, wgo[...])

    lane = lax.broadcasted_iota(jnp.int32, (LEN, LEN), 1)
    ltri = jnp.where(within, 1.0, 0.0)
    utri = jnp.where(row <= col, 1.0, 0.0)
    betas, decays, slopes = [], [], []
    for s, h in pairs:
        betas.append(sigmoid(pba[seq(s), h : h + 1]))
        pre = pba[seq(s), 2 + h : 3 + h] + sbias[0:1, h : h + 1]
        soft = jnp.maximum(pre, 0.0) + jnp.log1p(jnp.exp(-jnp.abs(pre)))
        rate = -jnp.exp(lrate[0:1, h : h + 1])
        decays.append(rate * soft)
        slopes.append(rate * sigmoid(pre))
    packed = jnp.zeros((LEN, LEN), F32)
    for i in range(4):
        packed = jnp.where(lane == i, decays[i], packed)
    cums = dot_full(ltri, packed)

    for s, h in pairs:
        z = conv_sum(proj[seq(s), qc(h)], taps_q[:, DK * h : DK * (h + 1)])
        zsum[seq(s), qc(h)] = z
        c = z * sigmoid(z)
        rq = lax.rsqrt(jnp.sum(c * c, axis=-1, keepdims=True) + 1e-06)
        qkv[seq(s), qc(h)] = c * (rq * SCALE)
        z = conv_sum(proj[seq(s), kc(h)], taps_k[:, DK * h : DK * (h + 1)])
        zsum[seq(s), kc(h)] = z
        c = z * sigmoid(z)
        rk = lax.rsqrt(jnp.sum(c * c, axis=-1, keepdims=True) + 1e-06)
        qkv[seq(s), kc(h)] = c * rk
        z = conv_sum(proj[seq(s), vc(h)], taps_v[:, hv(h)])
        zsum[seq(s), vc(h)] = z
        qkv[seq(s), vc(h)] = z * sigmoid(z)
        i = 2 * s + h
        cols[0, i] = jnp.broadcast_to(betas[i], (LEN, LEN))
        cols[1, i] = jnp.broadcast_to(decays[i], (LEN, LEN))
        cols[2, i] = jnp.broadcast_to(slopes[i], (LEN, LEN))
        cols[3, i] = jnp.broadcast_to(rq, (LEN, LEN))
        cols[4, i] = jnp.broadcast_to(rk, (LEN, LEN))

    systems = []
    for i, (s, h) in enumerate(pairs):
        cum = jnp.broadcast_to(cums[:, i : i + 1], (LEN, LEN))
        gaps = cum - cum.T
        decay = jnp.where(within, jnp.exp(jnp.where(within, gaps, 0.0)), 0.0)
        dmat[i] = decay
        kn = qkv[seq(s), kc(h)]
        e = jnp.where(strict, dot_nt(kn, kn) * decay, 0.0)
        emat[i] = e
        systems.append(cols[0, i] * e)
        amat[i] = dot_nt(qkv[seq(s), qc(h)], kn) * decay
    for i, inverse in enumerate(unit_inverses(systems)):
        tinv[i] = inverse.astype(BF16)
    for i, (s, h) in enumerate(pairs):
        w = qkv[seq(s), vc(h)] * cols[0, i][:, 0:1]
        umat[i] = dot(tinv[i], w).astype(BF16)
    for i, (s, h) in enumerate(pairs):
        o = dot(amat[i], umat[i])
        ro = lax.rsqrt(jnp.mean(o * o, axis=-1, keepdims=True) + 1e-05)
        cols[5, i] = jnp.broadcast_to(ro, (LEN, LEN))
        on = o * ro
        onorm[seq(s), hv(h)] = on
        gp = gpre[seq(s), hv(h)]
        mix[seq(s), hv(h)] = (on * ogains[:, hv(h)] * (gp * sigmoid(gp))).astype(BF16)

    put_part(0, dot(mix[...], wo[...]))

    def take_middle(p, total):
        h = xrow[piece(p)] + total
        hrow[piece(p)] = h
        return normed(h, gain2)

    all_sum(0, 1, take_middle)
    spread(1, a2)
    source = a2[...]
    upg[...] = dot_nt(source, wfg[...])
    upu[...] = dot_nt(source, wfu[...])

    outs = pair_sum(1)
    out_swaps = chip_swap(1)

    def output_part():
        ug = upg[...]
        s_act = (ug * sigmoid(ug) * upu[...]).astype(BF16)
        act[:, 704:FPAD] = jnp.zeros((2 * LEN, FPAD - 704), BF16)
        act[:, 0:704] = s_act
        put_part(1, dot(s_act, wfd[...]))
        started(outs)

    def output_sum():
        for p in pieces:
            outs[p].wait_recv()
            h = jnp.where(hi == 0, hrow[piece(p)], 0.0)
            fwd[1, p] = (pair_total(1, p) + h).astype(BF16)

    def take_cotangent(p, value):
        return value

    @pl.when(section == 0)
    def _():
        output_part()
        output_sum()
        hops = hop_send(1, 0)
        started(hops)
        sent(hops)
        started(out_swaps)
        hop_receive(1, 2, take_cotangent)
        spread(2, dyo)
        dact[...] = dot_nt(dyo[...], wfd[...])

    ds = dact[...]
    ug = upg[...]
    uu = upu[...]
    sg = sigmoid(ug)
    pad = jnp.zeros((2 * LEN, FPAD - 704), BF16)
    dgu[:, 704:FPAD] = pad
    dgu[:, FPAD + 704 :] = pad
    dgu[:, 0:704] = (ds * uu * (sg * (1.0 + ug * (1.0 - sg)))).astype(BF16)
    dgu[:, FPAD : FPAD + 704] = (ds * (ug * sg)).astype(BF16)
    put_part(2, dot(dgu[:, 0:704], wfg[...]) + dot(dgu[:, FPAD : FPAD + 704], wfu[...]))

    def take_gradient(p, total):
        dz, dgain = rms_back(hrow[piece(p)], gain2, total)
        at = pl.multiple_of(core * LEN + ROWS * p, ROWS)
        dh = dyo[pl.ds(at, ROWS)].astype(F32) + dz
        drow[piece(p)] = dh
        gains[0, p] = dgain
        return dh

    def second_output():
        pl.when(section == 1)(output_part)

    all_sum(2, 3, take_gradient, second_output)

    @pl.when(section == 1)
    def _():
        output_sum()
        started(out_swaps)

    spread(3, dho)
    dmix[...] = dot_nt(dho[...], wo[...])

    small[...] = jnp.zeros_like(small)
    douts = [jnp.zeros((1, DV), F32) for _ in range(HEADS)]
    dos = []
    for i, (s, h) in enumerate(pairs):
        dm = dmix[seq(s), hv(h)]
        gp = gpre[seq(s), hv(h)]
        sg = sigmoid(gp)
        on = onorm[seq(s), hv(h)]
        og = ogains[:, hv(h)]
        dgate = dm * on
        dpr[seq(s), PG + DV * h : PG + DV * (h + 1)] = (
            dgate * og * (sg * (1.0 + gp * (1.0 - sg)))
        ).astype(BF16)
        silu_g = gp * sg
        douts[h] = douts[h] + jnp.sum(dgate * silu_g, axis=0, keepdims=True)
        don = dm * silu_g * og
        ro = cols[5, i][:, 0:1]
        do = ro * (don - on * jnp.mean(don * on, axis=-1, keepdims=True))
        dos.append(do.astype(BF16))
    for h in range(HEADS):
        small[6:7, hv(h)] = douts[h]
    das = [dot_nt(dos[i], umat[i]) for i in range(4)]
    dus = [dot(amat[i].T, dos[i]) for i in range(4)]
    dws = [dot(tinv[i].astype(F32).T, dus[i]) for i in range(4)]
    dms = [jnp.where(strict, -dot_nt(dws[i], umat[i]), 0.0) for i in range(4)]
    dbetas, dcs, dqs, dks = [], [], [], []
    for i, (s, h) in enumerate(pairs):
        beta = cols[0, i]
        e = emat[i]
        decay = dmat[i]
        v = qkv[seq(s), vc(h)]
        de = dms[i] * e
        dbetas.append(
            jnp.sum(dws[i] * v, axis=-1, keepdims=True) + jnp.sum(de, axis=-1, keepdims=True)
        )
        dgap = das[i] * amat[i] + de * beta
        dcs.append(jnp.sum(dgap - dgap.T, axis=-1, keepdims=True))
        dqk = das[i] * decay
        dkk = dms[i] * beta * decay
        kn = qkv[seq(s), kc(h)]
        qn = qkv[seq(s), qc(h)]
        dqs.append(dot(dqk, kn))
        dks.append(dot(dqk.T, qn) + dot(dkk + dkk.T, kn))
    packed = jnp.zeros((LEN, LEN), F32)
    for i in range(4):
        packed = jnp.where(lane == i, dcs[i], packed)
    dgs = dot_full(utri, packed)

    dcq = [jnp.zeros((1, DK), F32) for _ in range(4 * HEADS)]
    dck = [jnp.zeros((1, DK), F32) for _ in range(4 * HEADS)]
    dcv = [jnp.zeros((1, DV), F32) for _ in range(4 * HEADS)]

    def conv_back(dz, at_rows, at_cols, taps, sums, h):
        pre = proj[at_rows, at_cols]
        total = dz * taps[3:4]
        for j in range(3):
            total = total + shift_up(dz, 3 - j) * taps[j : j + 1]
        for j in range(4):
            sums[4 * h + j] = sums[4 * h + j] + jnp.sum(
                dz * shift_down(pre, 3 - j), axis=0, keepdims=True
            )
        dpr[at_rows, at_cols] = total.astype(BF16)

    for i, (s, h) in enumerate(pairs):
        qn = qkv[seq(s), qc(h)]
        dq = dqs[i]
        dc = (cols[3, i] * SCALE) * (
            dq - qn * (jnp.sum(qn * dq, axis=-1, keepdims=True) * (1.0 / (SCALE * SCALE)))
        )
        dz = dc * silu_slope(zsum[seq(s), qc(h)])
        conv_back(dz, seq(s), qc(h), taps_q[:, DK * h : DK * (h + 1)], dcq, h)
        kn = qkv[seq(s), kc(h)]
        dk = dks[i]
        dc = cols[4, i] * (dk - kn * jnp.sum(kn * dk, axis=-1, keepdims=True))
        dz = dc * silu_slope(zsum[seq(s), kc(h)])
        conv_back(dz, seq(s), kc(h), taps_k[:, DK * h : DK * (h + 1)], dck, h)
        dv = dws[i] * cols[0, i][:, 0:1]
        dz = dv * silu_slope(zsum[seq(s), vc(h)])
        conv_back(dz, seq(s), vc(h), taps_v[:, hv(h)], dcv, h)
    for h in range(HEADS):
        for j in range(4):
            small[2 + j : 3 + j, DK * h : DK * (h + 1)] = dcq[4 * h + j]
            small[2 + j : 3 + j, 256 + DK * h : 256 + DK * (h + 1)] = dck[4 * h + j]
            small[2 + j : 3 + j, 512 + DV * h : 512 + DV * (h + 1)] = dcv[4 * h + j]
    lane_row = lax.broadcasted_iota(jnp.int32, (1, LEN), 1)
    scal = jnp.zeros((1, LEN), F32)
    for s in range(2):
        block = jnp.zeros((LEN, LEN), F32)
        for h in range(HEADS):
            i = 2 * s + h
            beta = cols[0, i]
            dg = jnp.broadcast_to(dgs[:, i : i + 1], (LEN, LEN))
            dpb = dbetas[i] * beta * (1.0 - beta)
            dpa = dg * cols[2, i]
            block = jnp.where(lane == h, dpb, block)
            block = jnp.where(lane == 2 + h, dpa, block)
            scal = scal + jnp.where(
                lane_row == h, jnp.sum(dg * cols[1, i], axis=0, keepdims=True), 0.0
            )
            scal = scal + jnp.where(lane_row == 2 + h, jnp.sum(dpa, axis=0, keepdims=True), 0.0)
        dpr[seq(s), PB:PEND] = block.astype(BF16)
    small[6:7, 512:640] = scal

    value = dot_nt(dpr[:, PQ:PK], wq[...])
    value = value + dot_nt(dpr[:, PK:PV], wk[...])
    value = value + dot_nt(dpr[:, PV:PG], wv[...])
    value = value + dot_nt(dpr[:, PG:PB], wgo[...])
    value = value + dot(dpr[:, PB:PEND][:, 0:8], wba)
    put_part(3, value)
    firsts, swaps = pair_sum(3), chip_swap(3)
    started(firsts)
    dgain1 = jnp.zeros((1, 1024), F32)
    for p in pieces:
        firsts[p].wait_recv()
        dz, dgain = rms_back(xrow[piece(p)], gain1, pair_total(3, p))
        dgain1 = dgain1 + dgain
        fwd[3, p] = (dz + jnp.where(hi == 0, drow[piece(p)], 0.0)).astype(BF16)

    @pl.when(section == 1)
    def _():
        hops = hop_send(3, 1)
        started(hops)
        sent(hops)

    started(swaps)
    dgain2 = jnp.where(hi == 0, gains[0, 0] + gains[0, 1], 0.0)
    gains[0, 0] = dgain1
    gains[0, 1] = dgain2
    sums = [
        remote(
            gains.at[0], gains.at[step], ga_s.at[step - 1], ga_r.at[step - 1],
            {"tensor": (t + step) % 4},
        )
        for step in range(1, 4)
    ]
    started(sums)
    hidden, back = pair_share(4), pair_share(5)
    for p in pieces:
        out_swaps[p].wait_recv()
        gbuf[4, core, p] = chip_total(1, p).astype(BF16)
        hidden[p].start()
    for p in pieces:
        swaps[p].wait_recv()
        gbuf[5, core, p] = chip_total(3, p).astype(BF16)
        back[p].start()
    received(sums)
    small[0:1] = (gains[0, 0] + gains[2, 0]) + (gains[1, 0] + gains[3, 0])
    small[1:2] = (gains[0, 1] + gains[2, 1]) + (gains[1, 1] + gains[3, 1])
    received(hidden)
    spread(4, hid)
    received(back)
    spread(5, ing)
    sent(outs + out_swaps + firsts + swaps + sums + hidden + back)


def run_layer(args):
    tokens = 2 * LEN
    results = (
        ((tokens, 1024), BF16), ((tokens, 1024), BF16), ((tokens, 1024), BF16),
        ((tokens, PEND), BF16), ((tokens, 1024), BF16), ((tokens, 2 * FPAD), BF16),
        ((tokens, 1024), BF16), ((tokens, 512), BF16), ((tokens, 1024), BF16),
        ((tokens, FPAD), BF16), ((8, 1024), F32),
    )
    rows = (2, ROWS, 1024)
    buffers = [
        pltpu.VMEM((4, 2) + rows, BF16),
        pltpu.VMEM((4,) + rows, BF16),
        pltpu.VMEM((4,) + rows, BF16),
        pltpu.VMEM((4,) + rows, BF16),
        pltpu.VMEM((2, 2) + rows, BF16),
        pltpu.VMEM((6, 2) + rows, BF16),
        pltpu.VMEM((LEN, 1024), F32),
        pltpu.VMEM((LEN, 1024), F32),
        pltpu.VMEM((LEN, 1024), F32),
        pltpu.VMEM((tokens, 1024), F32),
        pltpu.VMEM((tokens, 1024), F32),
        pltpu.VMEM((tokens, 1024), F32),
        pltpu.VMEM((tokens, 512), F32),
        pltpu.VMEM((tokens, 512), F32),
        pltpu.VMEM((tokens, 512), F32),
        pltpu.VMEM((tokens, 704), F32),
        pltpu.VMEM((tokens, 704), F32),
        pltpu.VMEM((tokens, 704), F32),
        pltpu.VMEM((4, LEN, LEN), BF16),
        pltpu.VMEM((4, LEN, LEN), F32),
        pltpu.VMEM((4, LEN, LEN), F32),
        pltpu.VMEM((4, LEN, LEN), F32),
        pltpu.VMEM((4, LEN, DV), BF16),
        pltpu.VMEM((6, 4, LEN, LEN), F32),
        pltpu.VMEM((4, 2, 1, 1024), F32),
    ]
    sems = [
        pltpu.SemaphoreType.DMA((4, 2)), pltpu.SemaphoreType.DMA((4, 2)),
        pltpu.SemaphoreType.DMA((4, 2)), pltpu.SemaphoreType.DMA((4, 2)),
        pltpu.SemaphoreType.DMA((6, 2)), pltpu.SemaphoreType.DMA((6, 2)),
        pltpu.SemaphoreType.DMA((2, 2, 2)), pltpu.SemaphoreType.DMA((2, 2, 2)),
        pltpu.SemaphoreType.DMA((3,)), pltpu.SemaphoreType.DMA((3,)),
    ]
    return pl.pallas_call(
        layer_kernel,
        out_shape=[jax.ShapeDtypeStruct(s, d) for s, d in results],
        in_specs=[pl.BlockSpec(memory_space=pltpu.VMEM)] * len(args),
        out_specs=[pl.BlockSpec(memory_space=pltpu.VMEM)] * len(results),
        scratch_shapes=buffers + sems,
        compiler_params=pltpu.CompilerParams(
            collective_id=0, has_side_effects=True, vmem_limit_bytes=58 * 1024 * 1024
        ),
        name="layer",
    )(*args)


def grad_kernel(
    a1, dpr, a2, dgu, dho, mix, dyo, act, small,
    gq, gk, gv, gb, gd, ggo, gout, gfg, gfu, gfd, gsmall,
    ga, gz, a1p, a1m, a2p, a2m, b1p, b1m, b2p, b2m,
    ha, hb, c1p, c1m, c2p, c2m, d1p, d1m, d2p, d2m,
    sx, sz, a1t, a2t, dht, dyt, send, recv, ssend, srecv,
):
    place = lax.axis_index("dp")
    z = place // 4
    x = place % 4

    def at_x(step):
        return {"dp": z * 4 + (x + step) % 4}

    def at_z(step):
        return {"dp": ((z + step) % 4) * 4 + x}

    def remote(src, dst, ssem, rsem, device):
        return pltpu.make_async_remote_copy(
            src_ref=src, dst_ref=dst, send_sem=ssem, recv_sem=rsem,
            device_id=device, device_id_type=MESH,
        )

    barrier = pltpu.get_barrier_semaphore()
    for step in range(1, 4):
        pl.semaphore_signal(barrier, inc=1, device_id=at_x(step), device_id_type=MESH)
        pl.semaphore_signal(barrier, inc=1, device_id=at_z(step), device_id_type=MESH)

    def turned(source, out):
        for rows in range(4):
            flat = source[:, 256 * rows : 256 * (rows + 1)].T
            for c in range(4):
                out[rows, c] = flat[ROWS * c : ROWS * (c + 1)]

    def outer(left, right, width, out, offset):
        for start in range(0, width, 256):
            size = min(256, width - start)
            value = jnp.dot(
                left, right[:, start : start + size], preferred_element_type=F32
            ).astype(BF16)
            for c in range(4):
                out[c, :, offset + start : offset + start + size] = value[
                    ROWS * c : ROWS * (c + 1)
                ]

    def chunk_a(c):
        outer(a1t[:, c].reshape(256, 256), dpr, PEND, ga.at[c], 0)
        outer(dht[:, c].reshape(256, 256), mix, 512, ga.at[c], PEND)

    def chunk_b(c):
        outer(a2t[c].reshape(256, 256), dgu, 2 * FPAD, gz.at[c], 0)
        outer(dyt[c].reshape(256, 256), act, FPAD, gz.at[c], 2 * FPAD)

    turned(a1, a1t)
    turned(dho, dht)
    turned(a2, a2t)
    turned(dyo, dyt)
    pl.semaphore_wait(barrier, 6)

    class Ring:
        def __init__(self, g, me, where, bufs, k, half):
            one_p, one_m, two_p, two_m = bufs
            self.g, self.me, self.bufs, self.half = g, me, bufs, half
            self.right = right = (me + 1) % 4
            self.left = left = (me + 3) % 4
            far = (me + 2) % 4
            lo, up = pl.ds(0, half), pl.ds(half, half)
            self.lo, self.up = lo, up
            self.p1 = remote(g.at[far, lo], one_p, send.at[k, 0], recv.at[k, 0], where(1))
            self.m1 = remote(g.at[far, up], one_m, send.at[k, 1], recv.at[k, 1], where(3))
            self.p2 = remote(g.at[right, up], two_p.at[up], send.at[k, 2], recv.at[k, 2], where(1))
            self.m2 = remote(g.at[left, lo], two_m.at[lo], send.at[k, 3], recv.at[k, 3], where(3))
            self.p3 = remote(g.at[right, lo], two_p.at[lo], send.at[k, 4], recv.at[k, 4], where(1))
            self.m3 = remote(g.at[left, up], two_m.at[up], send.at[k, 5], recv.at[k, 5], where(3))

        def start(self, chunk=None):
            for at, copies in (
                ((self.me + 2) % 4, (self.p1, self.m1)),
                (self.right, (self.p2,)),
                (self.left, (self.m2,)),
            ):
                if chunk is not None:
                    chunk(at)
                for copy in copies:
                    copy.start()
            if chunk is not None:
                chunk(self.me)

        def relay(self):
            one_p, one_m, two_p, two_m = self.bufs
            g, lo, up = self.g, self.lo, self.up
            self.p1.wait_recv()
            add_into(g.at[self.right, lo], one_p)
            self.p3.start()
            self.m1.wait_recv()
            add_into(g.at[self.left, up], one_m)
            self.m3.start()

        def arrive(self):
            for copy in (self.p2, self.m2, self.p3, self.m3):
                copy.wait_recv()

        def sent(self):
            for copy in (self.p1, self.m1, self.p2, self.m2, self.p3, self.m3):
                copy.wait_send()

    def add_into(ref, other):
        if len(other.shape) == 3:
            @pl.loop(0, other.shape[0])
            def _(c):
                ref[c] = (ref[c].astype(F32) + other[c].astype(F32)).astype(BF16)
        else:
            ref[...] = (ref[...].astype(F32) + other[...].astype(F32)).astype(BF16)

    sx[0] = small[...]
    small_x = [
        remote(sx.at[0], sx.at[step], ssend.at[step - 1], srecv.at[step - 1], at_x(step))
        for step in range(1, 4)
    ]
    small_z = [
        remote(sz.at[0], sz.at[step], ssend.at[step + 2], srecv.at[step + 2], at_z(step))
        for step in range(1, 4)
    ]
    first_a = Ring(ga, x, at_x, (a1p, a1m, a2p, a2m), 0, 2)
    first_b = Ring(gz, z, at_z, (b1p, b1m, b2p, b2m), 1, 2)
    second_a = Ring(ha, z, at_z, (c1p, c1m, c2p, c2m), 2, 32)
    second_b = Ring(hb, x, at_x, (d1p, d1m, d2p, d2m), 3, 32)
    first_a.start(chunk_a)
    first_b.start(chunk_b)
    for copy in small_x:
        copy.start()
    first_a.relay()
    first_b.relay()
    for copy in small_x:
        copy.wait_recv()
    sz[0] = (sx[0] + sx[2]) + (sx[1] + sx[3])
    for copy in small_z:
        copy.start()

    def merge(ring, out):
        _, _, two_p, two_m = ring.bufs

        @pl.loop(0, 4)
        def _(c):
            out[c] = (
                ring.g[ring.me, c].astype(F32) + two_p[c].astype(F32) + two_m[c].astype(F32)
            ).astype(BF16)

    first_a.arrive()
    merge(first_a, ha)
    second_a.start()
    first_b.arrive()
    merge(first_b, hb)
    second_b.start()
    second_a.relay()
    second_b.relay()
    for copy in small_z:
        copy.wait_recv()
    sums = (sz[0] + sz[2]) + (sz[1] + sz[3])
    gsmall[...] = sums

    def total(ring, start, size):
        _, _, two_p, two_m = ring.bufs
        at = slice(start, start + size)
        return (
            ring.g[ring.me, :, at].astype(F32)
            + two_p[:, at].astype(F32)
            + two_m[:, at].astype(F32)
        )

    second_a.arrive()
    gq[...] = total(second_a, PQ, 256)
    gk[...] = total(second_a, PK, 256)
    gv[...] = total(second_a, PV, 512)
    ggo[...] = total(second_a, PG, 512)
    pair = total(second_a, PB, 128).T
    gb[...] = pair[0:2]
    gd[...] = pair[2:4]
    gout[...] = total(second_a, PEND, 512)
    second_b.arrive()
    gfg[...] = total(second_b, 0, FPAD)[:, 0:704]
    gfu[...] = total(second_b, FPAD, FPAD)[:, 0:704]
    gfd[...] = total(second_b, 2 * FPAD, FPAD)[:, 0:704]
    for ring in (first_a, first_b, second_a, second_b):
        ring.sent()
    for copy in small_x + small_z:
        copy.wait_send()


def run_grads(args):
    results = (
        (ROWS, 256), (ROWS, 256), (ROWS, 512), (2, ROWS), (2, ROWS), (ROWS, 512),
        (ROWS, 512), (ROWS, 704), (ROWS, 704), (ROWS, 704), (8, 1024),
    )

    def first(n):
        return [pltpu.VMEM((2, ROWS, n), BF16)] * 2 + [pltpu.VMEM((4, ROWS, n), BF16)] * 2

    def second(n):
        return [pltpu.VMEM((ROWS // 2, n), BF16)] * 2 + [pltpu.VMEM((ROWS, n), BF16)] * 2

    buffers = (
        [pltpu.VMEM((4, 4, ROWS, NA), BF16), pltpu.VMEM((4, 4, ROWS, NB), BF16)]
        + first(NA)
        + first(NB)
        + [pltpu.VMEM((4, ROWS, NA), BF16), pltpu.VMEM((4, ROWS, NB), BF16)]
        + second(NA)
        + second(NB)
        + [pltpu.VMEM((4, 8, 1024), F32)] * 2
        + [pltpu.VMEM((4, 4, ROWS, 256), BF16)] * 4
    )
    sems = [
        pltpu.SemaphoreType.DMA((4, 6)), pltpu.SemaphoreType.DMA((4, 6)),
        pltpu.SemaphoreType.DMA((6,)), pltpu.SemaphoreType.DMA((6,)),
    ]
    return pl.pallas_call(
        grad_kernel,
        out_shape=[jax.ShapeDtypeStruct(s, F32) for s in results],
        in_specs=[pl.BlockSpec(memory_space=pltpu.VMEM)] * len(args),
        out_specs=[pl.BlockSpec(memory_space=pltpu.VMEM)] * len(results),
        scratch_shapes=buffers + sems,
        compiler_params=pltpu.CompilerParams(
            collective_id=1, has_side_effects=True, vmem_limit_bytes=58 * 1024 * 1024
        ),
        name="grads",
    )(*args)


def result_kernel(*refs):
    hid, ing, gq, gk, gv, gb, gd, ggo, gout, gfg, gfu, gfd, sums = refs[:13]
    outs = refs[13:]
    dg1, dcq, dck, dcv, dlr, dsb, dog, dg2 = outs[12:]
    for source, out in zip((hid, ing, gq, gk, gv, gb, gd, ggo, gout, gfg, gfu, gfd), outs):
        out[...] = source[...]
    dg1[...] = sums[0:1]
    dg2[...] = sums[1:2]
    dcq[...] = sums[2:6, 0:256]
    dck[...] = sums[2:6, 256:512]
    dcv[...] = sums[2:6, 512:1024]
    dog[...] = sums[6:7, 0:512]
    dlr[...] = sums[6:7, 512:514]
    dsb[...] = sums[6:7, 514:516]


def run_results(args):
    results = [(v.shape, v.dtype) for v in args[:12]] + [
        (shape, F32)
        for shape in (
            (1, 1024), (4, 256), (4, 256), (4, 512), (1, 2), (1, 2), (1, 512), (1, 1024)
        )
    ]
    return pl.pallas_call(
        result_kernel,
        out_shape=[jax.ShapeDtypeStruct(s, d) for s, d in results],
        in_specs=[pl.BlockSpec(memory_space=pltpu.VMEM)] * len(args),
        out_specs=[pl.BlockSpec(memory_space=pltpu.VMEM)] * len(results),
        compiler_params=pltpu.CompilerParams(vmem_limit_bytes=32 * 1024 * 1024),
        name="results",
    )(*args)


def per_device(
    inputs, cotangent, norm_gain1, w_query, w_key, w_value, conv_query, conv_key, conv_value,
    w_beta, w_decay, log_rate, step_bias, out_gain, w_gate_out, w_out, norm_gain2,
    w_ffn_gate, w_ffn_up, w_ffn_down,
):
    tokens = 2 * LEN
    width = inputs.shape[-1]
    out = run_layer((
        inputs.reshape(tokens, width), cotangent.reshape(tokens, width),
        norm_gain1, w_query[0], w_key[0], w_value[0],
        conv_query[0], conv_key[0], conv_value[0], w_beta[0].T, w_decay[0].T,
        log_rate, step_bias, out_gain, w_gate_out[0], w_out[0], norm_gain2,
        w_ffn_gate[0].T, w_ffn_up[0].T, w_ffn_down[0],
    ))
    grads = run_grads(tuple(out[2:]))
    (
        hidden, input_grad, gq, gk, gv, gb, gd, ggo, gout, gfg, gfu, gfd,
        dg1, dcq, dck, dcv, dlr, dsb, dog, dg2,
    ) = run_results(tuple(out[:2]) + tuple(grads))
    shape = (1,) + inputs.shape
    return (
        hidden.reshape(shape), input_grad.reshape(shape), dg1, gq[None], gk[None], gv[None],
        dcq[None], dck[None], dcv[None], gb.T[None], gd.T[None], dlr, dsb, dog,
        ggo[None], gout.T[None], dg2, gfg[None], gfu[None], gfd.T[None],
    )


def solution(mesh):
    three = P("section", None, "tensor")
    in_specs = (
        P(None, "dp", None, None), P(None, "dp", None, None), P("section", None),
        three, three, three, three, three, three, three, three,
        P("section", "tensor"), P("section", "tensor"), P("section", "tensor"),
        three, P("section", "tensor", None), P("section", None),
        three, three, P("section", "tensor", None),
    )
    spread = P("section", "dp", "tensor")
    out_specs = (
        P("section", None, "dp", None, None), P("section", None, "dp", None, None),
        P("section", None), spread, spread, spread, three, three, three, spread, spread,
        P("section", "tensor"), P("section", "tensor"), P("section", "tensor"),
        spread, P("section", "tensor", "dp"), P("section", None),
        spread, spread, P("section", "tensor", "dp"),
    )
    return jax.shard_map(
        per_device, mesh=mesh, in_specs=in_specs, out_specs=out_specs, check_vma=False
    )
```

```python
import jax
import jax.numpy as jnp
from jax import lax
from jax.experimental import pallas as pl
from jax.experimental.pallas import tpu as pltpu
from jax.sharding import PartitionSpec as P

F32 = jnp.float32
BF16 = jnp.bfloat16
MESH = pl.DeviceIdType.MESH
LEN = 128
ROWS = 64
HEADS = 2
DK = 128
DV = 256
SCALE = DK**-0.5
PQ, PK, PV, PG, PB, PEND = 0, 256, 512, 1024, 1536, 1664
FPAD = 768
NF = FPAD + FPAD // 2
NQ = PV + (PEND - PB) + 512
NV = PB - PV


def dot(left, right):
    return jnp.dot(left.astype(BF16), right.astype(BF16), preferred_element_type=F32)


def dot_nt(left, right):
    return lax.dot_general(
        left.astype(BF16),
        right.astype(BF16),
        (((1,), (1,)), ((), ())),
        preferred_element_type=F32,
    )


def dot_full(left, right):
    return jnp.dot(left, right, precision=lax.Precision.HIGHEST, preferred_element_type=F32)


def sigmoid(v):
    return 1.0 / (1.0 + jnp.exp(-v))


def rows_of(shape):
    return lax.broadcasted_iota(jnp.int32, shape, 0)


def shift_down(v, steps):
    if steps == 0:
        return v
    return jnp.where(rows_of(v.shape) >= steps, pltpu.roll(v, steps, 0), 0.0)


def shift_up(v, steps):
    if steps == 0:
        return v
    count = v.shape[0]
    return jnp.where(rows_of(v.shape) < count - steps, pltpu.roll(v, count - steps, 0), 0.0)


def conv_sum(v, taps):
    total = v * taps[3:4]
    for j in range(3):
        total = total + shift_down(v, 3 - j) * taps[j : j + 1]
    return total


def silu_slope(z):
    s = sigmoid(z)
    return s * (1.0 + z * (1.0 - s))


def unit_inverses(systems):
    row = lax.broadcasted_iota(jnp.int32, (LEN, LEN), 0)
    col = lax.broadcasted_iota(jnp.int32, (LEN, LEN), 1)
    eye = jnp.where(row == col, 1.0, 0.0)

    def band(level):
        same = (row >> (level + 1)) == (col >> (level + 1))
        return same & (((row >> level) & 1) == 1) & (((col >> level) & 1) == 0)

    first = band(0)
    inverses = [eye - jnp.where(first, m, 0.0) for m in systems]
    for level in range(1, 7):
        at = band(level)
        halves = [dot(t, jnp.where(at, m, 0.0)) for t, m in zip(inverses, systems)]
        inverses = [t - dot(x, t) for t, x in zip(inverses, halves)]
    return inverses


def rms_back(z, gain, dn):
    inv = lax.rsqrt(jnp.mean(z * z, axis=-1, keepdims=True) + 1e-06)
    hat = z * inv
    weighted = dn * gain
    dz = (weighted - hat * jnp.mean(weighted * hat, axis=-1, keepdims=True)) * inv
    return dz, jnp.sum(dn * hat, axis=0, keepdims=True)


def torus_steps(place):
    z = place // 4
    x = place % 4
    along_x = [{"dp": z * 4 + (x + step) % 4} for step in range(1, 4)]
    along_z = [{"dp": ((z + step) % 4) * 4 + x} for step in range(1, 4)]
    return along_x + along_z


def turned(source, out):
    for rows in range(4):
        flat = source[:, 256 * rows : 256 * (rows + 1)].T
        for c in range(4):
            out[rows, c] = flat[ROWS * c : ROWS * (c + 1)]


def add_into(ref, more):
    if len(more.shape) == 3:
        @pl.loop(0, more.shape[0])
        def _(c):
            ref[c] = (ref[c].astype(F32) + more[c].astype(F32)).astype(BF16)
    else:
        ref[...] = (ref[...].astype(F32) + more[...].astype(F32)).astype(BF16)


class Ring:
    def __init__(self, remote, g, me, devices, bufs, send, recv, half):
        one_p, one_m, two_p, two_m = bufs
        after, _, before = devices
        self.g, self.me, self.bufs = g, me, bufs
        self.right = right = (me + 1) % 4
        self.left = left = (me + 3) % 4
        self.far = far = (me + 2) % 4
        lo, up = pl.ds(0, half), pl.ds(half, half)
        self.lo, self.up = lo, up
        self.p1 = remote(g.at[far, lo], one_p, send.at[0], recv.at[0], after)
        self.m1 = remote(g.at[far, up], one_m, send.at[1], recv.at[1], before)
        self.p2 = remote(g.at[right, up], two_p.at[up], send.at[2], recv.at[2], after)
        self.m2 = remote(g.at[left, lo], two_m.at[lo], send.at[3], recv.at[3], before)
        self.p3 = remote(g.at[right, lo], two_p.at[lo], send.at[4], recv.at[4], after)
        self.m3 = remote(g.at[left, up], two_m.at[up], send.at[5], recv.at[5], before)
        self.steps = ((far, (self.p1, self.m1)), (right, (self.p2,)), (left, (self.m2,)))

    def start(self):
        for _, copies in self.steps:
            for copy in copies:
                copy.start()

    def relay(self):
        one_p, one_m, _, _ = self.bufs
        self.p1.wait_recv()
        add_into(self.g.at[self.right, self.lo], one_p)
        self.p3.start()
        self.m1.wait_recv()
        add_into(self.g.at[self.left, self.up], one_m)
        self.m3.start()

    def arrive(self):
        for copy in (self.p2, self.m2, self.p3, self.m3):
            copy.wait_recv()

    def sent(self):
        for copy in (self.p1, self.m1, self.p2, self.m2, self.p3, self.m3):
            copy.wait_send()

    def merge(self, out):
        _, _, two_p, two_m = self.bufs

        @pl.loop(0, 4)
        def _(c):
            out[c] = (
                self.g[self.me, c].astype(F32) + two_p[c].astype(F32) + two_m[c].astype(F32)
            ).astype(BF16)

    def total(self, start, size):
        _, _, two_p, two_m = self.bufs
        at = slice(start, start + size)
        return (
            self.g[self.me, :, at].astype(F32)
            + two_p[:, at].astype(F32)
            + two_m[:, at].astype(F32)
        )


WIDTHS = (NF, NF, NQ, NV)


def sum_scratch():
    scratch = []
    for n in WIDTHS:
        scratch.append(pltpu.VMEM((4, 4, ROWS, n), BF16))
        scratch += [pltpu.VMEM((2, ROWS, n), BF16)] * 2 + [pltpu.VMEM((4, ROWS, n), BF16)] * 3
        scratch += [pltpu.VMEM((ROWS // 2, n), BF16)] * 2 + [pltpu.VMEM((ROWS, n), BF16)] * 2
    scratch += [pltpu.VMEM((4, 8, 1024), F32)] * 2
    scratch += [pltpu.SemaphoreType.DMA((8, 6))] * 2 + [pltpu.SemaphoreType.DMA((6,))] * 2
    return scratch


class Sums:
    def __init__(self, place, remote, data, outs, refs):
        self.data, self.outs = data, outs
        z, x = place // 4, place % 4
        steps = torus_steps(place)
        ways = ((x, steps[:3]), (z, steps[3:]))
        self.sx, self.sz, send, recv, ssend, srecv = refs[-6:]
        self.first, self.second, self.half = [], [], []
        for k in range(4):
            g, one_p, one_m, two_p, two_m, h, a, b, c, d = refs[10 * k : 10 * k + 10]
            me, way = ways[k % 2]
            self.first.append(
                Ring(remote, g, me, way, (one_p, one_m, two_p, two_m), send.at[k], recv.at[k], 2)
            )
            me, way = ways[1 - k % 2]
            self.second.append(
                Ring(remote, h, me, way, (a, b, c, d), send.at[4 + k], recv.at[4 + k], ROWS // 2)
            )
        self.small_x = [
            remote(self.sx.at[0], self.sx.at[i + 1], ssend.at[i], srecv.at[i], steps[i])
            for i in range(3)
        ]
        self.small_z = [
            remote(self.sz.at[0], self.sz.at[i + 1], ssend.at[3 + i], srecv.at[3 + i], steps[3 + i])
            for i in range(3)
        ]

    def chunk(self, k, c):
        data = self.data
        out = self.first[k].g.at[c]

        def outer(left, right, first, width, offset):
            rows = left[:, c] if k % 2 == 0 else left[c]
            flat = rows.reshape(4 * ROWS, 2 * LEN)
            for start in range(0, width, 256):
                size = min(256, width - start)
                value = jnp.dot(
                    flat, right[:, first + start : first + start + size],
                    preferred_element_type=F32,
                ).astype(BF16)
                for i in range(4):
                    out[i, :, offset + start : offset + start + size] = value[
                        ROWS * i : ROWS * (i + 1)
                    ]

        if k < 2:
            outer(data["a2"], data["pair"], FPAD * k, FPAD, 0)
            outer(data["dy"], data["act"], FPAD // 2 * k, FPAD // 2, FPAD)
        elif k == 2:
            outer(data["a1"], data["proj"], PQ, PV, 0)
            outer(data["a1"], data["proj"], PB, PEND - PB, PV)
            outer(data["dh"], data["mix"], 0, 512, PV + PEND - PB)
        else:
            outer(data["a1"], data["proj"], PV, PB - PV, 0)

    def begin(self, groups):
        for step in range(3):
            for k in groups:
                at, copies = self.first[k].steps[step]
                self.chunk(k, at)
                for copy in copies:
                    copy.start()
        for k in groups:
            self.chunk(k, self.first[k].me)

    def merge(self, groups):
        for k in groups:
            self.first[k].arrive()
            self.first[k].merge(self.second[k].g)
            self.second[k].start()

    def ffn_start(self):
        self.begin((0, 1))

    def ffn_relay(self):
        self.first[0].relay()
        self.first[1].relay()

    def ffn_merge(self):
        self.merge((0, 1))

    def ffn_relay_second(self):
        self.second[0].relay()
        self.second[1].relay()

    def ffn_finish(self):
        one, two, outs = self.second[0], self.second[1], self.outs
        one.arrive()
        outs["fg"][...] = one.total(0, FPAD)[:, 0:704]
        outs["fd"][:, 0:384] = one.total(FPAD, 384)
        two.arrive()
        outs["fu"][...] = two.total(0, FPAD)[:, 0:704]
        outs["fd"][:, 384:704] = two.total(FPAD, 384)[:, 0:320]

    def mix_start(self):
        self.begin((2, 3))

    def mix_relay(self):
        self.first[2].relay()
        self.first[3].relay()

    def mix_merge(self):
        self.merge((2, 3))

    def mix_relay_second(self):
        self.second[2].relay()
        self.second[3].relay()

    def mix_finish(self):
        one, two, outs = self.second[2], self.second[3], self.outs
        one.arrive()
        outs["q"][...] = one.total(0, 256)
        outs["k"][...] = one.total(256, 256)
        both = one.total(PV, PEND - PB).T
        outs["b"][...] = both[0:2]
        outs["d"][...] = both[2:4]
        outs["out"][...] = one.total(PV + PEND - PB, 512)
        two.arrive()
        outs["v"][...] = two.total(0, 512)
        outs["go"][...] = two.total(512, 512)

    def small_start(self, small):
        self.sx[0] = small[...]
        for copy in self.small_x:
            copy.start()

    def small_relay(self):
        sx = self.sx
        for copy in self.small_x:
            copy.wait_recv()
        self.sz[0] = (sx[0] + sx[2]) + (sx[1] + sx[3])
        for copy in self.small_z:
            copy.start()

    def small_finish(self):
        sz = self.sz
        for copy in self.small_z:
            copy.wait_recv()
        self.outs["small"][...] = (sz[0] + sz[2]) + (sz[1] + sz[3])

    def sent(self):
        for ring in self.first + self.second:
            ring.sent()
        for copy in self.small_x + self.small_z:
            copy.wait_send()


def layer_kernel(
    inp, cot, g1, wq, wk, wv, cvq, cvk, cvv, wb, wd, lrate, sbias, ogain, wgo, wo, g2, wfg, wfu, wfd,
    hid, ing, gq, gk, gv, gb, gd, ggo, gout, gfg, gfu, gfd, gsmall,
    a1, dpr, a2, dgu, dho, mix, dyo, act, small, a1t, a2t, dht, dyt,
    part, r1, r2, fwd, hopb, gbuf, xrow, hrow, drow,
    proj, zsum, qkv, gpre, onorm, upg, upu, dact,
    tinv, amat, dmat, emat, umat, cols, gains, dg2s,
    rs_s, rs_r, op_s, op_r, ag_s, ag_r, hop_s, hop_r, ga_s, ga_r,
    *sum_refs,
):
    section = lax.axis_index("section")
    t = lax.axis_index("tensor")
    hi = t // 2
    core = t % 2
    sib = hi * 2 + (1 - core)
    opp = (1 - hi) * 2 + core
    other = 1 - section
    pieces = range(2)

    def remote(src, dst, ssem, rsem, device):
        return pltpu.make_async_remote_copy(
            src_ref=src, dst_ref=dst, send_sem=ssem, recv_sem=rsem,
            device_id=device, device_id_type=MESH,
        )

    barrier = pltpu.get_barrier_semaphore()
    for step in range(1, 4):
        pl.semaphore_signal(
            barrier, inc=1, device_id={"tensor": (t + step) % 4}, device_id_type=MESH
        )
    for step in range(4):
        pl.semaphore_signal(
            barrier, inc=1, device_id={"section": other, "tensor": (t + step) % 4},
            device_id_type=MESH,
        )
    place = lax.axis_index("dp")
    links = torus_steps(place)
    for device in links:
        pl.semaphore_signal(barrier, inc=1, device_id=device, device_id_type=MESH)
    pl.semaphore_wait(barrier, 7 + len(links))

    grads = Sums(
        place, remote,
        dict(a1=a1t, a2=a2t, dh=dht, dy=dyt, proj=dpr, pair=dgu, mix=mix, act=act),
        dict(q=gq, k=gk, v=gv, b=gb, d=gd, go=ggo, out=gout, fg=gfg, fu=gfu, fd=gfd, small=gsmall),
        sum_refs,
    )

    def pair_sum(ph):
        return [
            remote(part.at[ph, 1 - core, p], r1.at[ph, p], rs_s.at[ph, p], rs_r.at[ph, p],
                   {"tensor": sib})
            for p in pieces
        ]

    def chip_swap(ph):
        return [
            remote(fwd.at[ph, p], r2.at[ph, p], op_s.at[ph, p], op_r.at[ph, p], {"tensor": opp})
            for p in pieces
        ]

    def pair_share(k):
        return [
            remote(gbuf.at[k, core, p], gbuf.at[k, core, p], ag_s.at[k, p], ag_r.at[k, p],
                   {"tensor": sib})
            for p in pieces
        ]

    def started(copies):
        for copy in copies:
            copy.start()

    def received(copies):
        for copy in copies:
            copy.wait_recv()

    def sent(copies):
        for copy in copies:
            copy.wait_send()

    def pair_total(ph, p):
        return part[ph, core, p].astype(F32) + r1[ph, p].astype(F32)

    def chip_total(ph, p):
        return fwd[ph, p].astype(F32) + r2[ph, p].astype(F32)

    def all_sum(ph, k, finish, between=None):
        firsts, swaps, shares = pair_sum(ph), chip_swap(ph), pair_share(k)
        started(firsts)
        for p in pieces:
            firsts[p].wait_recv()
            fwd[ph, p] = pair_total(ph, p).astype(BF16)
            swaps[p].start()
        if between is not None:
            between()
        for p in pieces:
            swaps[p].wait_recv()
            gbuf[k, core, p] = finish(p, chip_total(ph, p)).astype(BF16)
            shares[p].start()
        received(shares)
        sent(firsts + swaps + shares)

    def hop_send(ph, k):
        return [
            remote(fwd.at[ph, p], hopb.at[k, hi, p], hop_s.at[k, y, p], hop_r.at[k, hi, p],
                   {"section": other, "tensor": 2 * y + core})
            for p in pieces
            for y in range(2)
        ]

    def hop_receive(k, share, finish):
        shares = pair_share(share)
        for p in pieces:
            for y in range(2):
                remote(hopb.at[k, y, p], hopb.at[k, y, p], hop_s.at[k, y, p], hop_r.at[k, y, p],
                       {"section": other, "tensor": t}).wait_recv()
            value = (hopb[k, 0, p].astype(F32) + hopb[k, 1, p].astype(F32)).astype(BF16)
            gbuf[share, core, p] = finish(p, value)
            shares[p].start()
        received(shares)
        sent(shares)

    def put_part(ph, value):
        for s in range(2):
            for p in pieces:
                at = LEN * s + ROWS * p
                part[ph, s, p] = value[at : at + ROWS].astype(BF16)

    def spread(k, out):
        for s in range(2):
            for p in pieces:
                at = LEN * s + ROWS * p
                out[at : at + ROWS] = gbuf[k, s, p]

    def piece(p):
        return slice(ROWS * p, ROWS * (p + 1))

    def normed(x, gain):
        inv = lax.rsqrt(jnp.mean(x * x, axis=-1, keepdims=True) + 1e-06)
        return (x * inv * gain).astype(BF16)

    pairs = [(s, h) for s in range(2) for h in range(HEADS)]
    row = lax.broadcasted_iota(jnp.int32, (LEN, LEN), 0)
    col = lax.broadcasted_iota(jnp.int32, (LEN, LEN), 1)
    within = row >= col
    strict = row > col
    gain1 = g1[...].astype(F32)
    gain2 = g2[...].astype(F32)
    ogains = ogain[...].astype(F32)
    taps_q = cvq[...].astype(F32)
    taps_k = cvk[...].astype(F32)
    taps_v = cvv[...].astype(F32)

    def seq(s):
        return slice(LEN * s, LEN * (s + 1))

    def qc(h):
        return slice(PQ + DK * h, PQ + DK * (h + 1))

    def kc(h):
        return slice(PK + DK * h, PK + DK * (h + 1))

    def vc(h):
        return slice(PV + DV * h, PV + DV * (h + 1))

    def hv(h):
        return slice(DV * h, DV * (h + 1))

    @pl.when(section == 0)
    def _():
        for c in range(4):
            at = slice(ROWS * c, ROWS * (c + 1))
            a1[at] = normed(inp[at].astype(F32), gain1)
        for p in pieces:
            at = pl.multiple_of(core * LEN + ROWS * p, ROWS)
            xrow[piece(p)] = inp[pl.ds(at, ROWS)].astype(F32)

    def take_input(p, value):
        x = value.astype(F32)
        xrow[piece(p)] = x
        return normed(x, gain1)

    @pl.when(section == 1)
    def _():
        dyo[...] = cot[...]
        dact[...] = dot_nt(cot[...], wfd[...])
        turned(dyo, dyt)
        hop_receive(0, 0, take_input)
        spread(0, a1)

    source = a1[...]
    proj[:, PQ:PK] = dot(source, wq[...])
    proj[:, PK:PV] = dot(source, wk[...])
    proj[:, PV:PG] = dot(source, wv[...])
    wba = jnp.concatenate(
        [wb[...].astype(F32), wd[...].astype(F32), jnp.zeros((4, 1024), F32)], axis=0
    ).astype(BF16)
    pba = dot_nt(source, wba)
    gpre[...] = dot(source, wgo[...])

    lane = lax.broadcasted_iota(jnp.int32, (LEN, LEN), 1)
    ltri = jnp.where(within, 1.0, 0.0)
    utri = jnp.where(row <= col, 1.0, 0.0)
    betas, decays, slopes = [], [], []
    for s, h in pairs:
        betas.append(sigmoid(pba[seq(s), h : h + 1]))
        pre = pba[seq(s), 2 + h : 3 + h] + sbias[0:1, h : h + 1]
        soft = jnp.maximum(pre, 0.0) + jnp.log1p(jnp.exp(-jnp.abs(pre)))
        rate = -jnp.exp(lrate[0:1, h : h + 1])
        decays.append(rate * soft)
        slopes.append(rate * sigmoid(pre))
    packed = jnp.zeros((LEN, LEN), F32)
    for i in range(4):
        packed = jnp.where(lane == i, decays[i], packed)
    cums = dot_full(ltri, packed)

    for s, h in pairs:
        z = conv_sum(proj[seq(s), qc(h)], taps_q[:, DK * h : DK * (h + 1)])
        zsum[seq(s), qc(h)] = z
        c = z * sigmoid(z)
        rq = lax.rsqrt(jnp.sum(c * c, axis=-1, keepdims=True) + 1e-06)
        qkv[seq(s), qc(h)] = c * (rq * SCALE)
        z = conv_sum(proj[seq(s), kc(h)], taps_k[:, DK * h : DK * (h + 1)])
        zsum[seq(s), kc(h)] = z
        c = z * sigmoid(z)
        rk = lax.rsqrt(jnp.sum(c * c, axis=-1, keepdims=True) + 1e-06)
        qkv[seq(s), kc(h)] = c * rk
        z = conv_sum(proj[seq(s), vc(h)], taps_v[:, hv(h)])
        zsum[seq(s), vc(h)] = z
        qkv[seq(s), vc(h)] = z * sigmoid(z)
        i = 2 * s + h
        cols[0, i] = jnp.broadcast_to(betas[i], (LEN, LEN))
        cols[1, i] = jnp.broadcast_to(decays[i], (LEN, LEN))
        cols[2, i] = jnp.broadcast_to(slopes[i], (LEN, LEN))
        cols[3, i] = jnp.broadcast_to(rq, (LEN, LEN))
        cols[4, i] = jnp.broadcast_to(rk, (LEN, LEN))

    systems = []
    for i, (s, h) in enumerate(pairs):
        cum = jnp.broadcast_to(cums[:, i : i + 1], (LEN, LEN))
        gaps = cum - cum.T
        decay = jnp.where(within, jnp.exp(jnp.where(within, gaps, 0.0)), 0.0)
        dmat[i] = decay
        kn = qkv[seq(s), kc(h)]
        e = jnp.where(strict, dot_nt(kn, kn) * decay, 0.0)
        emat[i] = e
        systems.append(cols[0, i] * e)
        amat[i] = dot_nt(qkv[seq(s), qc(h)], kn) * decay
    for i, inverse in enumerate(unit_inverses(systems)):
        tinv[i] = inverse.astype(BF16)
    for i, (s, h) in enumerate(pairs):
        w = qkv[seq(s), vc(h)] * cols[0, i][:, 0:1]
        umat[i] = dot(tinv[i], w).astype(BF16)
    for i, (s, h) in enumerate(pairs):
        o = dot(amat[i], umat[i])
        ro = lax.rsqrt(jnp.mean(o * o, axis=-1, keepdims=True) + 1e-05)
        cols[5, i] = jnp.broadcast_to(ro, (LEN, LEN))
        on = o * ro
        onorm[seq(s), hv(h)] = on
        gp = gpre[seq(s), hv(h)]
        mix[seq(s), hv(h)] = (on * ogains[:, hv(h)] * (gp * sigmoid(gp))).astype(BF16)

    put_part(0, dot(mix[...], wo[...]))

    def take_middle(p, total):
        h = xrow[piece(p)] + total
        hrow[piece(p)] = h
        return normed(h, gain2)

    all_sum(0, 1, take_middle)
    spread(1, a2)
    source = a2[...]
    upg[...] = dot_nt(source, wfg[...])
    upu[...] = dot_nt(source, wfu[...])

    outs = pair_sum(1)
    out_swaps = chip_swap(1)

    def output_part():
        ug = upg[...]
        s_act = (ug * sigmoid(ug) * upu[...]).astype(BF16)
        act[:, 704:FPAD] = jnp.zeros((2 * LEN, FPAD - 704), BF16)
        act[:, 0:704] = s_act
        put_part(1, dot(s_act, wfd[...]))
        started(outs)

    def output_sum():
        for p in pieces:
            outs[p].wait_recv()
            h = jnp.where(hi == 0, hrow[piece(p)], 0.0)
            fwd[1, p] = (pair_total(1, p) + h).astype(BF16)

    def take_cotangent(p, value):
        return value

    @pl.when(section == 0)
    def _():
        output_part()
        output_sum()
        hops = hop_send(1, 0)
        started(hops)
        sent(hops)
        started(out_swaps)
        turned(a1, a1t)
        turned(a2, a2t)
        hop_receive(1, 2, take_cotangent)
        spread(2, dyo)
        dact[...] = dot_nt(dyo[...], wfd[...])

    ds = dact[...]
    ug = upg[...]
    uu = upu[...]
    sg = sigmoid(ug)
    pad = jnp.zeros((2 * LEN, FPAD - 704), BF16)
    dgu[:, 704:FPAD] = pad
    dgu[:, FPAD + 704 :] = pad
    dgu[:, 0:704] = (ds * uu * (sg * (1.0 + ug * (1.0 - sg)))).astype(BF16)
    dgu[:, FPAD : FPAD + 704] = (ds * (ug * sg)).astype(BF16)
    put_part(2, dot(dgu[:, 0:704], wfg[...]) + dot(dgu[:, FPAD : FPAD + 704], wfu[...]))

    def take_gradient(p, total):
        dz, dgain = rms_back(hrow[piece(p)], gain2, total)
        at = pl.multiple_of(core * LEN + ROWS * p, ROWS)
        dh = dyo[pl.ds(at, ROWS)].astype(F32) + dz
        drow[piece(p)] = dh
        dg2s[p] = dgain
        return dh

    def second_output():
        @pl.when(section == 1)
        def _():
            output_part()
            turned(a1, a1t)
            turned(a2, a2t)

        @pl.when(section == 0)
        def _():
            turned(dyo, dyt)

        grads.ffn_start()

    all_sum(2, 3, take_gradient, second_output)

    @pl.when(section == 1)
    def _():
        output_sum()
        started(out_swaps)

    spread(3, dho)
    dact[:, 0:512] = dot_nt(dho[...], wo[...])
    grads.ffn_relay()

    small[...] = jnp.zeros_like(small)
    douts = [jnp.zeros((1, DV), F32) for _ in range(HEADS)]
    dos = []
    for i, (s, h) in enumerate(pairs):
        dm = dact[seq(s), hv(h)]
        gp = gpre[seq(s), hv(h)]
        sg = sigmoid(gp)
        on = onorm[seq(s), hv(h)]
        og = ogains[:, hv(h)]
        dgate = dm * on
        dpr[seq(s), PG + DV * h : PG + DV * (h + 1)] = (
            dgate * og * (sg * (1.0 + gp * (1.0 - sg)))
        ).astype(BF16)
        silu_g = gp * sg
        douts[h] = douts[h] + jnp.sum(dgate * silu_g, axis=0, keepdims=True)
        don = dm * silu_g * og
        ro = cols[5, i][:, 0:1]
        do = ro * (don - on * jnp.mean(don * on, axis=-1, keepdims=True))
        dos.append(do.astype(BF16))
    for h in range(HEADS):
        small[6:7, hv(h)] = douts[h]
    das = [dot_nt(dos[i], umat[i]) for i in range(4)]
    dus = [dot(amat[i].T, dos[i]) for i in range(4)]
    dws = [dot(tinv[i].astype(F32).T, dus[i]) for i in range(4)]
    dms = [jnp.where(strict, -dot_nt(dws[i], umat[i]), 0.0) for i in range(4)]
    dbetas, dcs, dqs, dks = [], [], [], []
    for i, (s, h) in enumerate(pairs):
        beta = cols[0, i]
        e = emat[i]
        decay = dmat[i]
        v = qkv[seq(s), vc(h)]
        de = dms[i] * e
        dbetas.append(
            jnp.sum(dws[i] * v, axis=-1, keepdims=True) + jnp.sum(de, axis=-1, keepdims=True)
        )
        dgap = das[i] * amat[i] + de * beta
        dcs.append(jnp.sum(dgap - dgap.T, axis=-1, keepdims=True))
        dqk = das[i] * decay
        dkk = dms[i] * beta * decay
        kn = qkv[seq(s), kc(h)]
        qn = qkv[seq(s), qc(h)]
        dqs.append(dot(dqk, kn))
        dks.append(dot(dqk.T, qn) + dot(dkk + dkk.T, kn))
    packed = jnp.zeros((LEN, LEN), F32)
    for i in range(4):
        packed = jnp.where(lane == i, dcs[i], packed)
    dgs = dot_full(utri, packed)

    dcq = [jnp.zeros((1, DK), F32) for _ in range(4 * HEADS)]
    dck = [jnp.zeros((1, DK), F32) for _ in range(4 * HEADS)]
    dcv = [jnp.zeros((1, DV), F32) for _ in range(4 * HEADS)]

    def conv_back(dz, at_rows, at_cols, taps, sums, h):
        pre = proj[at_rows, at_cols]
        total = dz * taps[3:4]
        for j in range(3):
            total = total + shift_up(dz, 3 - j) * taps[j : j + 1]
        for j in range(4):
            sums[4 * h + j] = sums[4 * h + j] + jnp.sum(
                dz * shift_down(pre, 3 - j), axis=0, keepdims=True
            )
        dpr[at_rows, at_cols] = total.astype(BF16)

    for i, (s, h) in enumerate(pairs):
        qn = qkv[seq(s), qc(h)]
        dq = dqs[i]
        dc = (cols[3, i] * SCALE) * (
            dq - qn * (jnp.sum(qn * dq, axis=-1, keepdims=True) * (1.0 / (SCALE * SCALE)))
        )
        dz = dc * silu_slope(zsum[seq(s), qc(h)])
        conv_back(dz, seq(s), qc(h), taps_q[:, DK * h : DK * (h + 1)], dcq, h)
        kn = qkv[seq(s), kc(h)]
        dk = dks[i]
        dc = cols[4, i] * (dk - kn * jnp.sum(kn * dk, axis=-1, keepdims=True))
        dz = dc * silu_slope(zsum[seq(s), kc(h)])
        conv_back(dz, seq(s), kc(h), taps_k[:, DK * h : DK * (h + 1)], dck, h)
        dv = dws[i] * cols[0, i][:, 0:1]
        dz = dv * silu_slope(zsum[seq(s), vc(h)])
        conv_back(dz, seq(s), vc(h), taps_v[:, hv(h)], dcv, h)
    for h in range(HEADS):
        for j in range(4):
            small[2 + j : 3 + j, DK * h : DK * (h + 1)] = dcq[4 * h + j]
            small[2 + j : 3 + j, 256 + DK * h : 256 + DK * (h + 1)] = dck[4 * h + j]
            small[2 + j : 3 + j, 512 + DV * h : 512 + DV * (h + 1)] = dcv[4 * h + j]
    lane_row = lax.broadcasted_iota(jnp.int32, (1, LEN), 1)
    scal = jnp.zeros((1, LEN), F32)
    for s in range(2):
        block = jnp.zeros((LEN, LEN), F32)
        for h in range(HEADS):
            i = 2 * s + h
            beta = cols[0, i]
            dg = jnp.broadcast_to(dgs[:, i : i + 1], (LEN, LEN))
            dpb = dbetas[i] * beta * (1.0 - beta)
            dpa = dg * cols[2, i]
            block = jnp.where(lane == h, dpb, block)
            block = jnp.where(lane == 2 + h, dpa, block)
            scal = scal + jnp.where(
                lane_row == h, jnp.sum(dg * cols[1, i], axis=0, keepdims=True), 0.0
            )
            scal = scal + jnp.where(lane_row == 2 + h, jnp.sum(dpa, axis=0, keepdims=True), 0.0)
        dpr[seq(s), PB:PEND] = block.astype(BF16)
    small[6:7, 512:640] = scal

    def mixer_grads():
        turned(dho, dht)
        grads.mix_start()

    pl.when(section == 0)(mixer_grads)
    value = dot_nt(dpr[:, PQ:PK], wq[...])
    value = value + dot_nt(dpr[:, PK:PV], wk[...])
    value = value + dot_nt(dpr[:, PV:PG], wv[...])
    value = value + dot_nt(dpr[:, PG:PB], wgo[...])
    value = value + dot(dpr[:, PB:PEND][:, 0:8], wba)
    put_part(3, value)
    firsts, swaps = pair_sum(3), chip_swap(3)
    started(firsts)
    dgain1 = jnp.zeros((1, 1024), F32)
    for p in pieces:
        firsts[p].wait_recv()
        dz, dgain = rms_back(xrow[piece(p)], gain1, pair_total(3, p))
        dgain1 = dgain1 + dgain
        fwd[3, p] = (dz + jnp.where(hi == 0, drow[piece(p)], 0.0)).astype(BF16)
    gains[0, 0] = dgain1
    gains[0, 1] = jnp.where(hi == 0, dg2s[0] + dg2s[1], 0.0)

    @pl.when(section == 1)
    def _():
        hops = hop_send(3, 1)
        started(hops)
        mixer_grads()
        sent(hops)

    started(swaps)
    sums = [
        remote(
            gains.at[0], gains.at[step], ga_s.at[step - 1], ga_r.at[step - 1],
            {"tensor": (t + step) % 4},
        )
        for step in range(1, 4)
    ]
    started(sums)
    hidden, back = pair_share(4), pair_share(5)
    for p in pieces:
        out_swaps[p].wait_recv()
        gbuf[4, core, p] = chip_total(1, p).astype(BF16)
        hidden[p].start()
    grads.ffn_merge()
    grads.mix_relay()
    for p in pieces:
        swaps[p].wait_recv()
        gbuf[5, core, p] = chip_total(3, p).astype(BF16)
        back[p].start()
    received(sums)
    small[0:1] = (gains[0, 0] + gains[2, 0]) + (gains[1, 0] + gains[3, 0])
    small[1:2] = (gains[0, 1] + gains[2, 1]) + (gains[1, 1] + gains[3, 1])
    grads.small_start(small)
    grads.ffn_relay_second()
    received(hidden)
    spread(4, hid)
    received(back)
    spread(5, ing)
    grads.mix_merge()
    grads.small_relay()
    grads.ffn_finish()
    grads.mix_relay_second()
    grads.small_finish()
    grads.mix_finish()
    sent(outs + out_swaps + firsts + swaps + sums + hidden + back)
    grads.sent()


def run_layer(args):
    tokens = 2 * LEN
    results = [((tokens, 1024), BF16)] * 2 + [
        (shape, F32)
        for shape in (
            (ROWS, 256), (ROWS, 256), (ROWS, 512), (2, ROWS), (2, ROWS), (ROWS, 512),
            (ROWS, 512), (ROWS, 704), (ROWS, 704), (ROWS, 704), (8, 1024),
        )
    ]
    rows = (2, ROWS, 1024)
    buffers = [
        pltpu.VMEM((tokens, n), BF16) for n in (1024, PEND, 1024, 2 * FPAD, 1024, 512, 1024, FPAD)
    ] + [pltpu.VMEM((8, 1024), F32)] + [pltpu.VMEM((4, 4, ROWS, 256), BF16)] * 4 + [
        pltpu.VMEM((4, 2) + rows, BF16),
        pltpu.VMEM((4,) + rows, BF16),
        pltpu.VMEM((4,) + rows, BF16),
        pltpu.VMEM((4,) + rows, BF16),
        pltpu.VMEM((2, 2) + rows, BF16),
        pltpu.VMEM((6, 2) + rows, BF16),
        pltpu.VMEM((LEN, 1024), F32),
        pltpu.VMEM((LEN, 1024), F32),
        pltpu.VMEM((LEN, 1024), F32),
        pltpu.VMEM((tokens, 1024), F32),
        pltpu.VMEM((tokens, 1024), F32),
        pltpu.VMEM((tokens, 1024), F32),
        pltpu.VMEM((tokens, 512), F32),
        pltpu.VMEM((tokens, 512), F32),
        pltpu.VMEM((tokens, 704), F32),
        pltpu.VMEM((tokens, 704), F32),
        pltpu.VMEM((tokens, 704), F32),
        pltpu.VMEM((4, LEN, LEN), BF16),
        pltpu.VMEM((4, LEN, LEN), F32),
        pltpu.VMEM((4, LEN, LEN), F32),
        pltpu.VMEM((4, LEN, LEN), F32),
        pltpu.VMEM((4, LEN, DV), BF16),
        pltpu.VMEM((6, 4, LEN, LEN), F32),
        pltpu.VMEM((4, 2, 1, 1024), F32),
        pltpu.VMEM((2, 1, 1024), F32),
    ]
    sems = [
        pltpu.SemaphoreType.DMA((4, 2)), pltpu.SemaphoreType.DMA((4, 2)),
        pltpu.SemaphoreType.DMA((4, 2)), pltpu.SemaphoreType.DMA((4, 2)),
        pltpu.SemaphoreType.DMA((6, 2)), pltpu.SemaphoreType.DMA((6, 2)),
        pltpu.SemaphoreType.DMA((2, 2, 2)), pltpu.SemaphoreType.DMA((2, 2, 2)),
        pltpu.SemaphoreType.DMA((3,)), pltpu.SemaphoreType.DMA((3,)),
    ]
    return pl.pallas_call(
        layer_kernel,
        out_shape=[jax.ShapeDtypeStruct(s, d) for s, d in results],
        in_specs=[pl.BlockSpec(memory_space=pltpu.VMEM)] * len(args),
        out_specs=[pl.BlockSpec(memory_space=pltpu.VMEM)] * len(results),
        scratch_shapes=buffers + sems + sum_scratch(),
        compiler_params=pltpu.CompilerParams(
            collective_id=0, has_side_effects=True, vmem_limit_bytes=61 * 1024 * 1024
        ),
        name="layer",
    )(*args)


def result_kernel(*refs):
    hid, ing, gq, gk, gv, gb, gd, ggo, gout, gfg, gfu, gfd, sums = refs[:13]
    outs = refs[13:]
    dg1, dcq, dck, dcv, dlr, dsb, dog, dg2 = outs[12:]
    for source, out in zip((hid, ing, gq, gk, gv, gb, gd, ggo, gout, gfg, gfu, gfd), outs):
        out[...] = source[...]
    dg1[...] = sums[0:1]
    dg2[...] = sums[1:2]
    dcq[...] = sums[2:6, 0:256]
    dck[...] = sums[2:6, 256:512]
    dcv[...] = sums[2:6, 512:1024]
    dog[...] = sums[6:7, 0:512]
    dlr[...] = sums[6:7, 512:514]
    dsb[...] = sums[6:7, 514:516]


def run_results(args):
    results = [(v.shape, v.dtype) for v in args[:12]] + [
        (shape, F32)
        for shape in (
            (1, 1024), (4, 256), (4, 256), (4, 512), (1, 2), (1, 2), (1, 512), (1, 1024)
        )
    ]
    return pl.pallas_call(
        result_kernel,
        out_shape=[jax.ShapeDtypeStruct(s, d) for s, d in results],
        in_specs=[pl.BlockSpec(memory_space=pltpu.VMEM)] * len(args),
        out_specs=[pl.BlockSpec(memory_space=pltpu.VMEM)] * len(results),
        compiler_params=pltpu.CompilerParams(vmem_limit_bytes=60 * 1024 * 1024),
        name="results",
    )(*args)


def per_device(
    inputs, cotangent, norm_gain1, w_query, w_key, w_value, conv_query, conv_key, conv_value,
    w_beta, w_decay, log_rate, step_bias, out_gain, w_gate_out, w_out, norm_gain2,
    w_ffn_gate, w_ffn_up, w_ffn_down,
):
    tokens = 2 * LEN
    width = inputs.shape[-1]
    out = run_layer((
        inputs.reshape(tokens, width), cotangent.reshape(tokens, width),
        norm_gain1, w_query[0], w_key[0], w_value[0],
        conv_query[0], conv_key[0], conv_value[0], w_beta[0].T, w_decay[0].T,
        log_rate, step_bias, out_gain, w_gate_out[0], w_out[0], norm_gain2,
        w_ffn_gate[0].T, w_ffn_up[0].T, w_ffn_down[0],
    ))
    (
        hidden, input_grad, gq, gk, gv, gb, gd, ggo, gout, gfg, gfu, gfd,
        dg1, dcq, dck, dcv, dlr, dsb, dog, dg2,
    ) = run_results(tuple(out))
    shape = (1,) + inputs.shape
    return (
        hidden.reshape(shape), input_grad.reshape(shape), dg1, gq[None], gk[None], gv[None],
        dcq[None], dck[None], dcv[None], gb.T[None], gd.T[None], dlr, dsb, dog,
        ggo[None], gout.T[None], dg2, gfg[None], gfu[None], gfd.T[None],
    )


def solution(mesh):
    three = P("section", None, "tensor")
    in_specs = (
        P(None, "dp", None, None), P(None, "dp", None, None), P("section", None),
        three, three, three, three, three, three, three, three,
        P("section", "tensor"), P("section", "tensor"), P("section", "tensor"),
        three, P("section", "tensor", None), P("section", None),
        three, three, P("section", "tensor", None),
    )
    spread = P("section", "dp", "tensor")
    out_specs = (
        P("section", None, "dp", None, None), P("section", None, "dp", None, None),
        P("section", None), spread, spread, spread, three, three, three, spread, spread,
        P("section", "tensor"), P("section", "tensor"), P("section", "tensor"),
        spread, P("section", "tensor", "dp"), P("section", None),
        spread, spread, P("section", "tensor", "dp"),
    )
    return jax.shard_map(
        per_device, mesh=mesh, in_specs=in_specs, out_specs=out_specs, check_vma=False
    )
```

```python
import jax
import jax.numpy as jnp
from jax import lax
from jax.experimental import pallas as pl
from jax.experimental.pallas import tpu as pltpu
from jax.sharding import PartitionSpec as P

F32 = jnp.float32
BF16 = jnp.bfloat16
MESH = pl.DeviceIdType.MESH
LEN = 128
ROWS = 64
HEADS = 2
DK = 128
DV = 256
SCALE = DK**-0.5
PQ, PK, PV, PG, PB, PEND = 0, 256, 512, 1024, 1536, 1664
FPAD = 768
FF = 704
PAIR = 2 * FF
NF = 1152
NG = PAIR - NF + FPAD
NQ = PV + 512
NV = PEND - PV


def dot(left, right):
    return jnp.dot(left.astype(BF16), right.astype(BF16), preferred_element_type=F32)


def dot_nt(left, right):
    return lax.dot_general(
        left.astype(BF16),
        right.astype(BF16),
        (((1,), (1,)), ((), ())),
        preferred_element_type=F32,
    )


def dot_full(left, right):
    return jnp.dot(left, right, precision=lax.Precision.HIGHEST, preferred_element_type=F32)


def sigmoid(v):
    return 1.0 / (1.0 + jnp.exp(-v))


def rows_of(shape):
    return lax.broadcasted_iota(jnp.int32, shape, 0)


def shift_down(v, steps):
    if steps == 0:
        return v
    return jnp.where(rows_of(v.shape) >= steps, pltpu.roll(v, steps, 0), 0.0)


def shift_up(v, steps):
    if steps == 0:
        return v
    count = v.shape[0]
    return jnp.where(rows_of(v.shape) < count - steps, pltpu.roll(v, count - steps, 0), 0.0)


def conv_sum(v, taps):
    total = v * taps[3:4]
    for j in range(3):
        total = total + shift_down(v, 3 - j) * taps[j : j + 1]
    return total


def silu_slope(z):
    s = sigmoid(z)
    return s * (1.0 + z * (1.0 - s))


def unit_inverses(systems):
    row = lax.broadcasted_iota(jnp.int32, (LEN, LEN), 0)
    col = lax.broadcasted_iota(jnp.int32, (LEN, LEN), 1)
    eye = jnp.where(row == col, 1.0, 0.0)

    def band(level):
        same = (row >> (level + 1)) == (col >> (level + 1))
        return same & (((row >> level) & 1) == 1) & (((col >> level) & 1) == 0)

    first = band(0)
    inverses = [eye - jnp.where(first, m, 0.0) for m in systems]
    for level in range(1, 7):
        at = band(level)
        halves = [dot(t, jnp.where(at, m, 0.0)) for t, m in zip(inverses, systems)]
        inverses = [t - dot(x, t) for t, x in zip(inverses, halves)]
    return inverses


def rms_back(z, gain, dn):
    inv = lax.rsqrt(jnp.mean(z * z, axis=-1, keepdims=True) + 1e-06)
    hat = z * inv
    weighted = dn * gain
    dz = (weighted - hat * jnp.mean(weighted * hat, axis=-1, keepdims=True)) * inv
    return dz, jnp.sum(dn * hat, axis=0, keepdims=True)


def torus_steps(place):
    z = place // 4
    x = place % 4
    along_x = [{"dp": z * 4 + (x + step) % 4} for step in range(1, 4)]
    along_z = [{"dp": ((z + step) % 4) * 4 + x} for step in range(1, 4)]
    return along_x + along_z


def turned(source, out):
    for rows in range(4):
        flat = source[:, 256 * rows : 256 * (rows + 1)].T
        for c in range(4):
            out[rows, c] = flat[ROWS * c : ROWS * (c + 1)]


def add_into(ref, more):
    if len(more.shape) == 3:
        @pl.loop(0, more.shape[0])
        def _(c):
            ref[c] = (ref[c].astype(F32) + more[c].astype(F32)).astype(BF16)
    else:
        ref[...] = (ref[...].astype(F32) + more[...].astype(F32)).astype(BF16)


class Ring:
    def __init__(self, remote, g, me, devices, bufs, send, recv, half):
        one_p, one_m, two_p, two_m = bufs
        after, _, before = devices
        self.g, self.me, self.bufs = g, me, bufs
        self.right = right = (me + 1) % 4
        self.left = left = (me + 3) % 4
        self.far = far = (me + 2) % 4
        lo, up = pl.ds(0, half), pl.ds(half, half)
        self.lo, self.up = lo, up
        self.p1 = remote(g.at[far, lo], one_p, send.at[0], recv.at[0], after)
        self.m1 = remote(g.at[far, up], one_m, send.at[1], recv.at[1], before)
        self.p2 = remote(g.at[right, up], two_p.at[up], send.at[2], recv.at[2], after)
        self.m2 = remote(g.at[left, lo], two_m.at[lo], send.at[3], recv.at[3], before)
        self.p3 = remote(g.at[right, lo], two_p.at[lo], send.at[4], recv.at[4], after)
        self.m3 = remote(g.at[left, up], two_m.at[up], send.at[5], recv.at[5], before)
        self.steps = ((far, (self.p1, self.m1)), (right, (self.p2,)), (left, (self.m2,)))

    def start(self):
        for _, copies in self.steps:
            for copy in copies:
                copy.start()

    def relay(self):
        one_p, one_m, _, _ = self.bufs
        self.p1.wait_recv()
        add_into(self.g.at[self.right, self.lo], one_p)
        self.p3.start()
        self.m1.wait_recv()
        add_into(self.g.at[self.left, self.up], one_m)
        self.m3.start()

    def arrive(self):
        for copy in (self.p2, self.m2, self.p3, self.m3):
            copy.wait_recv()

    def sent(self):
        for copy in (self.p1, self.m1, self.p2, self.m2, self.p3, self.m3):
            copy.wait_send()

    def merge(self, out):
        _, _, two_p, two_m = self.bufs

        @pl.loop(0, 4)
        def _(c):
            out[c] = (
                self.g[self.me, c].astype(F32) + two_p[c].astype(F32) + two_m[c].astype(F32)
            ).astype(BF16)

    def total(self, start, size):
        _, _, two_p, two_m = self.bufs
        at = slice(start, start + size)
        return (
            self.g[self.me, :, at].astype(F32)
            + two_p[:, at].astype(F32)
            + two_m[:, at].astype(F32)
        )


WIDTHS = (NF, NG, NQ, NV)


def sum_scratch():
    scratch = []
    for n in WIDTHS:
        scratch.append(pltpu.VMEM((4, 4, ROWS, n), BF16))
        scratch += [pltpu.VMEM((2, ROWS, n), BF16)] * 2 + [pltpu.VMEM((4, ROWS, n), BF16)] * 3
        scratch += [pltpu.VMEM((ROWS // 2, n), BF16)] * 2 + [pltpu.VMEM((ROWS, n), BF16)] * 2
    scratch += [pltpu.VMEM((4, 8, 1024), F32)] * 2
    scratch += [pltpu.SemaphoreType.DMA((8, 6))] * 2 + [pltpu.SemaphoreType.DMA((6,))] * 2
    return scratch


class Sums:
    def __init__(self, place, remote, data, outs, refs):
        self.data, self.outs = data, outs
        z, x = place // 4, place % 4
        steps = torus_steps(place)
        ways = ((x, steps[:3]), (z, steps[3:]))
        self.sx, self.sz, send, recv, ssend, srecv = refs[-6:]
        self.first, self.second, self.half = [], [], []
        for k in range(4):
            g, one_p, one_m, two_p, two_m, h, a, b, c, d = refs[10 * k : 10 * k + 10]
            me, way = ways[k % 2]
            self.first.append(
                Ring(remote, g, me, way, (one_p, one_m, two_p, two_m), send.at[k], recv.at[k], 2)
            )
            me, way = ways[1 - k % 2]
            self.second.append(
                Ring(remote, h, me, way, (a, b, c, d), send.at[4 + k], recv.at[4 + k], ROWS // 2)
            )
        self.small_x = [
            remote(self.sx.at[0], self.sx.at[i + 1], ssend.at[i], srecv.at[i], steps[i])
            for i in range(3)
        ]
        self.small_z = [
            remote(self.sz.at[0], self.sz.at[i + 1], ssend.at[3 + i], srecv.at[3 + i], steps[3 + i])
            for i in range(3)
        ]

    def chunk(self, k, c):
        data = self.data
        out = self.first[k].g.at[c]

        def outer(left, right, first, width, offset):
            rows = left[:, c] if k % 2 == 0 else left[c]
            flat = rows.reshape(4 * ROWS, 2 * LEN)
            for start in range(0, width, 256):
                size = min(256, width - start)
                value = jnp.dot(
                    flat, right[:, first + start : first + start + size],
                    preferred_element_type=F32,
                ).astype(BF16)
                for i in range(4):
                    out[i, :, offset + start : offset + start + size] = value[
                        ROWS * i : ROWS * (i + 1)
                    ]

        if k == 0:
            outer(data["a2"], data["pair"], 0, NF, 0)
        elif k == 1:
            outer(data["a2"], data["pair"], NF, PAIR - NF, 0)
            outer(data["dy"], data["act"], 0, FPAD, PAIR - NF)
        elif k == 2:
            outer(data["a1"], data["proj"], PQ, PV, 0)
            outer(data["dh"], data["mix"], 0, 512, PV)
        else:
            outer(data["a1"], data["proj"], PV, PEND - PV, 0)

    def begin(self, groups):
        for step in range(3):
            for k in groups:
                at, copies = self.first[k].steps[step]
                self.chunk(k, at)
                for copy in copies:
                    copy.start()
        for k in groups:
            self.chunk(k, self.first[k].me)

    def merge(self, groups):
        for k in groups:
            self.first[k].arrive()
            self.first[k].merge(self.second[k].g)
            self.second[k].start()

    def ffn_start(self):
        self.begin((0, 1))

    def ffn_relay(self):
        self.first[0].relay()
        self.first[1].relay()

    def ffn_merge(self):
        self.merge((0, 1))

    def ffn_relay_second(self):
        self.second[0].relay()
        self.second[1].relay()

    def ffn_finish(self):
        one, two, outs = self.second[0], self.second[1], self.outs
        one.arrive()
        outs["fg"][...] = one.total(0, FPAD)[:, 0:FF]
        outs["fu"][:, 0 : NF - FF] = one.total(640, NF - 640)[:, FF - 640 :]
        two.arrive()
        outs["fu"][:, NF - FF : FF] = two.total(0, PAIR - NF)
        outs["fd"][...] = two.total(PAIR - NF, FPAD)[:, 0:FF]

    def mix_start(self):
        self.begin((2, 3))

    def mix_relay(self):
        self.first[2].relay()
        self.first[3].relay()

    def mix_merge(self):
        self.merge((2, 3))

    def mix_relay_second(self):
        self.second[2].relay()
        self.second[3].relay()

    def mix_finish(self):
        one, two, outs = self.second[2], self.second[3], self.outs
        one.arrive()
        outs["q"][...] = one.total(0, 256)
        outs["k"][...] = one.total(256, 256)
        outs["out"][...] = one.total(PV, 512)
        two.arrive()
        outs["v"][...] = two.total(0, 512)
        outs["go"][...] = two.total(512, 512)
        both = two.total(1024, PEND - PB).T
        outs["b"][...] = both[0:2]
        outs["d"][...] = both[2:4]

    def small_start(self, small):
        self.sx[0] = small[...]
        for copy in self.small_x:
            copy.start()

    def small_relay(self):
        sx = self.sx
        for copy in self.small_x:
            copy.wait_recv()
        self.sz[0] = (sx[0] + sx[2]) + (sx[1] + sx[3])
        for copy in self.small_z:
            copy.start()

    def small_finish(self):
        sz = self.sz
        for copy in self.small_z:
            copy.wait_recv()
        self.outs["small"][...] = (sz[0] + sz[2]) + (sz[1] + sz[3])

    def sent(self):
        for ring in self.first + self.second:
            ring.sent()
        for copy in self.small_x + self.small_z:
            copy.wait_send()


def layer_kernel(
    inp, cot, g1, wq, wk, wv, cvq, cvk, cvv, wb, wd, lrate, sbias, ogain, wgo, wo, g2, wfg, wfu, wfd,
    hid, ing, gq, gk, gv, gb, gd, ggo, gout, gfg, gfu, gfd, gsmall,
    a1, dpr, a2, dgu, dho, mix, dyo, act, small, a1t, a2t, dht, dyt,
    part, r1, r2, fwd, hopb, gbuf, xrow, hrow, drow,
    proj, zsum, qkv, gpre, onorm, upg, upu, dact,
    tinv, amat, dmat, emat, umat, cols, gains, dg1s, dg2s,
    rs_s, rs_r, op_s, op_r, ag_s, ag_r, hop_s, hop_r, ga_s, ga_r,
    *sum_refs,
):
    section = lax.axis_index("section")
    t = lax.axis_index("tensor")
    hi = t // 2
    core = t % 2
    sib = hi * 2 + (1 - core)
    opp = (1 - hi) * 2 + core
    other = 1 - section
    seqs = range(2)

    def remote(src, dst, ssem, rsem, device):
        return pltpu.make_async_remote_copy(
            src_ref=src, dst_ref=dst, send_sem=ssem, recv_sem=rsem,
            device_id=device, device_id_type=MESH,
        )

    barrier = pltpu.get_barrier_semaphore()
    for step in range(1, 4):
        pl.semaphore_signal(
            barrier, inc=1, device_id={"tensor": (t + step) % 4}, device_id_type=MESH
        )
    for step in range(4):
        pl.semaphore_signal(
            barrier, inc=1, device_id={"section": other, "tensor": (t + step) % 4},
            device_id_type=MESH,
        )
    place = lax.axis_index("dp")
    links = torus_steps(place)
    for device in links:
        pl.semaphore_signal(barrier, inc=1, device_id=device, device_id_type=MESH)
    pl.semaphore_wait(barrier, 7 + len(links))

    grads = Sums(
        place, remote,
        dict(a1=a1t, a2=a2t, dh=dht, dy=dyt, proj=dpr, pair=dgu, mix=mix, act=act),
        dict(q=gq, k=gk, v=gv, b=gb, d=gd, go=ggo, out=gout, fg=gfg, fu=gfu, fd=gfd, small=gsmall),
        sum_refs,
    )

    def pair_sum(ph):
        return [
            remote(part.at[ph, s, 1 - core], r1.at[ph, s], rs_s.at[ph, s], rs_r.at[ph, s],
                   {"tensor": sib})
            for s in seqs
        ]

    def chip_swap(ph):
        return [
            remote(fwd.at[ph, s], r2.at[ph, s], op_s.at[ph, s], op_r.at[ph, s], {"tensor": opp})
            for s in seqs
        ]

    def pair_share(k):
        return [
            remote(gbuf.at[k, s, core], gbuf.at[k, s, core], ag_s.at[k, s], ag_r.at[k, s],
                   {"tensor": sib})
            for s in seqs
        ]

    def hop_send(ph, k, s):
        return [
            remote(fwd.at[ph, s], hopb.at[k, hi, s], hop_s.at[k, y, s], hop_r.at[k, hi, s],
                   {"section": other, "tensor": 2 * y + core})
            for y in range(2)
        ]

    def started(copies):
        for copy in copies:
            copy.start()

    def received(copies):
        for copy in copies:
            copy.wait_recv()

    def sent(copies):
        for copy in copies:
            copy.wait_send()

    def pair_total(ph, s):
        return part[ph, s, core].astype(F32) + r1[ph, s].astype(F32)

    def chip_total(ph, s):
        return fwd[ph, s].astype(F32) + r2[ph, s].astype(F32)

    def swap(ph, s):
        firsts[ph][s].wait_recv()
        fwd[ph, s] = pair_total(ph, s).astype(BF16)
        swaps[ph][s].start()

    def hop_receive(k, share, s, finish, out):
        passes = pair_share(share)[s]
        for y in range(2):
            remote(hopb.at[k, y, s], hopb.at[k, y, s], hop_s.at[k, y, s], hop_r.at[k, y, s],
                   {"section": other, "tensor": t}).wait_recv()
        value = (hopb[k, 0, s].astype(F32) + hopb[k, 1, s].astype(F32)).astype(BF16)
        gbuf[share, s, core] = finish(s, value)
        passes.start()
        passes.wait_recv()
        spread(share, s, out)
        passes.wait_send()

    def put_part(ph, s, value):
        for p in range(2):
            part[ph, s, p] = value[ROWS * p : ROWS * (p + 1)].astype(BF16)

    def spread(k, s, out):
        for p in range(2):
            at = LEN * s + ROWS * p
            out[at : at + ROWS] = gbuf[k, s, p]

    def piece(s):
        return slice(ROWS * s, ROWS * (s + 1))

    def mine(s):
        return pl.ds(pl.multiple_of(core * ROWS + LEN * s, ROWS), ROWS)

    def normed(x, gain):
        inv = lax.rsqrt(jnp.mean(x * x, axis=-1, keepdims=True) + 1e-06)
        return (x * inv * gain).astype(BF16)

    firsts = [pair_sum(ph) for ph in range(4)]
    swaps = [chip_swap(ph) for ph in range(4)]
    middles, backs, hiddens, inners = (pair_share(k) for k in (1, 3, 4, 5))
    row = lax.broadcasted_iota(jnp.int32, (LEN, LEN), 0)
    col = lax.broadcasted_iota(jnp.int32, (LEN, LEN), 1)
    within = row >= col
    strict = row > col
    gain1 = g1[...].astype(F32)
    gain2 = g2[...].astype(F32)
    ogains = ogain[...].astype(F32)
    taps_q = cvq[...].astype(F32)
    taps_k = cvk[...].astype(F32)
    taps_v = cvv[...].astype(F32)

    def seq(s):
        return slice(LEN * s, LEN * (s + 1))

    def qc(h):
        return slice(PQ + DK * h, PQ + DK * (h + 1))

    def kc(h):
        return slice(PK + DK * h, PK + DK * (h + 1))

    def vc(h):
        return slice(PV + DV * h, PV + DV * (h + 1))

    def hv(h):
        return slice(DV * h, DV * (h + 1))

    lane = lax.broadcasted_iota(jnp.int32, (LEN, LEN), 1)
    lane_row = lax.broadcasted_iota(jnp.int32, (1, LEN), 1)
    ltri = jnp.where(within, 1.0, 0.0)
    utri = jnp.where(row <= col, 1.0, 0.0)
    wba = jnp.concatenate(
        [wb[...].astype(F32), wd[...].astype(F32), jnp.zeros((4, 1024), F32)], axis=0
    ).astype(BF16)

    def pair_of(columns):
        packed = jnp.zeros((LEN, LEN), F32)
        for h in range(HEADS):
            packed = jnp.where(lane == h, columns[h], packed)
        return packed

    def mixer_systems(s):
        at = seq(s)
        source = a1[at]
        proj[at, PQ:PK] = dot(source, wq[...])
        proj[at, PK:PV] = dot(source, wk[...])
        proj[at, PV:PG] = dot(source, wv[...])
        pba = dot_nt(source, wba)
        gpre[at] = dot(source, wgo[...])
        betas, decays, slopes = [], [], []
        for h in range(HEADS):
            betas.append(sigmoid(pba[:, h : h + 1]))
            pre = pba[:, 2 + h : 3 + h] + sbias[0:1, h : h + 1]
            soft = jnp.maximum(pre, 0.0) + jnp.log1p(jnp.exp(-jnp.abs(pre)))
            rate = -jnp.exp(lrate[0:1, h : h + 1])
            decays.append(rate * soft)
            slopes.append(rate * sigmoid(pre))
        cums = dot_full(ltri, pair_of(decays))
        for h in range(HEADS):
            z = conv_sum(proj[at, qc(h)], taps_q[:, DK * h : DK * (h + 1)])
            zsum[at, qc(h)] = z
            c = z * sigmoid(z)
            rq = lax.rsqrt(jnp.sum(c * c, axis=-1, keepdims=True) + 1e-06)
            qkv[at, qc(h)] = c * (rq * SCALE)
            z = conv_sum(proj[at, kc(h)], taps_k[:, DK * h : DK * (h + 1)])
            zsum[at, kc(h)] = z
            c = z * sigmoid(z)
            rk = lax.rsqrt(jnp.sum(c * c, axis=-1, keepdims=True) + 1e-06)
            qkv[at, kc(h)] = c * rk
            z = conv_sum(proj[at, vc(h)], taps_v[:, hv(h)])
            zsum[at, vc(h)] = z
            qkv[at, vc(h)] = z * sigmoid(z)
            i = 2 * s + h
            cols[0, i] = jnp.broadcast_to(betas[h], (LEN, LEN))
            cols[1, i] = jnp.broadcast_to(decays[h], (LEN, LEN))
            cols[2, i] = jnp.broadcast_to(slopes[h], (LEN, LEN))
            cols[3, i] = jnp.broadcast_to(rq, (LEN, LEN))
            cols[4, i] = jnp.broadcast_to(rk, (LEN, LEN))
        systems = []
        for h in range(HEADS):
            i = 2 * s + h
            cum = jnp.broadcast_to(cums[:, h : h + 1], (LEN, LEN))
            gaps = cum - cum.T
            decay = jnp.where(within, jnp.exp(jnp.where(within, gaps, 0.0)), 0.0)
            dmat[i] = decay
            kn = qkv[at, kc(h)]
            e = jnp.where(strict, dot_nt(kn, kn) * decay, 0.0)
            emat[i] = e
            systems.append(cols[0, i] * e)
            amat[i] = dot_nt(qkv[at, qc(h)], kn) * decay
        return systems

    def mixer_outputs(s, systems):
        at = seq(s)
        for h, inverse in enumerate(unit_inverses(systems)):
            tinv[2 * s + h] = inverse.astype(BF16)
        for h in range(HEADS):
            i = 2 * s + h
            w = qkv[at, vc(h)] * cols[0, i][:, 0:1]
            umat[i] = dot(tinv[i], w).astype(BF16)
        for h in range(HEADS):
            i = 2 * s + h
            o = dot(amat[i], umat[i])
            ro = lax.rsqrt(jnp.mean(o * o, axis=-1, keepdims=True) + 1e-05)
            cols[5, i] = jnp.broadcast_to(ro, (LEN, LEN))
            on = o * ro
            onorm[at, hv(h)] = on
            gp = gpre[at, hv(h)]
            mix[at, hv(h)] = (on * ogains[:, hv(h)] * (gp * sigmoid(gp))).astype(BF16)
        put_part(0, s, dot(mix[at], wo[...]))

    def take_middle(s):
        swaps[0][s].wait_recv()
        h = xrow[piece(s)] + chip_total(0, s)
        hrow[piece(s)] = h
        gbuf[1, s, core] = normed(h, gain2)
        middles[s].start()

    def ffn_inputs(s):
        middles[s].wait_recv()
        spread(1, s, a2)
        source = a2[seq(s)]
        upg[seq(s)] = dot_nt(source, wfg[...])
        upu[seq(s)] = dot_nt(source, wfu[...])

    def ffn_outputs(s):
        at = seq(s)
        ug = upg[at]
        s_act = (ug * sigmoid(ug) * upu[at]).astype(BF16)
        act[at, FF:FPAD] = jnp.zeros((LEN, FPAD - FF), BF16)
        act[at, 0:FF] = s_act
        put_part(1, s, dot(s_act, wfd[...]))
        firsts[1][s].start()

    def ffn_output_sum(s):
        firsts[1][s].wait_recv()
        h = jnp.where(hi == 0, hrow[piece(s)], 0.0)
        fwd[1, s] = (pair_total(1, s) + h).astype(BF16)

    def ffn_back(s):
        at = seq(s)
        ds = dact[at]
        ug = upg[at]
        uu = upu[at]
        sg = sigmoid(ug)
        dug = (ds * uu * (sg * (1.0 + ug * (1.0 - sg)))).astype(BF16)
        duu = (ds * (ug * sg)).astype(BF16)
        put_part(2, s, dot(dug, wfg[...]) + dot(duu, wfu[...]))
        firsts[2][s].start()
        dgu[at, 0:FF] = dug
        dgu[at, FF:PAIR] = duu

    def take_gradient(s):
        swaps[2][s].wait_recv()
        dz, dgain = rms_back(hrow[piece(s)], gain2, chip_total(2, s))
        dh = dyo[mine(s)].astype(F32) + dz
        drow[piece(s)] = dh
        dg2s[s] = dgain
        gbuf[3, s, core] = dh.astype(BF16)
        backs[s].start()

    def mixer_back(s):
        at = seq(s)
        backs[s].wait_recv()
        spread(3, s, dho)
        dmix = dot_nt(dho[at], wo[...])
        dos = []
        for h in range(HEADS):
            i = 2 * s + h
            dm = dmix[:, hv(h)]
            gp = gpre[at, hv(h)]
            sg = sigmoid(gp)
            on = onorm[at, hv(h)]
            og = ogains[:, hv(h)]
            dgate = dm * on
            dpr[at, PG + DV * h : PG + DV * (h + 1)] = (
                dgate * og * (sg * (1.0 + gp * (1.0 - sg)))
            ).astype(BF16)
            silu_g = gp * sg
            small[6:7, hv(h)] += jnp.sum(dgate * silu_g, axis=0, keepdims=True)
            don = dm * silu_g * og
            ro = cols[5, i][:, 0:1]
            do = ro * (don - on * jnp.mean(don * on, axis=-1, keepdims=True))
            dos.append(do.astype(BF16))
        index = [2 * s + h for h in range(HEADS)]
        das = [dot_nt(do, umat[i]) for i, do in zip(index, dos)]
        dus = [dot(amat[i].T, do) for i, do in zip(index, dos)]
        dws = [dot(tinv[i].astype(F32).T, du) for i, du in zip(index, dus)]
        dms = [jnp.where(strict, -dot_nt(dw, umat[i]), 0.0) for i, dw in zip(index, dws)]
        return das, dws, dms

    def conv_back(dz, at_rows, at_cols, taps, place_in_small):
        pre = proj[at_rows, at_cols]
        total = dz * taps[3:4]
        for j in range(3):
            total = total + shift_up(dz, 3 - j) * taps[j : j + 1]
        for j in range(4):
            small[2 + j : 3 + j, place_in_small] += jnp.sum(
                dz * shift_down(pre, 3 - j), axis=0, keepdims=True
            )
        dpr[at_rows, at_cols] = total.astype(BF16)

    def mixer_inputs_back(s, kept):
        das, dws, dms = kept
        at = seq(s)
        dbetas, dcs, dqs, dks = [], [], [], []
        for h in range(HEADS):
            i = 2 * s + h
            beta = cols[0, i]
            e = emat[i]
            decay = dmat[i]
            de = dms[h] * e
            dbetas.append(
                jnp.sum(dws[h] * qkv[at, vc(h)], axis=-1, keepdims=True)
                + jnp.sum(de, axis=-1, keepdims=True)
            )
            dgap = das[h] * amat[i] + de * beta
            dcs.append(jnp.sum(dgap - dgap.T, axis=-1, keepdims=True))
            dqk = das[h] * decay
            dkk = dms[h] * beta * decay
            kn = qkv[at, kc(h)]
            qn = qkv[at, qc(h)]
            dqs.append(dot(dqk, kn))
            dks.append(dot(dqk.T, qn) + dot(dkk + dkk.T, kn))
        dgs = dot_full(utri, pair_of(dcs))
        for h in range(HEADS):
            i = 2 * s + h
            qn = qkv[at, qc(h)]
            dq = dqs[h]
            dc = (cols[3, i] * SCALE) * (
                dq - qn * (jnp.sum(qn * dq, axis=-1, keepdims=True) * (1.0 / (SCALE * SCALE)))
            )
            dz = dc * silu_slope(zsum[at, qc(h)])
            conv_back(dz, at, qc(h), taps_q[:, DK * h : DK * (h + 1)], qc(h))
            kn = qkv[at, kc(h)]
            dk = dks[h]
            dc = cols[4, i] * (dk - kn * jnp.sum(kn * dk, axis=-1, keepdims=True))
            dz = dc * silu_slope(zsum[at, kc(h)])
            conv_back(dz, at, kc(h), taps_k[:, DK * h : DK * (h + 1)], kc(h))
            dv = dws[h] * cols[0, i][:, 0:1]
            dz = dv * silu_slope(zsum[at, vc(h)])
            conv_back(dz, at, vc(h), taps_v[:, hv(h)], vc(h))
        scal = jnp.zeros((1, LEN), F32)
        block = jnp.zeros((LEN, LEN), F32)
        for h in range(HEADS):
            i = 2 * s + h
            beta = cols[0, i]
            dg = jnp.broadcast_to(dgs[:, h : h + 1], (LEN, LEN))
            dpb = dbetas[h] * beta * (1.0 - beta)
            dpa = dg * cols[2, i]
            block = jnp.where(lane == h, dpb, block)
            block = jnp.where(lane == 2 + h, dpa, block)
            scal = scal + jnp.where(
                lane_row == h, jnp.sum(dg * cols[1, i], axis=0, keepdims=True), 0.0
            )
            scal = scal + jnp.where(lane_row == 2 + h, jnp.sum(dpa, axis=0, keepdims=True), 0.0)
        dpr[at, PB:PEND] = block.astype(BF16)
        small[6:7, 512:640] += scal

    def layer_back(s):
        at = seq(s)
        value = dot_nt(dpr[at, PQ:PK], wq[...])
        value = value + dot_nt(dpr[at, PK:PV], wk[...])
        value = value + dot_nt(dpr[at, PV:PG], wv[...])
        value = value + dot_nt(dpr[at, PG:PB], wgo[...])
        value = value + dot(dpr[at, PB:PEND][:, 0:8], wba)
        put_part(3, s, value)
        firsts[3][s].start()

    def layer_back_sum(s):
        firsts[3][s].wait_recv()
        dz, dgain = rms_back(xrow[piece(s)], gain1, pair_total(3, s))
        dg1s[s] = dgain
        fwd[3, s] = (dz + jnp.where(hi == 0, drow[piece(s)], 0.0)).astype(BF16)

    small[...] = jnp.zeros_like(small)

    @pl.when(section == 0)
    def _():
        for c in range(4):
            at = slice(ROWS * c, ROWS * (c + 1))
            a1[at] = normed(inp[at].astype(F32), gain1)
        for s in seqs:
            xrow[piece(s)] = inp[mine(s)].astype(F32)

    @pl.when(section == 1)
    def _():
        dyo[...] = cot[...]
        dact[...] = dot_nt(cot[...], wfd[...])
        turned(dyo, dyt)

    def take_input(s, value):
        x = value.astype(F32)
        xrow[piece(s)] = x
        return normed(x, gain1)

    for s in seqs:
        @pl.when(section == 1)
        def _():
            hop_receive(0, 0, s, take_input, a1)

        systems = mixer_systems(s)
        if s == 1:
            swap(0, 0)
        mixer_outputs(s, systems)
        firsts[0][s].start()
    swap(0, 1)

    take_middle(0)
    ffn_inputs(0)

    @pl.when(section == 0)
    def _():
        ffn_outputs(0)

    @pl.when(section == 1)
    def _():
        ffn_back(0)

    take_middle(1)

    @pl.when(section == 0)
    def _():
        ffn_output_sum(0)
        started(hop_send(1, 0, 0))

    @pl.when(section == 1)
    def _():
        swap(2, 0)

    ffn_inputs(1)

    def take_cotangent(s, value):
        return value

    @pl.when(section == 0)
    def _():
        ffn_outputs(1)
        ffn_output_sum(1)
        started(hop_send(1, 0, 1))
        turned(a1, a1t)
        turned(a2, a2t)
        for s in seqs:
            sent(hop_send(1, 0, s))
        started(swaps[1])
        for s in seqs:
            hop_receive(1, 2, s, take_cotangent, dyo)
            dact[seq(s)] = dot_nt(dyo[seq(s)], wfd[...])
            ffn_back(s)
            swap(2, s)
        turned(dyo, dyt)
        grads.ffn_start()

    @pl.when(section == 1)
    def _():
        ffn_back(1)
        swap(2, 1)

    take_gradient(0)
    kept = mixer_back(0)
    take_gradient(1)
    mixer_inputs_back(0, kept)
    layer_back(0)
    kept = mixer_back(1)
    layer_back_sum(0)

    @pl.when(section == 0)
    def _():
        grads.ffn_relay()

    @pl.when(section == 1)
    def _():
        started(hop_send(3, 1, 0))

    mixer_inputs_back(1, kept)

    @pl.when(section == 0)
    def _():
        turned(dho, dht)
        grads.mix_start()

    layer_back(1)
    layer_back_sum(1)

    @pl.when(section == 1)
    def _():
        started(hop_send(3, 1, 1))
        for s in seqs:
            ffn_outputs(s)
        turned(a2, a2t)
        grads.ffn_start()
        for s in seqs:
            ffn_output_sum(s)
        turned(a1, a1t)
        turned(dho, dht)
        grads.ffn_relay()
        grads.mix_start()
        for s in seqs:
            sent(hop_send(3, 1, s))
        started(swaps[1])

    started(swaps[3])
    gains[0, 0] = dg1s[0] + dg1s[1]
    gains[0, 1] = jnp.where(hi == 0, dg2s[0] + dg2s[1], 0.0)
    sums = [
        remote(
            gains.at[0], gains.at[step], ga_s.at[step - 1], ga_r.at[step - 1],
            {"tensor": (t + step) % 4},
        )
        for step in range(1, 4)
    ]
    started(sums)
    grads.ffn_merge()
    for s in seqs:
        swaps[1][s].wait_recv()
        gbuf[4, s, core] = chip_total(1, s).astype(BF16)
        hiddens[s].start()
    received(sums)
    small[0:1] = (gains[0, 0] + gains[2, 0]) + (gains[1, 0] + gains[3, 0])
    small[1:2] = (gains[0, 1] + gains[2, 1]) + (gains[1, 1] + gains[3, 1])
    grads.small_start(small)
    for s in seqs:
        swaps[3][s].wait_recv()
        gbuf[5, s, core] = chip_total(3, s).astype(BF16)
        inners[s].start()
    grads.mix_relay()
    grads.ffn_relay_second()
    for s in seqs:
        hiddens[s].wait_recv()
        spread(4, s, hid)
        inners[s].wait_recv()
        spread(5, s, ing)
    grads.small_relay()
    grads.mix_merge()
    grads.ffn_finish()
    grads.small_finish()
    grads.mix_relay_second()
    grads.mix_finish()
    for ph in range(4):
        sent(firsts[ph] + swaps[ph])
    sent(sums + middles + backs + hiddens + inners)
    grads.sent()


def run_layer(args):
    tokens = 2 * LEN
    results = [((tokens, 1024), BF16)] * 2 + [
        (shape, F32)
        for shape in (
            (ROWS, 256), (ROWS, 256), (ROWS, 512), (2, ROWS), (2, ROWS), (ROWS, 512),
            (ROWS, 512), (ROWS, 704), (ROWS, 704), (ROWS, 704), (8, 1024),
        )
    ]
    rows = (2, ROWS, 1024)
    buffers = [
        pltpu.VMEM((tokens, n), BF16) for n in (1024, PEND, 1024, PAIR, 1024, 512, 1024, FPAD)
    ] + [pltpu.VMEM((8, 1024), F32)] + [pltpu.VMEM((4, 4, ROWS, 256), BF16)] * 4 + [
        pltpu.VMEM((4, 2) + rows, BF16),
        pltpu.VMEM((4,) + rows, BF16),
        pltpu.VMEM((4,) + rows, BF16),
        pltpu.VMEM((4,) + rows, BF16),
        pltpu.VMEM((2, 2) + rows, BF16),
        pltpu.VMEM((6, 2) + rows, BF16),
        pltpu.VMEM((LEN, 1024), F32),
        pltpu.VMEM((LEN, 1024), F32),
        pltpu.VMEM((LEN, 1024), F32),
        pltpu.VMEM((tokens, 1024), F32),
        pltpu.VMEM((tokens, 1024), F32),
        pltpu.VMEM((tokens, 1024), F32),
        pltpu.VMEM((tokens, 512), F32),
        pltpu.VMEM((tokens, 512), F32),
        pltpu.VMEM((tokens, 704), F32),
        pltpu.VMEM((tokens, 704), F32),
        pltpu.VMEM((tokens, 704), F32),
        pltpu.VMEM((4, LEN, LEN), BF16),
        pltpu.VMEM((4, LEN, LEN), F32),
        pltpu.VMEM((4, LEN, LEN), F32),
        pltpu.VMEM((4, LEN, LEN), F32),
        pltpu.VMEM((4, LEN, DV), BF16),
        pltpu.VMEM((6, 4, LEN, LEN), F32),
        pltpu.VMEM((4, 2, 1, 1024), F32),
        pltpu.VMEM((2, 1, 1024), F32),
        pltpu.VMEM((2, 1, 1024), F32),
    ]
    sems = [
        pltpu.SemaphoreType.DMA((4, 2)), pltpu.SemaphoreType.DMA((4, 2)),
        pltpu.SemaphoreType.DMA((4, 2)), pltpu.SemaphoreType.DMA((4, 2)),
        pltpu.SemaphoreType.DMA((6, 2)), pltpu.SemaphoreType.DMA((6, 2)),
        pltpu.SemaphoreType.DMA((2, 2, 2)), pltpu.SemaphoreType.DMA((2, 2, 2)),
        pltpu.SemaphoreType.DMA((3,)), pltpu.SemaphoreType.DMA((3,)),
    ]
    return pl.pallas_call(
        layer_kernel,
        out_shape=[jax.ShapeDtypeStruct(s, d) for s, d in results],
        in_specs=[pl.BlockSpec(memory_space=pltpu.VMEM)] * len(args),
        out_specs=[pl.BlockSpec(memory_space=pltpu.VMEM)] * len(results),
        scratch_shapes=buffers + sems + sum_scratch(),
        compiler_params=pltpu.CompilerParams(
            collective_id=0, has_side_effects=True, vmem_limit_bytes=61 * 1024 * 1024
        ),
        name="layer",
    )(*args)


def result_kernel(*refs):
    hid, ing, gq, gk, gv, gb, gd, ggo, gout, gfg, gfu, gfd, sums = refs[:13]
    outs = refs[13:]
    dg1, dcq, dck, dcv, dlr, dsb, dog, dg2 = outs[12:]
    for source, out in zip((hid, ing, gq, gk, gv, gb, gd, ggo, gout, gfg, gfu, gfd), outs):
        out[...] = source[...]
    dg1[...] = sums[0:1]
    dg2[...] = sums[1:2]
    dcq[...] = sums[2:6, 0:256]
    dck[...] = sums[2:6, 256:512]
    dcv[...] = sums[2:6, 512:1024]
    dog[...] = sums[6:7, 0:512]
    dlr[...] = sums[6:7, 512:514]
    dsb[...] = sums[6:7, 514:516]


def run_results(args):
    results = [(v.shape, v.dtype) for v in args[:12]] + [
        (shape, F32)
        for shape in (
            (1, 1024), (4, 256), (4, 256), (4, 512), (1, 2), (1, 2), (1, 512), (1, 1024)
        )
    ]
    return pl.pallas_call(
        result_kernel,
        out_shape=[jax.ShapeDtypeStruct(s, d) for s, d in results],
        in_specs=[pl.BlockSpec(memory_space=pltpu.VMEM)] * len(args),
        out_specs=[pl.BlockSpec(memory_space=pltpu.VMEM)] * len(results),
        compiler_params=pltpu.CompilerParams(vmem_limit_bytes=60 * 1024 * 1024),
        name="results",
    )(*args)


def per_device(
    inputs, cotangent, norm_gain1, w_query, w_key, w_value, conv_query, conv_key, conv_value,
    w_beta, w_decay, log_rate, step_bias, out_gain, w_gate_out, w_out, norm_gain2,
    w_ffn_gate, w_ffn_up, w_ffn_down,
):
    tokens = 2 * LEN
    width = inputs.shape[-1]
    out = run_layer((
        inputs.reshape(tokens, width), cotangent.reshape(tokens, width),
        norm_gain1, w_query[0], w_key[0], w_value[0],
        conv_query[0], conv_key[0], conv_value[0], w_beta[0].T, w_decay[0].T,
        log_rate, step_bias, out_gain, w_gate_out[0], w_out[0], norm_gain2,
        w_ffn_gate[0].T, w_ffn_up[0].T, w_ffn_down[0],
    ))
    (
        hidden, input_grad, gq, gk, gv, gb, gd, ggo, gout, gfg, gfu, gfd,
        dg1, dcq, dck, dcv, dlr, dsb, dog, dg2,
    ) = run_results(tuple(out))
    shape = (1,) + inputs.shape
    return (
        hidden.reshape(shape), input_grad.reshape(shape), dg1, gq[None], gk[None], gv[None],
        dcq[None], dck[None], dcv[None], gb.T[None], gd.T[None], dlr, dsb, dog,
        ggo[None], gout.T[None], dg2, gfg[None], gfu[None], gfd.T[None],
    )


def solution(mesh):
    three = P("section", None, "tensor")
    in_specs = (
        P(None, "dp", None, None), P(None, "dp", None, None), P("section", None),
        three, three, three, three, three, three, three, three,
        P("section", "tensor"), P("section", "tensor"), P("section", "tensor"),
        three, P("section", "tensor", None), P("section", None),
        three, three, P("section", "tensor", None),
    )
    spread = P("section", "dp", "tensor")
    out_specs = (
        P("section", None, "dp", None, None), P("section", None, "dp", None, None),
        P("section", None), spread, spread, spread, three, three, three, spread, spread,
        P("section", "tensor"), P("section", "tensor"), P("section", "tensor"),
        spread, P("section", "tensor", "dp"), P("section", None),
        spread, spread, P("section", "tensor", "dp"),
    )
    return jax.shard_map(
        per_device, mesh=mesh, in_specs=in_specs, out_specs=out_specs, check_vma=False
    )
```

```python
import jax
import jax.numpy as jnp
from jax import lax
from jax.experimental import pallas as pl
from jax.experimental.pallas import tpu as pltpu
from jax.sharding import PartitionSpec as P

F32 = jnp.float32
BF16 = jnp.bfloat16
MESH = pl.DeviceIdType.MESH
LEN = 128
ROWS = 64
HEADS = 2
DK = 128
DV = 256
SCALE = DK**-0.5
PQ, PK, PV, PG, PB, PEND = 0, 256, 512, 1024, 1536, 1664
FPAD = 768
FF = 704
PAIR = 2 * FF
NF = 1152
NG = PAIR - NF + FPAD
NO = 512
NV = 512 + PEND - PB


def dot(left, right):
    return jnp.dot(left.astype(BF16), right.astype(BF16), preferred_element_type=F32)


def dot_nt(left, right):
    return lax.dot_general(
        left.astype(BF16),
        right.astype(BF16),
        (((1,), (1,)), ((), ())),
        preferred_element_type=F32,
    )


def dot_full(left, right):
    return jnp.dot(left, right, precision=lax.Precision.HIGHEST, preferred_element_type=F32)


def sigmoid(v):
    return 1.0 / (1.0 + jnp.exp(-v))


def rows_of(shape):
    return lax.broadcasted_iota(jnp.int32, shape, 0)


def shift_down(v, steps):
    if steps == 0:
        return v
    return jnp.where(rows_of(v.shape) >= steps, pltpu.roll(v, steps, 0), 0.0)


def shift_up(v, steps):
    if steps == 0:
        return v
    count = v.shape[0]
    return jnp.where(rows_of(v.shape) < count - steps, pltpu.roll(v, count - steps, 0), 0.0)


def conv_sum(v, taps):
    total = v * taps[3:4]
    for j in range(3):
        total = total + shift_down(v, 3 - j) * taps[j : j + 1]
    return total


def silu_slope(z):
    s = sigmoid(z)
    return s * (1.0 + z * (1.0 - s))


def unit_inverses(systems):
    row = lax.broadcasted_iota(jnp.int32, (LEN, LEN), 0)
    col = lax.broadcasted_iota(jnp.int32, (LEN, LEN), 1)
    eye = jnp.where(row == col, 1.0, 0.0)

    def band(level):
        same = (row >> (level + 1)) == (col >> (level + 1))
        return same & (((row >> level) & 1) == 1) & (((col >> level) & 1) == 0)

    first = band(0)
    inverses = [eye - jnp.where(first, m, 0.0) for m in systems]
    for level in range(1, 7):
        at = band(level)
        halves = [dot(t, jnp.where(at, m, 0.0)) for t, m in zip(inverses, systems)]
        inverses = [t - dot(x, t) for t, x in zip(inverses, halves)]
    return inverses


def rms_back(z, gain, dn):
    inv = lax.rsqrt(jnp.mean(z * z, axis=-1, keepdims=True) + 1e-06)
    hat = z * inv
    weighted = dn * gain
    dz = (weighted - hat * jnp.mean(weighted * hat, axis=-1, keepdims=True)) * inv
    return dz, jnp.sum(dn * hat, axis=0, keepdims=True)


def torus_steps(place):
    z = place // 4
    x = place % 4
    along_x = [{"dp": z * 4 + (x + step) % 4} for step in range(1, 4)]
    along_z = [{"dp": ((z + step) % 4) * 4 + x} for step in range(1, 4)]
    return along_x + along_z


def turned(source, out):
    for rows in range(4):
        flat = source[:, 256 * rows : 256 * (rows + 1)].T
        for c in range(4):
            out[rows, c] = flat[ROWS * c : ROWS * (c + 1)]


def add_into(ref, more):
    if len(more.shape) == 3:
        @pl.loop(0, more.shape[0])
        def _(c):
            ref[c] = (ref[c].astype(F32) + more[c].astype(F32)).astype(BF16)
    else:
        ref[...] = (ref[...].astype(F32) + more[...].astype(F32)).astype(BF16)


class Ring:
    def __init__(self, remote, g, me, devices, bufs, send, recv, half):
        one_p, one_m, two_p, two_m = bufs
        after, _, before = devices
        self.g, self.me, self.bufs = g, me, bufs
        self.right = right = (me + 1) % 4
        self.left = left = (me + 3) % 4
        self.far = far = (me + 2) % 4
        lo, up = pl.ds(0, half), pl.ds(half, half)
        self.lo, self.up = lo, up
        self.p1 = remote(g.at[far, lo], one_p, send.at[0], recv.at[0], after)
        self.m1 = remote(g.at[far, up], one_m, send.at[1], recv.at[1], before)
        self.p2 = remote(g.at[right, up], two_p.at[up], send.at[2], recv.at[2], after)
        self.m2 = remote(g.at[left, lo], two_m.at[lo], send.at[3], recv.at[3], before)
        self.p3 = remote(g.at[right, lo], two_p.at[lo], send.at[4], recv.at[4], after)
        self.m3 = remote(g.at[left, up], two_m.at[up], send.at[5], recv.at[5], before)
        self.steps = ((far, (self.p1, self.m1)), (right, (self.p2,)), (left, (self.m2,)))

    def start(self):
        for _, copies in self.steps:
            for copy in copies:
                copy.start()

    def relay(self):
        one_p, one_m, _, _ = self.bufs
        self.p1.wait_recv()
        add_into(self.g.at[self.right, self.lo], one_p)
        self.p3.start()
        self.m1.wait_recv()
        add_into(self.g.at[self.left, self.up], one_m)
        self.m3.start()

    def arrive(self):
        for copy in (self.p2, self.m2, self.p3, self.m3):
            copy.wait_recv()

    def sent(self):
        for copy in (self.p1, self.m1, self.p2, self.m2, self.p3, self.m3):
            copy.wait_send()

    def merge(self, out):
        _, _, two_p, two_m = self.bufs

        @pl.loop(0, 4)
        def _(c):
            out[c] = (
                self.g[self.me, c].astype(F32) + two_p[c].astype(F32) + two_m[c].astype(F32)
            ).astype(BF16)

    def total(self, start, size):
        _, _, two_p, two_m = self.bufs
        at = slice(start, start + size)
        return (
            self.g[self.me, :, at].astype(F32)
            + two_p[:, at].astype(F32)
            + two_m[:, at].astype(F32)
        )


FFN, GATE, MIX = (0, 1), (2, 3), (4, 5)
WIDTHS = (NF, NG, NO, NO, PV, NV)


def sum_scratch():
    scratch = []
    for n in WIDTHS:
        scratch.append(pltpu.VMEM((4, 4, ROWS, n), BF16))
        scratch += [pltpu.VMEM((2, ROWS, n), BF16)] * 2 + [pltpu.VMEM((4, ROWS, n), BF16)] * 3
        scratch += [pltpu.VMEM((ROWS // 2, n), BF16)] * 2 + [pltpu.VMEM((ROWS, n), BF16)] * 2
    scratch += [pltpu.VMEM((4, 8, 1024), F32)] * 2
    scratch += [pltpu.SemaphoreType.DMA((12, 6))] * 2 + [pltpu.SemaphoreType.DMA((6,))] * 2
    return scratch


class Sums:
    def __init__(self, place, remote, data, outs, refs):
        self.data, self.outs = data, outs
        z, x = place // 4, place % 4
        steps = torus_steps(place)
        ways = ((x, steps[:3]), (z, steps[3:]))
        self.sx, self.sz, send, recv, ssend, srecv = refs[-6:]
        self.first, self.second, self.half = [], [], []
        for k in range(6):
            g, one_p, one_m, two_p, two_m, h, a, b, c, d = refs[10 * k : 10 * k + 10]
            me, way = ways[k % 2]
            self.first.append(
                Ring(remote, g, me, way, (one_p, one_m, two_p, two_m), send.at[k], recv.at[k], 2)
            )
            me, way = ways[1 - k % 2]
            self.second.append(
                Ring(remote, h, me, way, (a, b, c, d), send.at[6 + k], recv.at[6 + k], ROWS // 2)
            )
        self.small_x = [
            remote(self.sx.at[0], self.sx.at[i + 1], ssend.at[i], srecv.at[i], steps[i])
            for i in range(3)
        ]
        self.small_z = [
            remote(self.sz.at[0], self.sz.at[i + 1], ssend.at[3 + i], srecv.at[3 + i], steps[3 + i])
            for i in range(3)
        ]

    def chunk(self, k, c):
        data = self.data
        out = self.first[k].g.at[c]

        def outer(left, right, first, width, offset):
            rows = left[:, c] if k % 2 == 0 else left[c]
            flat = rows.reshape(4 * ROWS, 2 * LEN)
            for start in range(0, width, 256):
                size = min(256, width - start)
                value = jnp.dot(
                    flat, right[:, first + start : first + start + size],
                    preferred_element_type=F32,
                ).astype(BF16)
                for i in range(4):
                    out[i, :, offset + start : offset + start + size] = value[
                        ROWS * i : ROWS * (i + 1)
                    ]

        if k == 0:
            outer(data["a2"], data["pair"], 0, NF, 0)
        elif k == 1:
            outer(data["a2"], data["pair"], NF, PAIR - NF, 0)
            outer(data["dy"], data["act"], 0, FPAD, PAIR - NF)
        elif k == 2:
            outer(data["dh"], data["mix"], 0, NO, 0)
        elif k == 3:
            outer(data["a1"], data["proj"], PG, NO, 0)
        elif k == 4:
            outer(data["a1"], data["proj"], PQ, PV, 0)
        else:
            outer(data["a1"], data["proj"], PV, PG - PV, 0)
            outer(data["a1"], data["proj"], PB, PEND - PB, PG - PV)

    def begin(self, groups):
        for step in range(3):
            for k in groups:
                at, copies = self.first[k].steps[step]
                self.chunk(k, at)
                for copy in copies:
                    copy.start()
        for k in groups:
            self.chunk(k, self.first[k].me)

    def merge(self, groups):
        for k in groups:
            self.first[k].arrive()
            self.first[k].merge(self.second[k].g)
            self.second[k].start()

    def relay(self, groups):
        for k in groups:
            self.first[k].relay()

    def relay_second(self, groups):
        for k in groups:
            self.second[k].relay()

    def ffn_finish(self):
        one, two, outs = self.second[0], self.second[1], self.outs
        one.arrive()
        outs["fg"][...] = one.total(0, FPAD)[:, 0:FF]
        outs["fu"][:, 0 : NF - FF] = one.total(640, NF - 640)[:, FF - 640 :]
        two.arrive()
        outs["fu"][:, NF - FF : FF] = two.total(0, PAIR - NF)
        outs["fd"][...] = two.total(PAIR - NF, FPAD)[:, 0:FF]

    def gate_finish(self):
        one, two, outs = self.second[2], self.second[3], self.outs
        one.arrive()
        outs["out"][...] = one.total(0, NO)
        two.arrive()
        outs["go"][...] = two.total(0, NO)

    def mix_finish(self):
        one, two, outs = self.second[4], self.second[5], self.outs
        one.arrive()
        outs["q"][...] = one.total(0, 256)
        outs["k"][...] = one.total(256, 256)
        two.arrive()
        outs["v"][...] = two.total(0, 512)
        both = two.total(512, PEND - PB).T
        outs["b"][...] = both[0:2]
        outs["d"][...] = both[2:4]

    def small_start(self, small):
        self.sx[0] = small[...]
        for copy in self.small_x:
            copy.start()

    def small_relay(self):
        sx = self.sx
        for copy in self.small_x:
            copy.wait_recv()
        self.sz[0] = (sx[0] + sx[2]) + (sx[1] + sx[3])
        for copy in self.small_z:
            copy.start()

    def small_finish(self):
        sz = self.sz
        for copy in self.small_z:
            copy.wait_recv()
        self.outs["small"][...] = (sz[0] + sz[2]) + (sz[1] + sz[3])

    def sent(self):
        for ring in self.first + self.second:
            ring.sent()
        for copy in self.small_x + self.small_z:
            copy.wait_send()


def layer_kernel(
    inp, cot, g1, cvq, cvk, cvv, wb, wd, lrate, sbias, ogain, g2,
    hq, hk, hval, hgo, ho, hfg, hfu, hfd,
    hid, ing, gq, gk, gv, gb, gd, ggo, gout, gfg, gfu, gfd, gsmall,
    wq, wk, wv, wgo, wo, wfg, wfu, wfd, w_s,
    a1, dpr, a2, dgu, dho, mix, dyo, act, small, a1t, a2t, dht, dyt,
    part, r1, r2, fwd, hopb, gbuf, xrow, hrow, drow,
    proj, zsum, qkv, gpre, onorm, upg, upu, dact,
    tinv, amat, dmat, emat, umat, cols, gains, dg1s, dg2s,
    rs_s, rs_r, op_s, op_r, ag_s, ag_r, hop_s, hop_r, ga_s, ga_r,
    *sum_refs,
):
    section = lax.axis_index("section")
    t = lax.axis_index("tensor")
    hi = t // 2
    core = t % 2
    sib = hi * 2 + (1 - core)
    opp = (1 - hi) * 2 + core
    other = 1 - section
    seqs = range(2)

    def remote(src, dst, ssem, rsem, device):
        return pltpu.make_async_remote_copy(
            src_ref=src, dst_ref=dst, send_sem=ssem, recv_sem=rsem,
            device_id=device, device_id_type=MESH,
        )

    stored = (hq, hk, hval, hgo, ho, hfg, hfu, hfd)
    held = (wq, wk, wv, wgo, wo, wfg, wfu, wfd)
    loads = [pltpu.make_async_copy(a, b, w_s.at[i]) for i, (a, b) in enumerate(zip(stored, held))]
    for i in (0, 1, 2, 3, 4, 7, 5, 6):
        loads[i].start()

    barrier = pltpu.get_barrier_semaphore()
    for step in range(1, 4):
        pl.semaphore_signal(
            barrier, inc=1, device_id={"tensor": (t + step) % 4}, device_id_type=MESH
        )
    for step in range(4):
        pl.semaphore_signal(
            barrier, inc=1, device_id={"section": other, "tensor": (t + step) % 4},
            device_id_type=MESH,
        )
    place = lax.axis_index("dp")
    links = torus_steps(place)
    for device in links:
        pl.semaphore_signal(barrier, inc=1, device_id=device, device_id_type=MESH)

    def all_entered():
        pl.semaphore_wait(barrier, 7 + len(links))

    grads = Sums(
        place, remote,
        dict(a1=a1t, a2=a2t, dh=dht, dy=dyt, proj=dpr, pair=dgu, mix=mix, act=act),
        dict(q=gq, k=gk, v=gv, b=gb, d=gd, go=ggo, out=gout, fg=gfg, fu=gfu, fd=gfd, small=gsmall),
        sum_refs,
    )

    def pair_sum(ph):
        return [
            remote(part.at[ph, s, 1 - core], r1.at[ph, s], rs_s.at[ph, s], rs_r.at[ph, s],
                   {"tensor": sib})
            for s in seqs
        ]

    def chip_swap(ph):
        return [
            remote(fwd.at[ph, s], r2.at[ph, s], op_s.at[ph, s], op_r.at[ph, s], {"tensor": opp})
            for s in seqs
        ]

    def pair_share(k):
        return [
            remote(gbuf.at[k, s, core], gbuf.at[k, s, core], ag_s.at[k, s], ag_r.at[k, s],
                   {"tensor": sib})
            for s in seqs
        ]

    def hop_send(ph, k, s):
        return [
            remote(fwd.at[ph, s], hopb.at[k, hi, s], hop_s.at[k, y, s], hop_r.at[k, hi, s],
                   {"section": other, "tensor": 2 * y + core})
            for y in range(2)
        ]

    def started(copies):
        for copy in copies:
            copy.start()

    def received(copies):
        for copy in copies:
            copy.wait_recv()

    def sent(copies):
        for copy in copies:
            copy.wait_send()

    def pair_total(ph, s):
        return part[ph, s, core].astype(F32) + r1[ph, s].astype(F32)

    def chip_total(ph, s):
        return fwd[ph, s].astype(F32) + r2[ph, s].astype(F32)

    def swap(ph, s):
        firsts[ph][s].wait_recv()
        fwd[ph, s] = pair_total(ph, s).astype(BF16)
        swaps[ph][s].start()

    def hop_receive(k, share, s, finish, out):
        passes = pair_share(share)[s]
        for y in range(2):
            remote(hopb.at[k, y, s], hopb.at[k, y, s], hop_s.at[k, y, s], hop_r.at[k, y, s],
                   {"section": other, "tensor": t}).wait_recv()
        value = (hopb[k, 0, s].astype(F32) + hopb[k, 1, s].astype(F32)).astype(BF16)
        gbuf[share, s, core] = finish(s, value)
        passes.start()
        passes.wait_recv()
        spread(share, s, out)
        passes.wait_send()

    def put_part(ph, s, value):
        for p in range(2):
            part[ph, s, p] = value[ROWS * p : ROWS * (p + 1)].astype(BF16)

    def spread(k, s, out):
        for p in range(2):
            at = LEN * s + ROWS * p
            out[at : at + ROWS] = gbuf[k, s, p]

    def piece(s):
        return slice(ROWS * s, ROWS * (s + 1))

    def mine(s):
        return pl.ds(pl.multiple_of(core * ROWS + LEN * s, ROWS), ROWS)

    def normed(x, gain):
        inv = lax.rsqrt(jnp.mean(x * x, axis=-1, keepdims=True) + 1e-06)
        return (x * inv * gain).astype(BF16)

    firsts = [pair_sum(ph) for ph in range(4)]
    swaps = [chip_swap(ph) for ph in range(4)]
    middles, backs, hiddens, inners = (pair_share(k) for k in (1, 3, 4, 5))
    row = lax.broadcasted_iota(jnp.int32, (LEN, LEN), 0)
    col = lax.broadcasted_iota(jnp.int32, (LEN, LEN), 1)
    within = row >= col
    strict = row > col
    gain1 = g1[...].astype(F32)
    gain2 = g2[...].astype(F32)
    ogains = ogain[...].astype(F32)
    taps_q = cvq[...].astype(F32)
    taps_k = cvk[...].astype(F32)
    taps_v = cvv[...].astype(F32)

    def seq(s):
        return slice(LEN * s, LEN * (s + 1))

    def qc(h):
        return slice(PQ + DK * h, PQ + DK * (h + 1))

    def kc(h):
        return slice(PK + DK * h, PK + DK * (h + 1))

    def vc(h):
        return slice(PV + DV * h, PV + DV * (h + 1))

    def hv(h):
        return slice(DV * h, DV * (h + 1))

    lane = lax.broadcasted_iota(jnp.int32, (LEN, LEN), 1)
    lane_row = lax.broadcasted_iota(jnp.int32, (1, LEN), 1)
    ltri = jnp.where(within, 1.0, 0.0)
    utri = jnp.where(row <= col, 1.0, 0.0)
    wba = jnp.concatenate(
        [wb[...].astype(F32), wd[...].astype(F32), jnp.zeros((4, 1024), F32)], axis=0
    ).astype(BF16)

    def pair_of(columns):
        packed = jnp.zeros((LEN, LEN), F32)
        for h in range(HEADS):
            packed = jnp.where(lane == h, columns[h], packed)
        return packed

    def mixer_systems(s):
        at = seq(s)
        source = a1[at]
        proj[at, PQ:PK] = dot(source, wq[...])
        proj[at, PK:PV] = dot(source, wk[...])
        proj[at, PV:PG] = dot(source, wv[...])
        pba = dot_nt(source, wba)
        gpre[at] = dot(source, wgo[...])
        betas, decays, slopes = [], [], []
        for h in range(HEADS):
            betas.append(sigmoid(pba[:, h : h + 1]))
            pre = pba[:, 2 + h : 3 + h] + sbias[0:1, h : h + 1]
            soft = jnp.maximum(pre, 0.0) + jnp.log1p(jnp.exp(-jnp.abs(pre)))
            rate = -jnp.exp(lrate[0:1, h : h + 1])
            decays.append(rate * soft)
            slopes.append(rate * sigmoid(pre))
        cums = dot_full(ltri, pair_of(decays))
        for h in range(HEADS):
            z = conv_sum(proj[at, qc(h)], taps_q[:, DK * h : DK * (h + 1)])
            zsum[at, qc(h)] = z
            c = z * sigmoid(z)
            rq = lax.rsqrt(jnp.sum(c * c, axis=-1, keepdims=True) + 1e-06)
            qkv[at, qc(h)] = c * (rq * SCALE)
            z = conv_sum(proj[at, kc(h)], taps_k[:, DK * h : DK * (h + 1)])
            zsum[at, kc(h)] = z
            c = z * sigmoid(z)
            rk = lax.rsqrt(jnp.sum(c * c, axis=-1, keepdims=True) + 1e-06)
            qkv[at, kc(h)] = c * rk
            z = conv_sum(proj[at, vc(h)], taps_v[:, hv(h)])
            zsum[at, vc(h)] = z
            qkv[at, vc(h)] = z * sigmoid(z)
            i = 2 * s + h
            cols[0, i] = jnp.broadcast_to(betas[h], (LEN, LEN))
            cols[1, i] = jnp.broadcast_to(decays[h], (LEN, LEN))
            cols[2, i] = jnp.broadcast_to(slopes[h], (LEN, LEN))
            cols[3, i] = jnp.broadcast_to(rq, (LEN, LEN))
            cols[4, i] = jnp.broadcast_to(rk, (LEN, LEN))
        systems = []
        for h in range(HEADS):
            i = 2 * s + h
            cum = jnp.broadcast_to(cums[:, h : h + 1], (LEN, LEN))
            gaps = cum - cum.T
            decay = jnp.where(within, jnp.exp(jnp.where(within, gaps, 0.0)), 0.0)
            dmat[i] = decay
            kn = qkv[at, kc(h)]
            e = jnp.where(strict, dot_nt(kn, kn) * decay, 0.0)
            emat[i] = e
            systems.append(cols[0, i] * e)
            amat[i] = dot_nt(qkv[at, qc(h)], kn) * decay
        return systems

    def mixer_outputs(s, systems):
        at = seq(s)
        for h, inverse in enumerate(unit_inverses(systems)):
            tinv[2 * s + h] = inverse.astype(BF16)
        for h in range(HEADS):
            i = 2 * s + h
            w = qkv[at, vc(h)] * cols[0, i][:, 0:1]
            umat[i] = dot(tinv[i], w).astype(BF16)
        for h in range(HEADS):
            i = 2 * s + h
            o = dot(amat[i], umat[i])
            ro = lax.rsqrt(jnp.mean(o * o, axis=-1, keepdims=True) + 1e-05)
            cols[5, i] = jnp.broadcast_to(ro, (LEN, LEN))
            on = o * ro
            onorm[at, hv(h)] = on
            gp = gpre[at, hv(h)]
            mix[at, hv(h)] = (on * ogains[:, hv(h)] * (gp * sigmoid(gp))).astype(BF16)
        put_part(0, s, dot(mix[at], wo[...]))

    def take_middle(s):
        swaps[0][s].wait_recv()
        h = xrow[piece(s)] + chip_total(0, s)
        hrow[piece(s)] = h
        gbuf[1, s, core] = normed(h, gain2)
        middles[s].start()

    def ffn_inputs(s):
        middles[s].wait_recv()
        spread(1, s, a2)
        source = a2[seq(s)]
        upg[seq(s)] = dot_nt(source, wfg[...])
        upu[seq(s)] = dot_nt(source, wfu[...])

    def ffn_outputs(s):
        at = seq(s)
        ug = upg[at]
        s_act = (ug * sigmoid(ug) * upu[at]).astype(BF16)
        act[at, FF:FPAD] = jnp.zeros((LEN, FPAD - FF), BF16)
        act[at, 0:FF] = s_act
        put_part(1, s, dot(s_act, wfd[...]))
        firsts[1][s].start()

    def ffn_output_sum(s):
        firsts[1][s].wait_recv()
        h = jnp.where(hi == 0, hrow[piece(s)], 0.0)
        fwd[1, s] = (pair_total(1, s) + h).astype(BF16)

    def ffn_back(s):
        at = seq(s)
        ds = dact[at]
        ug = upg[at]
        uu = upu[at]
        sg = sigmoid(ug)
        dug = (ds * uu * (sg * (1.0 + ug * (1.0 - sg)))).astype(BF16)
        duu = (ds * (ug * sg)).astype(BF16)
        put_part(2, s, dot(dug, wfg[...]) + dot(duu, wfu[...]))
        firsts[2][s].start()
        dgu[at, 0:FF] = dug
        dgu[at, FF:PAIR] = duu

    def take_gradient(s):
        swaps[2][s].wait_recv()
        dz, dgain = rms_back(hrow[piece(s)], gain2, chip_total(2, s))
        dh = dyo[mine(s)].astype(F32) + dz
        drow[piece(s)] = dh
        dg2s[s] = dgain
        gbuf[3, s, core] = dh.astype(BF16)
        backs[s].start()

    def mixer_back(s):
        at = seq(s)
        backs[s].wait_recv()
        spread(3, s, dho)
        dmix = dot_nt(dho[at], wo[...])
        dos = []
        for h in range(HEADS):
            i = 2 * s + h
            dm = dmix[:, hv(h)]
            gp = gpre[at, hv(h)]
            sg = sigmoid(gp)
            on = onorm[at, hv(h)]
            og = ogains[:, hv(h)]
            dgate = dm * on
            dpr[at, PG + DV * h : PG + DV * (h + 1)] = (
                dgate * og * (sg * (1.0 + gp * (1.0 - sg)))
            ).astype(BF16)
            silu_g = gp * sg
            small[6:7, hv(h)] += jnp.sum(dgate * silu_g, axis=0, keepdims=True)
            don = dm * silu_g * og
            ro = cols[5, i][:, 0:1]
            do = ro * (don - on * jnp.mean(don * on, axis=-1, keepdims=True))
            dos.append(do.astype(BF16))
        index = [2 * s + h for h in range(HEADS)]
        das = [dot_nt(do, umat[i]) for i, do in zip(index, dos)]
        dus = [dot(amat[i].T, do) for i, do in zip(index, dos)]
        dws = [dot(tinv[i].astype(F32).T, du) for i, du in zip(index, dus)]
        dms = [jnp.where(strict, -dot_nt(dw, umat[i]), 0.0) for i, dw in zip(index, dws)]
        return das, dws, dms

    def conv_back(dz, at_rows, at_cols, taps, place_in_small):
        pre = proj[at_rows, at_cols]
        total = dz * taps[3:4]
        for j in range(3):
            total = total + shift_up(dz, 3 - j) * taps[j : j + 1]
        for j in range(4):
            small[2 + j : 3 + j, place_in_small] += jnp.sum(
                dz * shift_down(pre, 3 - j), axis=0, keepdims=True
            )
        dpr[at_rows, at_cols] = total.astype(BF16)

    def mixer_inputs_back(s, kept):
        das, dws, dms = kept
        at = seq(s)
        dbetas, dcs, dqs, dks = [], [], [], []
        for h in range(HEADS):
            i = 2 * s + h
            beta = cols[0, i]
            e = emat[i]
            decay = dmat[i]
            de = dms[h] * e
            dbetas.append(
                jnp.sum(dws[h] * qkv[at, vc(h)], axis=-1, keepdims=True)
                + jnp.sum(de, axis=-1, keepdims=True)
            )
            dgap = das[h] * amat[i] + de * beta
            dcs.append(jnp.sum(dgap - dgap.T, axis=-1, keepdims=True))
            dqk = das[h] * decay
            dkk = dms[h] * beta * decay
            kn = qkv[at, kc(h)]
            qn = qkv[at, qc(h)]
            dqs.append(dot(dqk, kn))
            dks.append(dot(dqk.T, qn) + dot(dkk + dkk.T, kn))
        dgs = dot_full(utri, pair_of(dcs))
        for h in range(HEADS):
            i = 2 * s + h
            qn = qkv[at, qc(h)]
            dq = dqs[h]
            dc = (cols[3, i] * SCALE) * (
                dq - qn * (jnp.sum(qn * dq, axis=-1, keepdims=True) * (1.0 / (SCALE * SCALE)))
            )
            dz = dc * silu_slope(zsum[at, qc(h)])
            conv_back(dz, at, qc(h), taps_q[:, DK * h : DK * (h + 1)], qc(h))
            kn = qkv[at, kc(h)]
            dk = dks[h]
            dc = cols[4, i] * (dk - kn * jnp.sum(kn * dk, axis=-1, keepdims=True))
            dz = dc * silu_slope(zsum[at, kc(h)])
            conv_back(dz, at, kc(h), taps_k[:, DK * h : DK * (h + 1)], kc(h))
            dv = dws[h] * cols[0, i][:, 0:1]
            dz = dv * silu_slope(zsum[at, vc(h)])
            conv_back(dz, at, vc(h), taps_v[:, hv(h)], vc(h))
        scal = jnp.zeros((1, LEN), F32)
        block = jnp.zeros((LEN, LEN), F32)
        for h in range(HEADS):
            i = 2 * s + h
            beta = cols[0, i]
            dg = jnp.broadcast_to(dgs[:, h : h + 1], (LEN, LEN))
            dpb = dbetas[h] * beta * (1.0 - beta)
            dpa = dg * cols[2, i]
            block = jnp.where(lane == h, dpb, block)
            block = jnp.where(lane == 2 + h, dpa, block)
            scal = scal + jnp.where(
                lane_row == h, jnp.sum(dg * cols[1, i], axis=0, keepdims=True), 0.0
            )
            scal = scal + jnp.where(lane_row == 2 + h, jnp.sum(dpa, axis=0, keepdims=True), 0.0)
        dpr[at, PB:PEND] = block.astype(BF16)
        small[6:7, 512:640] += scal

    def layer_back(s):
        at = seq(s)
        value = dot_nt(dpr[at, PQ:PK], wq[...])
        value = value + dot_nt(dpr[at, PK:PV], wk[...])
        value = value + dot_nt(dpr[at, PV:PG], wv[...])
        value = value + dot_nt(dpr[at, PG:PB], wgo[...])
        value = value + dot(dpr[at, PB:PEND][:, 0:8], wba)
        put_part(3, s, value)
        firsts[3][s].start()

    def layer_back_sum(s):
        firsts[3][s].wait_recv()
        dz, dgain = rms_back(xrow[piece(s)], gain1, pair_total(3, s))
        dg1s[s] = dgain
        fwd[3, s] = (dz + jnp.where(hi == 0, drow[piece(s)], 0.0)).astype(BF16)

    small[...] = jnp.zeros_like(small)

    @pl.when(section == 0)
    def _():
        for c in range(4):
            at = slice(ROWS * c, ROWS * (c + 1))
            a1[at] = normed(inp[at].astype(F32), gain1)
        for s in seqs:
            xrow[piece(s)] = inp[mine(s)].astype(F32)

    @pl.when(section == 1)
    def _():
        dyo[...] = cot[...]
        turned(dyo, dyt)
        loads[7].wait()
        dact[...] = dot_nt(cot[...], wfd[...])
        all_entered()

    def take_input(s, value):
        x = value.astype(F32)
        xrow[piece(s)] = x
        return normed(x, gain1)

    for load in loads[:5]:
        load.wait()
    for s in seqs:
        @pl.when(section == 1)
        def _():
            hop_receive(0, 0, s, take_input, a1)

        systems = mixer_systems(s)
        if s == 1:
            swap(0, 0)
        mixer_outputs(s, systems)
        if s == 0:
            pl.when(section == 0)(all_entered)
        firsts[0][s].start()
    swap(0, 1)

    for load in loads[5:7]:
        load.wait()
    pl.when(section == 0)(loads[7].wait)
    take_middle(0)
    ffn_inputs(0)

    @pl.when(section == 0)
    def _():
        ffn_outputs(0)

    @pl.when(section == 1)
    def _():
        ffn_back(0)

    take_middle(1)

    @pl.when(section == 0)
    def _():
        ffn_output_sum(0)
        started(hop_send(1, 0, 0))

    @pl.when(section == 1)
    def _():
        swap(2, 0)

    ffn_inputs(1)

    def take_cotangent(s, value):
        return value

    @pl.when(section == 0)
    def _():
        ffn_outputs(1)
        ffn_output_sum(1)
        started(hop_send(1, 0, 1))
        turned(a1, a1t)
        turned(a2, a2t)
        for s in seqs:
            sent(hop_send(1, 0, s))
        started(swaps[1])
        for s in seqs:
            hop_receive(1, 2, s, take_cotangent, dyo)
            dact[seq(s)] = dot_nt(dyo[seq(s)], wfd[...])
            ffn_back(s)
            swap(2, s)
        turned(dyo, dyt)
        grads.begin(FFN)

    @pl.when(section == 1)
    def _():
        ffn_back(1)
        swap(2, 1)

    take_gradient(0)
    kept = mixer_back(0)
    take_gradient(1)
    mixer_inputs_back(0, kept)
    layer_back(0)
    kept = mixer_back(1)
    layer_back_sum(0)

    @pl.when(section == 0)
    def _():
        grads.relay(FFN)
        turned(dho, dht)
        grads.begin(GATE)

    @pl.when(section == 1)
    def _():
        started(hop_send(3, 1, 0))

    mixer_inputs_back(1, kept)

    @pl.when(section == 0)
    def _():
        grads.begin(MIX)

    layer_back(1)
    layer_back_sum(1)

    @pl.when(section == 1)
    def _():
        started(hop_send(3, 1, 1))
        for s in seqs:
            ffn_outputs(s)
        turned(a2, a2t)
        grads.begin(FFN)
        for s in seqs:
            ffn_output_sum(s)
        turned(a1, a1t)
        turned(dho, dht)
        grads.begin(GATE)
        grads.relay(FFN)
        grads.begin(MIX)
        for s in seqs:
            sent(hop_send(3, 1, s))
        started(swaps[1])

    started(swaps[3])
    gains[0, 0] = dg1s[0] + dg1s[1]
    gains[0, 1] = jnp.where(hi == 0, dg2s[0] + dg2s[1], 0.0)
    sums = [
        remote(
            gains.at[0], gains.at[step], ga_s.at[step - 1], ga_r.at[step - 1],
            {"tensor": (t + step) % 4},
        )
        for step in range(1, 4)
    ]
    started(sums)
    for s in seqs:
        swaps[1][s].wait_recv()
        gbuf[4, s, core] = chip_total(1, s).astype(BF16)
        hiddens[s].start()
    grads.relay(GATE)
    grads.merge(FFN)
    received(sums)
    small[0:1] = (gains[0, 0] + gains[2, 0]) + (gains[1, 0] + gains[3, 0])
    small[1:2] = (gains[0, 1] + gains[2, 1]) + (gains[1, 1] + gains[3, 1])
    grads.small_start(small)
    for s in seqs:
        swaps[3][s].wait_recv()
        gbuf[5, s, core] = chip_total(3, s).astype(BF16)
        inners[s].start()
    grads.relay(MIX)
    grads.merge(GATE)
    grads.relay_second(FFN)
    for s in seqs:
        hiddens[s].wait_recv()
        spread(4, s, hid)
        inners[s].wait_recv()
        spread(5, s, ing)
    grads.small_relay()
    grads.merge(MIX)
    grads.relay_second(GATE)
    grads.ffn_finish()
    grads.small_finish()
    grads.relay_second(MIX)
    grads.gate_finish()
    grads.mix_finish()
    for ph in range(4):
        sent(firsts[ph] + swaps[ph])
    sent(sums + middles + backs + hiddens + inners)
    grads.sent()


def run_layer(args):
    tokens = 2 * LEN
    results = [((tokens, 1024), BF16)] * 2 + [
        (shape, F32)
        for shape in (
            (ROWS, 256), (ROWS, 256), (ROWS, 512), (2, ROWS), (2, ROWS), (ROWS, 512),
            (ROWS, 512), (ROWS, 704), (ROWS, 704), (ROWS, 704), (8, 1024),
        )
    ]
    rows = (2, ROWS, 1024)
    weights = args[12:]
    buffers = [pltpu.VMEM(w.shape, w.dtype) for w in weights] + [pltpu.SemaphoreType.DMA((8,))] + [
        pltpu.VMEM((tokens, n), BF16) for n in (1024, PEND, 1024, PAIR, 1024, 512, 1024, FPAD)
    ] + [pltpu.VMEM((8, 1024), F32)] + [pltpu.VMEM((4, 4, ROWS, 256), BF16)] * 4 + [
        pltpu.VMEM((4, 2) + rows, BF16),
        pltpu.VMEM((4,) + rows, BF16),
        pltpu.VMEM((4,) + rows, BF16),
        pltpu.VMEM((4,) + rows, BF16),
        pltpu.VMEM((2, 2) + rows, BF16),
        pltpu.VMEM((6, 2) + rows, BF16),
        pltpu.VMEM((LEN, 1024), F32),
        pltpu.VMEM((LEN, 1024), F32),
        pltpu.VMEM((LEN, 1024), F32),
        pltpu.VMEM((tokens, 1024), F32),
        pltpu.VMEM((tokens, 1024), F32),
        pltpu.VMEM((tokens, 1024), F32),
        pltpu.VMEM((tokens, 512), F32),
        pltpu.VMEM((tokens, 512), F32),
        pltpu.VMEM((tokens, 704), F32),
        pltpu.VMEM((tokens, 704), F32),
        pltpu.VMEM((tokens, 704), F32),
        pltpu.VMEM((4, LEN, LEN), BF16),
        pltpu.VMEM((4, LEN, LEN), F32),
        pltpu.VMEM((4, LEN, LEN), F32),
        pltpu.VMEM((4, LEN, LEN), F32),
        pltpu.VMEM((4, LEN, DV), BF16),
        pltpu.VMEM((6, 4, LEN, LEN), F32),
        pltpu.VMEM((4, 2, 1, 1024), F32),
        pltpu.VMEM((2, 1, 1024), F32),
        pltpu.VMEM((2, 1, 1024), F32),
    ]
    sems = [
        pltpu.SemaphoreType.DMA((4, 2)), pltpu.SemaphoreType.DMA((4, 2)),
        pltpu.SemaphoreType.DMA((4, 2)), pltpu.SemaphoreType.DMA((4, 2)),
        pltpu.SemaphoreType.DMA((6, 2)), pltpu.SemaphoreType.DMA((6, 2)),
        pltpu.SemaphoreType.DMA((2, 2, 2)), pltpu.SemaphoreType.DMA((2, 2, 2)),
        pltpu.SemaphoreType.DMA((3,)), pltpu.SemaphoreType.DMA((3,)),
    ]
    return pl.pallas_call(
        layer_kernel,
        out_shape=[jax.ShapeDtypeStruct(s, d) for s, d in results],
        in_specs=[pl.BlockSpec(memory_space=pltpu.VMEM)] * 12
        + [pl.BlockSpec(memory_space=pl.ANY)] * len(weights),
        out_specs=[pl.BlockSpec(memory_space=pltpu.VMEM)] * len(results),
        scratch_shapes=buffers + sems + sum_scratch(),
        compiler_params=pltpu.CompilerParams(
            collective_id=0, has_side_effects=True, vmem_limit_bytes=61 * 1024 * 1024
        ),
        name="layer",
    )(*args)


def result_kernel(*refs):
    hid, ing, gq, gk, gv, gb, gd, ggo, gout, gfg, gfu, gfd, sums = refs[:13]
    outs = refs[13:]
    dg1, dcq, dck, dcv, dlr, dsb, dog, dg2 = outs[12:]
    for source, out in zip((hid, ing, gq, gk, gv, gb, gd, ggo, gout, gfg, gfu, gfd), outs):
        out[...] = source[...]
    dg1[...] = sums[0:1]
    dg2[...] = sums[1:2]
    dcq[...] = sums[2:6, 0:256]
    dck[...] = sums[2:6, 256:512]
    dcv[...] = sums[2:6, 512:1024]
    dog[...] = sums[6:7, 0:512]
    dlr[...] = sums[6:7, 512:514]
    dsb[...] = sums[6:7, 514:516]


def run_results(args):
    results = [(v.shape, v.dtype) for v in args[:12]] + [
        (shape, F32)
        for shape in (
            (1, 1024), (4, 256), (4, 256), (4, 512), (1, 2), (1, 2), (1, 512), (1, 1024)
        )
    ]
    return pl.pallas_call(
        result_kernel,
        out_shape=[jax.ShapeDtypeStruct(s, d) for s, d in results],
        in_specs=[pl.BlockSpec(memory_space=pltpu.VMEM)] * len(args),
        out_specs=[pl.BlockSpec(memory_space=pltpu.VMEM)] * len(results),
        compiler_params=pltpu.CompilerParams(vmem_limit_bytes=60 * 1024 * 1024),
        name="results",
    )(*args)


def per_device(
    inputs, cotangent, norm_gain1, w_query, w_key, w_value, conv_query, conv_key, conv_value,
    w_beta, w_decay, log_rate, step_bias, out_gain, w_gate_out, w_out, norm_gain2,
    w_ffn_gate, w_ffn_up, w_ffn_down,
):
    tokens = 2 * LEN
    width = inputs.shape[-1]
    out = run_layer((
        inputs.reshape(tokens, width), cotangent.reshape(tokens, width),
        norm_gain1, conv_query[0], conv_key[0], conv_value[0], w_beta[0].T, w_decay[0].T,
        log_rate, step_bias, out_gain, norm_gain2,
        w_query[0], w_key[0], w_value[0], w_gate_out[0], w_out[0],
        w_ffn_gate[0].T, w_ffn_up[0].T, w_ffn_down[0],
    ))
    (
        hidden, input_grad, gq, gk, gv, gb, gd, ggo, gout, gfg, gfu, gfd,
        dg1, dcq, dck, dcv, dlr, dsb, dog, dg2,
    ) = run_results(tuple(out))
    shape = (1,) + inputs.shape
    return (
        hidden.reshape(shape), input_grad.reshape(shape), dg1, gq[None], gk[None], gv[None],
        dcq[None], dck[None], dcv[None], gb.T[None], gd.T[None], dlr, dsb, dog,
        ggo[None], gout.T[None], dg2, gfg[None], gfu[None], gfd.T[None],
    )


def solution(mesh):
    three = P("section", None, "tensor")
    in_specs = (
        P(None, "dp", None, None), P(None, "dp", None, None), P("section", None),
        three, three, three, three, three, three, three, three,
        P("section", "tensor"), P("section", "tensor"), P("section", "tensor"),
        three, P("section", "tensor", None), P("section", None),
        three, three, P("section", "tensor", None),
    )
    spread = P("section", "dp", "tensor")
    out_specs = (
        P("section", None, "dp", None, None), P("section", None, "dp", None, None),
        P("section", None), spread, spread, spread, three, three, three, spread, spread,
        P("section", "tensor"), P("section", "tensor"), P("section", "tensor"),
        spread, P("section", "tensor", "dp"), P("section", None),
        spread, spread, P("section", "tensor", "dp"),
    )
    return jax.shard_map(
        per_device, mesh=mesh, in_specs=in_specs, out_specs=out_specs, check_vma=False
    )
```

```python
import jax
import jax.numpy as jnp
from jax import lax
from jax.experimental import pallas as pl
from jax.experimental.pallas import tpu as pltpu
from jax.sharding import PartitionSpec as P

F32 = jnp.float32
BF16 = jnp.bfloat16
MESH = pl.DeviceIdType.MESH
LEN = 128
ROWS = 64
HEADS = 2
DK = 128
DV = 256
SCALE = DK**-0.5
PQ, PK, PV, PG, PB, PEND = 0, 256, 512, 1024, 1536, 1664
FPAD = 768
FF = 704
PAIR = 2 * FF
NF = 1152
NG = PAIR - NF + FPAD
NO = 512
NV = 512 + PEND - PB


def dot(left, right):
    return jnp.dot(left.astype(BF16), right.astype(BF16), preferred_element_type=F32)


def dot_nt(left, right):
    return lax.dot_general(
        left.astype(BF16),
        right.astype(BF16),
        (((1,), (1,)), ((), ())),
        preferred_element_type=F32,
    )


def dot_full(left, right):
    return jnp.dot(left, right, precision=lax.Precision.HIGHEST, preferred_element_type=F32)


def sigmoid(v):
    return 1.0 / (1.0 + jnp.exp(-v))


def rows_of(shape):
    return lax.broadcasted_iota(jnp.int32, shape, 0)


def shift_down(v, steps):
    if steps == 0:
        return v
    return jnp.where(rows_of(v.shape) >= steps, pltpu.roll(v, steps, 0), 0.0)


def shift_up(v, steps):
    if steps == 0:
        return v
    count = v.shape[0]
    return jnp.where(rows_of(v.shape) < count - steps, pltpu.roll(v, count - steps, 0), 0.0)


def conv_sum(v, taps):
    total = v * taps[3:4]
    for j in range(3):
        total = total + shift_down(v, 3 - j) * taps[j : j + 1]
    return total


def silu_slope(z):
    s = sigmoid(z)
    return s * (1.0 + z * (1.0 - s))


def unit_inverses(systems):
    row = lax.broadcasted_iota(jnp.int32, (LEN, LEN), 0)
    col = lax.broadcasted_iota(jnp.int32, (LEN, LEN), 1)
    eye = jnp.where(row == col, 1.0, 0.0)

    def band(level):
        same = (row >> (level + 1)) == (col >> (level + 1))
        return same & (((row >> level) & 1) == 1) & (((col >> level) & 1) == 0)

    first = band(0)
    inverses = [eye - jnp.where(first, m, 0.0) for m in systems]
    for level in range(1, 7):
        at = band(level)
        halves = [dot(t, jnp.where(at, m, 0.0)) for t, m in zip(inverses, systems)]
        inverses = [t - dot(x, t) for t, x in zip(inverses, halves)]
    return inverses


def rms_back(z, gain, dn):
    inv = lax.rsqrt(jnp.mean(z * z, axis=-1, keepdims=True) + 1e-06)
    hat = z * inv
    weighted = dn * gain
    dz = (weighted - hat * jnp.mean(weighted * hat, axis=-1, keepdims=True)) * inv
    return dz, jnp.sum(dn * hat, axis=0, keepdims=True)


def torus_steps(place):
    z = place // 4
    x = place % 4
    along_x = [{"dp": z * 4 + (x + step) % 4} for step in range(1, 4)]
    along_z = [{"dp": ((z + step) % 4) * 4 + x} for step in range(1, 4)]
    return along_x + along_z


def turned(source, out):
    for rows in range(4):
        flat = source[:, 256 * rows : 256 * (rows + 1)].T
        for c in range(4):
            out[rows, c] = flat[ROWS * c : ROWS * (c + 1)]


def add_into(ref, more):
    if len(more.shape) == 3:
        @pl.loop(0, more.shape[0])
        def _(c):
            ref[c] = (ref[c].astype(F32) + more[c].astype(F32)).astype(BF16)
    else:
        ref[...] = (ref[...].astype(F32) + more[...].astype(F32)).astype(BF16)


class Ring:
    def __init__(self, remote, g, me, devices, bufs, send, recv, half):
        one_p, one_m, two_p, two_m = bufs
        after, _, before = devices
        self.g, self.me, self.bufs = g, me, bufs
        self.right = right = (me + 1) % 4
        self.left = left = (me + 3) % 4
        self.far = far = (me + 2) % 4
        lo, up = pl.ds(0, half), pl.ds(half, half)
        self.lo, self.up = lo, up
        self.p1 = remote(g.at[far, lo], one_p, send.at[0], recv.at[0], after)
        self.m1 = remote(g.at[far, up], one_m, send.at[1], recv.at[1], before)
        self.p2 = remote(g.at[right, up], two_p.at[up], send.at[2], recv.at[2], after)
        self.m2 = remote(g.at[left, lo], two_m.at[lo], send.at[3], recv.at[3], before)
        self.p3 = remote(g.at[right, lo], two_p.at[lo], send.at[4], recv.at[4], after)
        self.m3 = remote(g.at[left, up], two_m.at[up], send.at[5], recv.at[5], before)
        self.steps = ((far, (self.p1, self.m1)), (right, (self.p2,)), (left, (self.m2,)))

    def start(self):
        for _, copies in self.steps:
            for copy in copies:
                copy.start()

    def relay(self):
        one_p, one_m, _, _ = self.bufs
        self.p1.wait_recv()
        add_into(self.g.at[self.right, self.lo], one_p)
        self.p3.start()
        self.m1.wait_recv()
        add_into(self.g.at[self.left, self.up], one_m)
        self.m3.start()

    def arrive(self):
        for copy in (self.p2, self.m2, self.p3, self.m3):
            copy.wait_recv()

    def sent(self):
        for copy in (self.p1, self.m1, self.p2, self.m2, self.p3, self.m3):
            copy.wait_send()

    def merge(self, out):
        _, _, two_p, two_m = self.bufs

        @pl.loop(0, 4)
        def _(c):
            out[c] = (
                self.g[self.me, c].astype(F32) + two_p[c].astype(F32) + two_m[c].astype(F32)
            ).astype(BF16)

    def total(self, start, size):
        _, _, two_p, two_m = self.bufs
        at = slice(start, start + size)
        return (
            self.g[self.me, :, at].astype(F32)
            + two_p[:, at].astype(F32)
            + two_m[:, at].astype(F32)
        )


FFN, GATE, MIX = (0, 1), (2, 3), (4, 5)
WIDTHS = (NF, NG, NO, NO, PV, NV)


def sum_scratch():
    scratch = []
    for n in WIDTHS:
        scratch.append(pltpu.VMEM((4, 4, ROWS, n), BF16))
        scratch += [pltpu.VMEM((2, ROWS, n), BF16)] * 2 + [pltpu.VMEM((4, ROWS, n), BF16)] * 3
        scratch += [pltpu.VMEM((ROWS // 2, n), BF16)] * 2 + [pltpu.VMEM((ROWS, n), BF16)] * 2
    scratch += [pltpu.VMEM((4, 8, 1024), F32)] * 2
    scratch += [pltpu.SemaphoreType.DMA((12, 6))] * 2 + [pltpu.SemaphoreType.DMA((6,))] * 2
    return scratch


class Sums:
    def __init__(self, place, remote, data, outs, refs):
        self.data, self.outs = data, outs
        z, x = place // 4, place % 4
        steps = torus_steps(place)
        ways = ((x, steps[:3]), (z, steps[3:]))
        self.sx, self.sz, send, recv, ssend, srecv = refs[-6:]
        self.first, self.second, self.half = [], [], []
        for k in range(6):
            g, one_p, one_m, two_p, two_m, h, a, b, c, d = refs[10 * k : 10 * k + 10]
            me, way = ways[k % 2]
            self.first.append(
                Ring(remote, g, me, way, (one_p, one_m, two_p, two_m), send.at[k], recv.at[k], 2)
            )
            me, way = ways[1 - k % 2]
            self.second.append(
                Ring(remote, h, me, way, (a, b, c, d), send.at[6 + k], recv.at[6 + k], ROWS // 2)
            )
        self.small_x = [
            remote(self.sx.at[0], self.sx.at[i + 1], ssend.at[i], srecv.at[i], steps[i])
            for i in range(3)
        ]
        self.small_z = [
            remote(self.sz.at[0], self.sz.at[i + 1], ssend.at[3 + i], srecv.at[3 + i], steps[3 + i])
            for i in range(3)
        ]

    def chunk(self, k, c):
        data = self.data
        out = self.first[k].g.at[c]

        def outer(left, right, first, width, offset):
            rows = left[:, c] if k % 2 == 0 else left[c]
            flat = rows.reshape(4 * ROWS, 2 * LEN)
            for start in range(0, width, 256):
                size = min(256, width - start)
                value = jnp.dot(
                    flat, right[:, first + start : first + start + size],
                    preferred_element_type=F32,
                ).astype(BF16)
                for i in range(4):
                    out[i, :, offset + start : offset + start + size] = value[
                        ROWS * i : ROWS * (i + 1)
                    ]

        if k == 0:
            outer(data["a2"], data["pair"], 0, NF, 0)
        elif k == 1:
            outer(data["a2"], data["pair"], NF, PAIR - NF, 0)
            outer(data["dy"], data["act"], 0, FPAD, PAIR - NF)
        elif k == 2:
            outer(data["dh"], data["mix"], 0, NO, 0)
        elif k == 3:
            outer(data["a1"], data["proj"], PG, NO, 0)
        elif k == 4:
            outer(data["a1"], data["proj"], PQ, PV, 0)
        else:
            outer(data["a1"], data["proj"], PV, PG - PV, 0)
            outer(data["a1"], data["proj"], PB, PEND - PB, PG - PV)

    def begin(self, groups, after_first=None):
        for step in range(3):
            for k in groups:
                at, copies = self.first[k].steps[step]
                self.chunk(k, at)
                for copy in copies:
                    copy.start()
            if step == 0 and after_first is not None:
                after_first()
        for k in groups:
            self.chunk(k, self.first[k].me)

    def merge(self, groups):
        for k in groups:
            self.first[k].arrive()
            self.first[k].merge(self.second[k].g)
            self.second[k].start()

    def relay(self, groups):
        for k in groups:
            self.first[k].relay()

    def relay_second(self, groups):
        for k in groups:
            self.second[k].relay()

    def ffn_finish(self):
        one, two, outs = self.second[0], self.second[1], self.outs
        one.arrive()
        outs["fg"][...] = one.total(0, FPAD)[:, 0:FF]
        outs["fu"][:, 0 : NF - FF] = one.total(640, NF - 640)[:, FF - 640 :]
        two.arrive()
        outs["fu"][:, NF - FF : FF] = two.total(0, PAIR - NF)
        outs["fd"][...] = two.total(PAIR - NF, FPAD)[:, 0:FF]

    def gate_finish(self):
        one, two, outs = self.second[2], self.second[3], self.outs
        one.arrive()
        outs["out"][...] = one.total(0, NO)
        two.arrive()
        outs["go"][...] = two.total(0, NO)

    def mix_finish(self):
        one, two, outs = self.second[4], self.second[5], self.outs
        one.arrive()
        outs["q"][...] = one.total(0, 256)
        outs["k"][...] = one.total(256, 256)
        two.arrive()
        outs["v"][...] = two.total(0, 512)
        both = two.total(512, PEND - PB).T
        outs["b"][...] = both[0:2]
        outs["d"][...] = both[2:4]

    def small_start(self, small):
        self.sx[0] = small[...]
        for copy in self.small_x:
            copy.start()

    def small_relay(self):
        sx = self.sx
        for copy in self.small_x:
            copy.wait_recv()
        self.sz[0] = (sx[0] + sx[2]) + (sx[1] + sx[3])
        for copy in self.small_z:
            copy.start()

    def small_finish(self):
        sz = self.sz
        for copy in self.small_z:
            copy.wait_recv()
        self.outs["small"][...] = (sz[0] + sz[2]) + (sz[1] + sz[3])

    def sent(self):
        for ring in self.first + self.second:
            ring.sent()
        for copy in self.small_x + self.small_z:
            copy.wait_send()


def layer_kernel(
    inp, cot, g1, cvq, cvk, cvv, wb, wd, lrate, sbias, ogain, g2,
    hq, hk, hval, hgo, ho, hfg, hfu, hfd,
    hid, ing, gq, gk, gv, gb, gd, ggo, gout, gfg, gfu, gfd, gsmall,
    wq, wk, wv, wgo, wo, wfg, wfu, wfd, w_s,
    a1, dpr, a2, dgu, dho, mix, dyo, act, small, a1t, a2t, dht, dyt,
    part, r1, r2, fwd, hopb, gbuf, xrow, hrow, drow,
    proj, zsum, qkv, gpre, onorm, upg, upu, dact,
    tinv, amat, dmat, emat, umat, cols, gains, dg1s, dg2s,
    rs_s, rs_r, op_s, op_r, ag_s, ag_r, hop_s, hop_r, ga_s, ga_r,
    *sum_refs,
):
    section = lax.axis_index("section")
    t = lax.axis_index("tensor")
    hi = t // 2
    core = t % 2
    sib = hi * 2 + (1 - core)
    opp = (1 - hi) * 2 + core
    other = 1 - section
    seqs = range(2)

    def remote(src, dst, ssem, rsem, device):
        return pltpu.make_async_remote_copy(
            src_ref=src, dst_ref=dst, send_sem=ssem, recv_sem=rsem,
            device_id=device, device_id_type=MESH,
        )

    stored = (hq, hk, hval, hgo, ho, hfg, hfu, hfd)
    held = (wq, wk, wv, wgo, wo, wfg, wfu, wfd)
    loads = [pltpu.make_async_copy(a, b, w_s.at[i]) for i, (a, b) in enumerate(zip(stored, held))]
    for i in (0, 1, 2, 3, 4, 7, 5, 6):
        loads[i].start()

    barrier = pltpu.get_barrier_semaphore()
    for step in range(1, 4):
        pl.semaphore_signal(
            barrier, inc=1, device_id={"tensor": (t + step) % 4}, device_id_type=MESH
        )
    for step in range(4):
        pl.semaphore_signal(
            barrier, inc=1, device_id={"section": other, "tensor": (t + step) % 4},
            device_id_type=MESH,
        )
    place = lax.axis_index("dp")
    links = torus_steps(place)
    for device in links:
        pl.semaphore_signal(barrier, inc=1, device_id=device, device_id_type=MESH)

    def all_entered():
        pl.semaphore_wait(barrier, 7 + len(links))

    grads = Sums(
        place, remote,
        dict(a1=a1t, a2=a2t, dh=dht, dy=dyt, proj=dpr, pair=dgu, mix=mix, act=act),
        dict(q=gq, k=gk, v=gv, b=gb, d=gd, go=ggo, out=gout, fg=gfg, fu=gfu, fd=gfd, small=gsmall),
        sum_refs,
    )

    def pair_sum(ph):
        return [
            remote(part.at[ph, s, 1 - core], r1.at[ph, s], rs_s.at[ph, s], rs_r.at[ph, s],
                   {"tensor": sib})
            for s in seqs
        ]

    def chip_swap(ph):
        return [
            remote(fwd.at[ph, s], r2.at[ph, s], op_s.at[ph, s], op_r.at[ph, s], {"tensor": opp})
            for s in seqs
        ]

    def pair_share(k):
        return [
            remote(gbuf.at[k, s, core], gbuf.at[k, s, core], ag_s.at[k, s], ag_r.at[k, s],
                   {"tensor": sib})
            for s in seqs
        ]

    def hop_send(ph, k, s):
        return [
            remote(fwd.at[ph, s], hopb.at[k, hi, s], hop_s.at[k, y, s], hop_r.at[k, hi, s],
                   {"section": other, "tensor": 2 * y + core})
            for y in range(2)
        ]

    def started(copies):
        for copy in copies:
            copy.start()

    def received(copies):
        for copy in copies:
            copy.wait_recv()

    def sent(copies):
        for copy in copies:
            copy.wait_send()

    def pair_total(ph, s):
        return part[ph, s, core].astype(F32) + r1[ph, s].astype(F32)

    def chip_total(ph, s):
        return fwd[ph, s].astype(F32) + r2[ph, s].astype(F32)

    def swap(ph, s):
        firsts[ph][s].wait_recv()
        fwd[ph, s] = pair_total(ph, s).astype(BF16)
        swaps[ph][s].start()

    def hop_receive(k, share, s, finish, out):
        passes = pair_share(share)[s]
        for y in range(2):
            remote(hopb.at[k, y, s], hopb.at[k, y, s], hop_s.at[k, y, s], hop_r.at[k, y, s],
                   {"section": other, "tensor": t}).wait_recv()
        value = (hopb[k, 0, s].astype(F32) + hopb[k, 1, s].astype(F32)).astype(BF16)
        gbuf[share, s, core] = finish(s, value)
        passes.start()
        passes.wait_recv()
        spread(share, s, out)
        passes.wait_send()

    def put_part(ph, s, value):
        for p in range(2):
            part[ph, s, p] = value[ROWS * p : ROWS * (p + 1)].astype(BF16)

    def spread(k, s, out):
        for p in range(2):
            at = LEN * s + ROWS * p
            out[at : at + ROWS] = gbuf[k, s, p]

    def piece(s):
        return slice(ROWS * s, ROWS * (s + 1))

    def mine(s):
        return pl.ds(pl.multiple_of(core * ROWS + LEN * s, ROWS), ROWS)

    def normed(x, gain):
        inv = lax.rsqrt(jnp.mean(x * x, axis=-1, keepdims=True) + 1e-06)
        return (x * inv * gain).astype(BF16)

    firsts = [pair_sum(ph) for ph in range(4)]
    swaps = [chip_swap(ph) for ph in range(4)]
    middles, backs, hiddens, inners = (pair_share(k) for k in (1, 3, 4, 5))
    row = lax.broadcasted_iota(jnp.int32, (LEN, LEN), 0)
    col = lax.broadcasted_iota(jnp.int32, (LEN, LEN), 1)
    within = row >= col
    strict = row > col
    gain1 = g1[...].astype(F32)
    gain2 = g2[...].astype(F32)
    ogains = ogain[...].astype(F32)
    taps_q = cvq[...].astype(F32)
    taps_k = cvk[...].astype(F32)
    taps_v = cvv[...].astype(F32)

    def seq(s):
        return slice(LEN * s, LEN * (s + 1))

    def qc(h):
        return slice(PQ + DK * h, PQ + DK * (h + 1))

    def kc(h):
        return slice(PK + DK * h, PK + DK * (h + 1))

    def vc(h):
        return slice(PV + DV * h, PV + DV * (h + 1))

    def hv(h):
        return slice(DV * h, DV * (h + 1))

    lane = lax.broadcasted_iota(jnp.int32, (LEN, LEN), 1)
    lane_row = lax.broadcasted_iota(jnp.int32, (1, LEN), 1)
    ltri = jnp.where(within, 1.0, 0.0)
    utri = jnp.where(row <= col, 1.0, 0.0)
    wba = jnp.concatenate(
        [wb[...].astype(F32), wd[...].astype(F32), jnp.zeros((4, 1024), F32)], axis=0
    ).astype(BF16)

    def pair_of(columns):
        packed = jnp.zeros((LEN, LEN), F32)
        for h in range(HEADS):
            packed = jnp.where(lane == h, columns[h], packed)
        return packed

    def mixer_systems(s):
        at = seq(s)
        source = a1[at]
        proj[at, PQ:PK] = dot(source, wq[...])
        proj[at, PK:PV] = dot(source, wk[...])
        proj[at, PV:PG] = dot(source, wv[...])
        pba = dot_nt(source, wba)
        gpre[at] = dot(source, wgo[...])
        betas, decays, slopes = [], [], []
        for h in range(HEADS):
            betas.append(sigmoid(pba[:, h : h + 1]))
            pre = pba[:, 2 + h : 3 + h] + sbias[0:1, h : h + 1]
            soft = jnp.maximum(pre, 0.0) + jnp.log1p(jnp.exp(-jnp.abs(pre)))
            rate = -jnp.exp(lrate[0:1, h : h + 1])
            decays.append(rate * soft)
            slopes.append(rate * sigmoid(pre))
        cums = dot_full(ltri, pair_of(decays))
        for h in range(HEADS):
            z = conv_sum(proj[at, qc(h)], taps_q[:, DK * h : DK * (h + 1)])
            zsum[at, qc(h)] = z
            c = z * sigmoid(z)
            rq = lax.rsqrt(jnp.sum(c * c, axis=-1, keepdims=True) + 1e-06)
            qkv[at, qc(h)] = c * (rq * SCALE)
            z = conv_sum(proj[at, kc(h)], taps_k[:, DK * h : DK * (h + 1)])
            zsum[at, kc(h)] = z
            c = z * sigmoid(z)
            rk = lax.rsqrt(jnp.sum(c * c, axis=-1, keepdims=True) + 1e-06)
            qkv[at, kc(h)] = c * rk
            z = conv_sum(proj[at, vc(h)], taps_v[:, hv(h)])
            zsum[at, vc(h)] = z
            qkv[at, vc(h)] = z * sigmoid(z)
            i = 2 * s + h
            cols[0, i] = jnp.broadcast_to(betas[h], (LEN, LEN))
            cols[1, i] = jnp.broadcast_to(decays[h], (LEN, LEN))
            cols[2, i] = jnp.broadcast_to(slopes[h], (LEN, LEN))
            cols[3, i] = jnp.broadcast_to(rq, (LEN, LEN))
            cols[4, i] = jnp.broadcast_to(rk, (LEN, LEN))
        systems = []
        for h in range(HEADS):
            i = 2 * s + h
            cum = jnp.broadcast_to(cums[:, h : h + 1], (LEN, LEN))
            gaps = cum - cum.T
            decay = jnp.where(within, jnp.exp(jnp.where(within, gaps, 0.0)), 0.0)
            dmat[i] = decay
            kn = qkv[at, kc(h)]
            e = jnp.where(strict, dot_nt(kn, kn) * decay, 0.0)
            emat[i] = e
            systems.append(cols[0, i] * e)
            amat[i] = dot_nt(qkv[at, qc(h)], kn) * decay
        return systems

    def mixer_outputs(s, systems):
        at = seq(s)
        for h, inverse in enumerate(unit_inverses(systems)):
            tinv[2 * s + h] = inverse.astype(BF16)
        for h in range(HEADS):
            i = 2 * s + h
            w = qkv[at, vc(h)] * cols[0, i][:, 0:1]
            umat[i] = dot(tinv[i], w).astype(BF16)
        for h in range(HEADS):
            i = 2 * s + h
            o = dot(amat[i], umat[i])
            ro = lax.rsqrt(jnp.mean(o * o, axis=-1, keepdims=True) + 1e-05)
            cols[5, i] = jnp.broadcast_to(ro, (LEN, LEN))
            on = o * ro
            onorm[at, hv(h)] = on
            gp = gpre[at, hv(h)]
            mix[at, hv(h)] = (on * ogains[:, hv(h)] * (gp * sigmoid(gp))).astype(BF16)
        put_part(0, s, dot(mix[at], wo[...]))

    def take_middle(s):
        swaps[0][s].wait_recv()
        h = xrow[piece(s)] + chip_total(0, s)
        hrow[piece(s)] = h
        gbuf[1, s, core] = normed(h, gain2)
        middles[s].start()

    def ffn_inputs(s):
        middles[s].wait_recv()
        spread(1, s, a2)
        source = a2[seq(s)]
        upg[seq(s)] = dot_nt(source, wfg[...])
        upu[seq(s)] = dot_nt(source, wfu[...])

    def ffn_outputs(s):
        at = seq(s)
        ug = upg[at]
        s_act = (ug * sigmoid(ug) * upu[at]).astype(BF16)
        act[at, FF:FPAD] = jnp.zeros((LEN, FPAD - FF), BF16)
        act[at, 0:FF] = s_act
        put_part(1, s, dot(s_act, wfd[...]))
        firsts[1][s].start()

    def ffn_output_sum(s):
        firsts[1][s].wait_recv()
        h = jnp.where(hi == 0, hrow[piece(s)], 0.0)
        fwd[1, s] = (pair_total(1, s) + h).astype(BF16)

    def ffn_back(s):
        at = seq(s)
        ds = dact[at]
        ug = upg[at]
        uu = upu[at]
        sg = sigmoid(ug)
        dug = (ds * uu * (sg * (1.0 + ug * (1.0 - sg)))).astype(BF16)
        duu = (ds * (ug * sg)).astype(BF16)
        put_part(2, s, dot(dug, wfg[...]) + dot(duu, wfu[...]))
        firsts[2][s].start()
        dgu[at, 0:FF] = dug
        dgu[at, FF:PAIR] = duu

    def take_gradient(s):
        swaps[2][s].wait_recv()
        dz, dgain = rms_back(hrow[piece(s)], gain2, chip_total(2, s))
        dh = dyo[mine(s)].astype(F32) + dz
        drow[piece(s)] = dh
        dg2s[s] = dgain
        gbuf[3, s, core] = dh.astype(BF16)
        backs[s].start()

    def mixer_back(s):
        at = seq(s)
        backs[s].wait_recv()
        spread(3, s, dho)
        dmix = dot_nt(dho[at], wo[...])
        dos = []
        for h in range(HEADS):
            i = 2 * s + h
            dm = dmix[:, hv(h)]
            gp = gpre[at, hv(h)]
            sg = sigmoid(gp)
            on = onorm[at, hv(h)]
            og = ogains[:, hv(h)]
            dgate = dm * on
            dpr[at, PG + DV * h : PG + DV * (h + 1)] = (
                dgate * og * (sg * (1.0 + gp * (1.0 - sg)))
            ).astype(BF16)
            silu_g = gp * sg
            small[6:7, hv(h)] += jnp.sum(dgate * silu_g, axis=0, keepdims=True)
            don = dm * silu_g * og
            ro = cols[5, i][:, 0:1]
            do = ro * (don - on * jnp.mean(don * on, axis=-1, keepdims=True))
            dos.append(do.astype(BF16))
        index = [2 * s + h for h in range(HEADS)]
        das = [dot_nt(do, umat[i]) for i, do in zip(index, dos)]
        dus = [dot(amat[i].T, do) for i, do in zip(index, dos)]
        dws = [dot(tinv[i].astype(F32).T, du) for i, du in zip(index, dus)]
        dms = [jnp.where(strict, -dot_nt(dw, umat[i]), 0.0) for i, dw in zip(index, dws)]
        return das, dws, dms

    def conv_back(dz, at_rows, at_cols, taps, place_in_small):
        pre = proj[at_rows, at_cols]
        total = dz * taps[3:4]
        for j in range(3):
            total = total + shift_up(dz, 3 - j) * taps[j : j + 1]
        for j in range(4):
            small[2 + j : 3 + j, place_in_small] += jnp.sum(
                dz * shift_down(pre, 3 - j), axis=0, keepdims=True
            )
        dpr[at_rows, at_cols] = total.astype(BF16)

    def mixer_inputs_back(s, kept):
        das, dws, dms = kept
        at = seq(s)
        dbetas, dcs, dqs, dks = [], [], [], []
        for h in range(HEADS):
            i = 2 * s + h
            beta = cols[0, i]
            e = emat[i]
            decay = dmat[i]
            de = dms[h] * e
            dbetas.append(
                jnp.sum(dws[h] * qkv[at, vc(h)], axis=-1, keepdims=True)
                + jnp.sum(de, axis=-1, keepdims=True)
            )
            dgap = das[h] * amat[i] + de * beta
            dcs.append(jnp.sum(dgap - dgap.T, axis=-1, keepdims=True))
            dqk = das[h] * decay
            dkk = dms[h] * beta * decay
            kn = qkv[at, kc(h)]
            qn = qkv[at, qc(h)]
            dqs.append(dot(dqk, kn))
            dks.append(dot(dqk.T, qn) + dot(dkk + dkk.T, kn))
        dgs = dot_full(utri, pair_of(dcs))
        for h in range(HEADS):
            i = 2 * s + h
            qn = qkv[at, qc(h)]
            dq = dqs[h]
            dc = (cols[3, i] * SCALE) * (
                dq - qn * (jnp.sum(qn * dq, axis=-1, keepdims=True) * (1.0 / (SCALE * SCALE)))
            )
            dz = dc * silu_slope(zsum[at, qc(h)])
            conv_back(dz, at, qc(h), taps_q[:, DK * h : DK * (h + 1)], qc(h))
            kn = qkv[at, kc(h)]
            dk = dks[h]
            dc = cols[4, i] * (dk - kn * jnp.sum(kn * dk, axis=-1, keepdims=True))
            dz = dc * silu_slope(zsum[at, kc(h)])
            conv_back(dz, at, kc(h), taps_k[:, DK * h : DK * (h + 1)], kc(h))
            dv = dws[h] * cols[0, i][:, 0:1]
            dz = dv * silu_slope(zsum[at, vc(h)])
            conv_back(dz, at, vc(h), taps_v[:, hv(h)], vc(h))
        scal = jnp.zeros((1, LEN), F32)
        block = jnp.zeros((LEN, LEN), F32)
        for h in range(HEADS):
            i = 2 * s + h
            beta = cols[0, i]
            dg = jnp.broadcast_to(dgs[:, h : h + 1], (LEN, LEN))
            dpb = dbetas[h] * beta * (1.0 - beta)
            dpa = dg * cols[2, i]
            block = jnp.where(lane == h, dpb, block)
            block = jnp.where(lane == 2 + h, dpa, block)
            scal = scal + jnp.where(
                lane_row == h, jnp.sum(dg * cols[1, i], axis=0, keepdims=True), 0.0
            )
            scal = scal + jnp.where(lane_row == 2 + h, jnp.sum(dpa, axis=0, keepdims=True), 0.0)
        dpr[at, PB:PEND] = block.astype(BF16)
        small[6:7, 512:640] += scal

    def layer_back(s):
        at = seq(s)
        value = dot_nt(dpr[at, PQ:PK], wq[...])
        value = value + dot_nt(dpr[at, PK:PV], wk[...])
        value = value + dot_nt(dpr[at, PV:PG], wv[...])
        value = value + dot_nt(dpr[at, PG:PB], wgo[...])
        value = value + dot(dpr[at, PB:PEND][:, 0:8], wba)
        put_part(3, s, value)
        firsts[3][s].start()

    def layer_back_sum(s):
        firsts[3][s].wait_recv()
        dz, dgain = rms_back(xrow[piece(s)], gain1, pair_total(3, s))
        dg1s[s] = dgain
        fwd[3, s] = (dz + jnp.where(hi == 0, drow[piece(s)], 0.0)).astype(BF16)

    small[...] = jnp.zeros_like(small)

    @pl.when(section == 0)
    def _():
        for c in range(4):
            at = slice(ROWS * c, ROWS * (c + 1))
            a1[at] = normed(inp[at].astype(F32), gain1)
        for s in seqs:
            xrow[piece(s)] = inp[mine(s)].astype(F32)

    @pl.when(section == 1)
    def _():
        dyo[...] = cot[...]
        turned(dyo, dyt)
        loads[7].wait()
        dact[...] = dot_nt(cot[...], wfd[...])
        all_entered()

    def take_input(s, value):
        x = value.astype(F32)
        xrow[piece(s)] = x
        return normed(x, gain1)

    for load in loads[:5]:
        load.wait()
    for s in seqs:
        @pl.when(section == 1)
        def _():
            hop_receive(0, 0, s, take_input, a1)

        systems = mixer_systems(s)
        if s == 1:
            swap(0, 0)
        mixer_outputs(s, systems)
        if s == 0:
            pl.when(section == 0)(all_entered)
        firsts[0][s].start()
    swap(0, 1)

    for load in loads[5:7]:
        load.wait()
    pl.when(section == 0)(loads[7].wait)
    take_middle(0)
    ffn_inputs(0)

    @pl.when(section == 0)
    def _():
        ffn_outputs(0)

    @pl.when(section == 1)
    def _():
        ffn_back(0)

    take_middle(1)

    @pl.when(section == 0)
    def _():
        ffn_output_sum(0)
        started(hop_send(1, 0, 0))

    @pl.when(section == 1)
    def _():
        swap(2, 0)

    ffn_inputs(1)

    def take_cotangent(s, value):
        return value

    @pl.when(section == 0)
    def _():
        ffn_outputs(1)
        ffn_output_sum(1)
        started(hop_send(1, 0, 1))
        turned(a1, a1t)
        turned(a2, a2t)
        for s in seqs:
            sent(hop_send(1, 0, s))
        started(swaps[1])
        for s in seqs:
            hop_receive(1, 2, s, take_cotangent, dyo)
            dact[seq(s)] = dot_nt(dyo[seq(s)], wfd[...])
            ffn_back(s)
            if s == 0:
                swap(2, 0)
        turned(dyo, dyt)
        grads.begin(FFN, lambda: swap(2, 1))

    @pl.when(section == 1)
    def _():
        ffn_back(1)
        swap(2, 1)

    take_gradient(0)
    kept = mixer_back(0)
    take_gradient(1)
    mixer_inputs_back(0, kept)
    layer_back(0)
    kept = mixer_back(1)
    layer_back_sum(0)

    @pl.when(section == 0)
    def _():
        turned(dho, dht)
        grads.begin(GATE)
        grads.relay(FFN)

    @pl.when(section == 1)
    def _():
        started(hop_send(3, 1, 0))

    mixer_inputs_back(1, kept)

    @pl.when(section == 0)
    def _():
        grads.begin(MIX)

    layer_back(1)
    layer_back_sum(1)

    @pl.when(section == 1)
    def _():
        started(hop_send(3, 1, 1))
        for s in seqs:
            ffn_outputs(s)
        turned(a2, a2t)
        grads.begin(FFN)
        for s in seqs:
            ffn_output_sum(s)
        turned(a1, a1t)
        turned(dho, dht)
        grads.begin(GATE)
        grads.relay(FFN)
        grads.begin(MIX)
        for s in seqs:
            sent(hop_send(3, 1, s))
        started(swaps[1])

    started(swaps[3])
    gains[0, 0] = dg1s[0] + dg1s[1]
    gains[0, 1] = jnp.where(hi == 0, dg2s[0] + dg2s[1], 0.0)
    sums = [
        remote(
            gains.at[0], gains.at[step], ga_s.at[step - 1], ga_r.at[step - 1],
            {"tensor": (t + step) % 4},
        )
        for step in range(1, 4)
    ]
    started(sums)
    for s in seqs:
        swaps[1][s].wait_recv()
        gbuf[4, s, core] = chip_total(1, s).astype(BF16)
        hiddens[s].start()
    grads.relay(GATE)
    grads.merge(FFN)
    received(sums)
    small[0:1] = (gains[0, 0] + gains[2, 0]) + (gains[1, 0] + gains[3, 0])
    small[1:2] = (gains[0, 1] + gains[2, 1]) + (gains[1, 1] + gains[3, 1])
    grads.small_start(small)
    for s in seqs:
        swaps[3][s].wait_recv()
        gbuf[5, s, core] = chip_total(3, s).astype(BF16)
        inners[s].start()
    grads.relay(MIX)
    grads.merge(GATE)
    grads.relay_second(FFN)
    for s in seqs:
        hiddens[s].wait_recv()
        spread(4, s, hid)
        inners[s].wait_recv()
        spread(5, s, ing)
    grads.small_relay()
    grads.merge(MIX)
    grads.relay_second(GATE)
    grads.ffn_finish()
    grads.small_finish()
    grads.relay_second(MIX)
    grads.gate_finish()
    grads.mix_finish()
    for ph in range(4):
        sent(firsts[ph] + swaps[ph])
    sent(sums + middles + backs + hiddens + inners)
    grads.sent()


def run_layer(args):
    tokens = 2 * LEN
    results = [((tokens, 1024), BF16)] * 2 + [
        (shape, F32)
        for shape in (
            (ROWS, 256), (ROWS, 256), (ROWS, 512), (2, ROWS), (2, ROWS), (ROWS, 512),
            (ROWS, 512), (ROWS, 704), (ROWS, 704), (ROWS, 704), (8, 1024),
        )
    ]
    rows = (2, ROWS, 1024)
    weights = args[12:]
    buffers = [pltpu.VMEM(w.shape, w.dtype) for w in weights] + [pltpu.SemaphoreType.DMA((8,))] + [
        pltpu.VMEM((tokens, n), BF16) for n in (1024, PEND, 1024, PAIR, 1024, 512, 1024, FPAD)
    ] + [pltpu.VMEM((8, 1024), F32)] + [pltpu.VMEM((4, 4, ROWS, 256), BF16)] * 4 + [
        pltpu.VMEM((4, 2) + rows, BF16),
        pltpu.VMEM((4,) + rows, BF16),
        pltpu.VMEM((4,) + rows, BF16),
        pltpu.VMEM((4,) + rows, BF16),
        pltpu.VMEM((2, 2) + rows, BF16),
        pltpu.VMEM((6, 2) + rows, BF16),
        pltpu.VMEM((LEN, 1024), F32),
        pltpu.VMEM((LEN, 1024), F32),
        pltpu.VMEM((LEN, 1024), F32),
        pltpu.VMEM((tokens, 1024), F32),
        pltpu.VMEM((tokens, 1024), F32),
        pltpu.VMEM((tokens, 1024), F32),
        pltpu.VMEM((tokens, 512), F32),
        pltpu.VMEM((tokens, 512), F32),
        pltpu.VMEM((tokens, 704), F32),
        pltpu.VMEM((tokens, 704), F32),
        pltpu.VMEM((tokens, 704), F32),
        pltpu.VMEM((4, LEN, LEN), BF16),
        pltpu.VMEM((4, LEN, LEN), F32),
        pltpu.VMEM((4, LEN, LEN), F32),
        pltpu.VMEM((4, LEN, LEN), F32),
        pltpu.VMEM((4, LEN, DV), BF16),
        pltpu.VMEM((6, 4, LEN, LEN), F32),
        pltpu.VMEM((4, 2, 1, 1024), F32),
        pltpu.VMEM((2, 1, 1024), F32),
        pltpu.VMEM((2, 1, 1024), F32),
    ]
    sems = [
        pltpu.SemaphoreType.DMA((4, 2)), pltpu.SemaphoreType.DMA((4, 2)),
        pltpu.SemaphoreType.DMA((4, 2)), pltpu.SemaphoreType.DMA((4, 2)),
        pltpu.SemaphoreType.DMA((6, 2)), pltpu.SemaphoreType.DMA((6, 2)),
        pltpu.SemaphoreType.DMA((2, 2, 2)), pltpu.SemaphoreType.DMA((2, 2, 2)),
        pltpu.SemaphoreType.DMA((3,)), pltpu.SemaphoreType.DMA((3,)),
    ]
    return pl.pallas_call(
        layer_kernel,
        out_shape=[jax.ShapeDtypeStruct(s, d) for s, d in results],
        in_specs=[pl.BlockSpec(memory_space=pltpu.VMEM)] * 12
        + [pl.BlockSpec(memory_space=pl.ANY)] * len(weights),
        out_specs=[pl.BlockSpec(memory_space=pltpu.VMEM)] * len(results),
        scratch_shapes=buffers + sems + sum_scratch(),
        compiler_params=pltpu.CompilerParams(
            collective_id=0, has_side_effects=True, vmem_limit_bytes=61 * 1024 * 1024
        ),
        name="layer",
    )(*args)


def result_kernel(*refs):
    gb, gd, sums = refs[10:13]
    large = refs[13:23]
    ogb, ogd, dg1, dcq, dck, dcv, dlr, dsb, dog, dg2, sems = refs[23:]
    copies = [
        pltpu.make_async_copy(a, b, sems.at[i]) for i, (a, b) in enumerate(zip(refs[:10], large))
    ]
    for copy in copies:
        copy.start()
    ogb[...] = gb[...]
    ogd[...] = gd[...]
    dg1[...] = sums[0:1]
    dg2[...] = sums[1:2]
    dcq[...] = sums[2:6, 0:256]
    dck[...] = sums[2:6, 256:512]
    dcv[...] = sums[2:6, 512:1024]
    dog[...] = sums[6:7, 0:512]
    dlr[...] = sums[6:7, 512:514]
    dsb[...] = sums[6:7, 514:516]
    for copy in copies:
        copy.wait()


def run_results(large, small):
    results = [(v.shape, v.dtype) for v in large + small[:2]] + [
        (shape, F32)
        for shape in (
            (1, 1024), (4, 256), (4, 256), (4, 512), (1, 2), (1, 2), (1, 512), (1, 1024)
        )
    ]
    far = [pl.BlockSpec(memory_space=pl.ANY)] * len(large)
    return pl.pallas_call(
        result_kernel,
        out_shape=[jax.ShapeDtypeStruct(s, d) for s, d in results],
        in_specs=far + [pl.BlockSpec(memory_space=pltpu.VMEM)] * len(small),
        out_specs=far + [pl.BlockSpec(memory_space=pltpu.VMEM)] * (len(results) - len(large)),
        scratch_shapes=[pltpu.SemaphoreType.DMA((len(large),))],
        compiler_params=pltpu.CompilerParams(vmem_limit_bytes=60 * 1024 * 1024),
        name="results",
    )(*large, *small)


def per_device(
    inputs, cotangent, norm_gain1, w_query, w_key, w_value, conv_query, conv_key, conv_value,
    w_beta, w_decay, log_rate, step_bias, out_gain, w_gate_out, w_out, norm_gain2,
    w_ffn_gate, w_ffn_up, w_ffn_down,
):
    tokens = 2 * LEN
    width = inputs.shape[-1]
    out = run_layer((
        inputs.reshape(tokens, width), cotangent.reshape(tokens, width),
        norm_gain1, conv_query[0], conv_key[0], conv_value[0], w_beta[0].T, w_decay[0].T,
        log_rate, step_bias, out_gain, norm_gain2,
        w_query[0], w_key[0], w_value[0], w_gate_out[0], w_out[0],
        w_ffn_gate[0].T, w_ffn_up[0].T, w_ffn_down[0],
    ))
    hidden, input_grad, gq, gk, gv, gb, gd, ggo, gout, gfg, gfu, gfd, sums = out
    (
        hidden, input_grad, gq, gk, gv, ggo, gout, gfg, gfu, gfd, gb, gd,
        dg1, dcq, dck, dcv, dlr, dsb, dog, dg2,
    ) = run_results(
        (hidden, input_grad, gq, gk, gv, ggo, gout, gfg, gfu, gfd), (gb, gd, sums)
    )
    shape = (1,) + inputs.shape
    return (
        hidden.reshape(shape), input_grad.reshape(shape), dg1, gq[None], gk[None], gv[None],
        dcq[None], dck[None], dcv[None], gb.T[None], gd.T[None], dlr, dsb, dog,
        ggo[None], gout.T[None], dg2, gfg[None], gfu[None], gfd.T[None],
    )


def solution(mesh):
    three = P("section", None, "tensor")
    in_specs = (
        P(None, "dp", None, None), P(None, "dp", None, None), P("section", None),
        three, three, three, three, three, three, three, three,
        P("section", "tensor"), P("section", "tensor"), P("section", "tensor"),
        three, P("section", "tensor", None), P("section", None),
        three, three, P("section", "tensor", None),
    )
    spread = P("section", "dp", "tensor")
    out_specs = (
        P("section", None, "dp", None, None), P("section", None, "dp", None, None),
        P("section", None), spread, spread, spread, three, three, three, spread, spread,
        P("section", "tensor"), P("section", "tensor"), P("section", "tensor"),
        spread, P("section", "tensor", "dp"), P("section", None),
        spread, spread, P("section", "tensor", "dp"),
    )
    return jax.shard_map(
        per_device, mesh=mesh, in_specs=in_specs, out_specs=out_specs, check_vma=False
    )
```
